32 devices in a mesh: dp: 16 (over z, x, core), tensor: 2 (over y).
Axes of the slice: x: 2, y: 2, z: 4, core: 2. Of those that a mesh axis runs over, the one named last changes fastest.
Arguments:
- tokens: bfloat16 [16384, 1536], P('dp'), may hold values from -6 to 6
- norm_gain: float32 [1536], replicated, may hold values from 0.5 to 1.5
- mix_weight: bfloat16 [1536, 2, 3072], P(None, None, 'tensor'), may hold values from -0.15625 to 0.15625
- state_weight: bfloat16 [1536, 256], replicated, may hold values from -0.15625 to 0.15625
- step_weight: bfloat16 [1536, 48], P(None, 'tensor'), may hold values from -0.15625 to 0.15625
- conv_weight: float32 [4, 3072], P(None, 'tensor'), may hold values from -3 to 3
- conv_bias: float32 [3072], P('tensor'), may hold values from -3 to 3
- state_conv_weight: float32 [4, 256], replicated, may hold values from -3 to 3
- state_conv_bias: float32 [256], replicated, may hold values from -3 to 3
- step_bias: float32 [48], P('tensor'), may hold values from -6.9 to -2.3
- log_rate: float32 [48], P('tensor'), may hold values from 0 to 2.77
- skip_gain: float32 [48], P('tensor'), may hold values from 0.5 to 1.5
- gate_gain: float32 [3072], P('tensor'), may hold values from 0.5 to 1.5
- out_weight: bfloat16 [3072, 1536], P('tensor'), may hold values from -0.109375 to 0.109375
- cotangent: bfloat16 [16384, 1536], P('dp'), may hold values from -6 to 6
Outputs:
- block_out: bfloat16 [16384, 1536], P('dp')
- grad_tokens: bfloat16 [16384, 1536], P('dp')
- grad_norm_gain: bfloat16 [1536], replicated
- grad_mix_weight: bfloat16 [1536, 2, 3072], P(None, None, 'tensor')
- grad_state_weight: bfloat16 [1536, 256], replicated
- grad_step_weight: bfloat16 [1536, 48], P(None, 'tensor')
- grad_conv_weight: bfloat16 [4, 3072], P(None, 'tensor')
- grad_conv_bias: bfloat16 [3072], P('tensor')
- grad_state_conv_weight: bfloat16 [4, 256], replicated
- grad_state_conv_bias: bfloat16 [256], replicated
- grad_step_bias: bfloat16 [48], P('tensor')
- grad_log_rate: bfloat16 [48], P('tensor')
- grad_skip_gain: bfloat16 [48], P('tensor')
- grad_gate_gain: bfloat16 [3072], P('tensor')
- grad_out_weight: bfloat16 [3072, 1536], P('tensor')
The draws below stay inside these ranges and needn't reach their ends.
All inputs are finite; a program needn't handle non-finite values.
Results may differ from the reference program's by a relative error of at most 0.0095.
Values may be sent and summed in bfloat16 or wider, within the bound.
A program may use at most 320 MiB of HBM per device.

```python
import jax
import jax.numpy as jnp
from jax import lax

D = 1536
INNER = 3072
HEADS = 48
NS = 128
CONV_WIDTH = 4
GROUP = 256
SEQ = 1024
TOKENS = 16384


def steps_of(own_key, dims, split, smallest, high):
    gain, own = 1.0, jax.random.fold_in(own_key, 6)
    for axis_at, shards_of in split:
        heights = jnp.exp(jax.random.uniform(jax.random.fold_in(own, axis_at), (shards_of,), jnp.float32, smallest / len(split), high / len(split)))
        gain = gain * jnp.repeat(heights, dims[axis_at] // shards_of).reshape([-1 if axis == axis_at else 1 for axis in range(len(dims))])
    return gain


def gaussian(own_key, extent, width, limit, split=(), held_as=jnp.bfloat16):
    values = width * jax.random.normal(own_key, extent, jnp.float32)
    if split:
        values = values * steps_of(own_key, extent, split, -0.22, 0.18)
    return jnp.clip(values, -limit, limit).astype(held_as)


def setup_inputs(seed: int = 0) -> dict:
    keys = jax.random.split(jax.random.key(seed), 16)
    return {
        "tokens": gaussian(keys[0], (TOKENS, D), 1.0, 6.0, ((0, 16),)),
        "norm_gain": jnp.clip(1.0 + 0.1 * jax.random.normal(keys[1], (D,), jnp.float32), 0.5, 1.5),
        "mix_weight": gaussian(keys[2], (D, 2, INNER), D ** -0.5, 0.15625, ((2, 2),)),
        "state_weight": gaussian(keys[3], (D, 2 * NS), D ** -0.5, 0.15625),
        "step_weight": gaussian(keys[4], (D, HEADS), D ** -0.5, 0.15625, ((1, 2),)),
        "conv_weight": gaussian(keys[5], (CONV_WIDTH, INNER), CONV_WIDTH ** -0.5, 3.0, ((1, 2),), jnp.float32),
        "conv_bias": gaussian(keys[6], (INNER,), 0.5, 3.0, ((0, 2),), jnp.float32),
        "state_conv_weight": gaussian(keys[7], (CONV_WIDTH, 2 * NS), CONV_WIDTH ** -0.5, 3.0, (), jnp.float32),
        "state_conv_bias": gaussian(keys[8], (2 * NS,), 0.5, 3.0, (), jnp.float32),
        "step_bias": jnp.clip(-6.9 + 4.6000001430511475 * jax.random.uniform(keys[9], (HEADS,), jnp.float32) ** steps_of(keys[9], (HEADS,), ((0, 2),), -0.2, 0.2), -6.9, -2.3),
        "log_rate": jnp.clip(2.77 * jax.random.uniform(keys[10], (HEADS,), jnp.float32) ** steps_of(keys[10], (HEADS,), ((0, 2),), -0.2, 0.2), 0.0, 2.77),
        "skip_gain": jnp.clip(0.5 + 1.0 * jax.random.uniform(keys[11], (HEADS,), jnp.float32) ** steps_of(keys[11], (HEADS,), ((0, 2),), -0.2, 0.2), 0.5, 1.5),
        "gate_gain": jnp.clip(1.0 + 0.1 * jax.random.normal(keys[12], (INNER,), jnp.float32), 0.5, 1.5),
        "out_weight": gaussian(keys[13], (INNER, D), INNER ** -0.5, 0.109375, ((0, 2),)),
        "cotangent": gaussian(keys[14], (TOKENS, D), 1.0, 6.0, ((0, 16),)),
    }


EPSILON = 1e-05
HIGHEST = lax.Precision.HIGHEST

@jax.custom_vjp
def low(v):
    return lax.optimization_barrier(v.astype(jnp.bfloat16)).astype(jnp.float32)

@jax.custom_vjp
def low_back(v):
    return v

def low_keep(v):
    return (low(v), None)

def low_pass(kept, grad):
    return (grad,)

def back_keep(v):
    return (v, None)

def back_low(kept, grad):
    return (low(grad),)
low.defvjp(low_keep, low_pass)
low_back.defvjp(back_keep, back_low)

def pre_norm(values, gain_wide):
    return values * lax.rsqrt(lax.optimization_barrier(jnp.mean(values * values, axis=-1, keepdims=True)) + EPSILON) * gain_wide

def conv_silu(values, kernel, offset):
    tap_count = kernel.shape[0]
    seq_len = values.shape[0]
    padded = jnp.pad(values, ((tap_count - 1, 0), (0, 0)))
    summed = offset + sum((padded[tap_index:tap_index + seq_len] * kernel[tap_index] for tap_index in range(tap_count)))
    return jax.nn.silu(summed)

def state_space(x_conv, step_size, rates, b_rows, c_rows, skip_gain):
    seq_len, head_count, head_size = x_conv.shape
    blocks = seq_len // GROUP
    x_scaled = (x_conv * step_size[:, :, None]).reshape(blocks, GROUP, head_count, head_size)
    log_decay = (step_size * rates[None, :]).reshape(blocks, GROUP, head_count)
    cumulated = jnp.cumsum(log_decay, axis=1)
    b_blocks = b_rows.reshape(blocks, GROUP, -1)
    c_blocks = c_rows.reshape(blocks, GROUP, -1)
    scores = jnp.einsum('cin,cjn->cij', c_blocks, b_blocks, precision=HIGHEST)
    lower_mask = jnp.tril(jnp.ones((GROUP, GROUP), dtype=bool))[None, None]
    cum_heads = jnp.transpose(cumulated, (0, 2, 1))
    differences = cum_heads[:, :, :, None] - cum_heads[:, :, None, :]
    decays = jnp.where(lower_mask, jnp.exp(jnp.where(lower_mask, differences, 0.0)), 0.0)
    mixing = scores[:, None] * decays
    within = jnp.einsum('chij,cjhp->cihp', mixing, x_scaled, precision=HIGHEST)
    final_cum = cumulated[:, -1, :]
    to_end = jnp.exp(final_cum[:, None, :] - cumulated)
    weighted = x_scaled * to_end[:, :, :, None]
    states = jnp.einsum('cjn,cjhp->chnp', b_blocks, weighted, precision=HIGHEST)

    def carry_step(carried, pieces):
        factor, fresh = pieces
        return (factor[:, None, None] * carried + fresh, carried)
    _, entering = lax.scan(carry_step, jnp.zeros_like(states[0]), (jnp.exp(final_cum), states))
    across = jnp.einsum('cin,chnp->cihp', c_blocks, entering, precision=HIGHEST) * jnp.exp(cumulated)[:, :, :, None]
    result = (within + across).reshape(seq_len, head_count, head_size) + skip_gain[None, :, None] * x_conv
    return result.reshape(seq_len, head_count * head_size)

def mixer_local(mix_pre, step_pre, conv_weight, conv_bias, step_bias, log_rate, skip_gain, b_rows, c_rows):
    x_conv = conv_silu(mix_pre, conv_weight, conv_bias)
    step_size = jax.nn.softplus(step_pre + step_bias)
    head_count = step_size.shape[1]
    return state_space(x_conv.reshape(x_conv.shape[0], head_count, -1), step_size, -jnp.exp(log_rate), b_rows, c_rows, skip_gain)

def block(tokens, norm_gain, mix_weight, state_weight, step_weight, conv_weight, conv_bias, state_conv_weight, state_conv_bias, step_bias, log_rate, skip_gain, gate_gain, out_weight):
    model = tokens.shape[1]
    inner = out_weight.shape[0]
    state = state_weight.shape[1] // 2
    normed = low(pre_norm(tokens, norm_gain))
    mix_proj = low_back(jnp.dot(normed, mix_weight.reshape(model, 2 * inner), precision=HIGHEST))
    state_pre = low_back(jnp.dot(normed, state_weight, precision=HIGHEST))
    step_pre = low_back(jnp.dot(normed, step_weight, precision=HIGHEST))
    state_act = conv_silu(state_pre, state_conv_weight, state_conv_bias)
    mixed_ssd = mixer_local(mix_proj[:, inner:], step_pre, conv_weight, conv_bias, step_bias, log_rate, skip_gain, state_act[:, :state], state_act[:, state:])
    gated = mixed_ssd * jax.nn.silu(mix_proj[:, :inner])
    scaled = low(pre_norm(gated, gate_gain))
    return tokens + jnp.dot(scaled, out_weight, precision=HIGHEST)

def reference(tokens, norm_gain, mix_weight, state_weight, step_weight, conv_weight, conv_bias, state_conv_weight, state_conv_bias, step_bias, log_rate, skip_gain, gate_gain, out_weight, cotangent):
    params = tuple((item.astype(jnp.float32) for item in (norm_gain, mix_weight, state_weight, step_weight, conv_weight, conv_bias, state_conv_weight, state_conv_bias, step_bias, log_rate, skip_gain, gate_gain, out_weight)))
    sequences = tokens.astype(jnp.float32).reshape(-1, SEQ, D)
    cot_seqs = cotangent.astype(jnp.float32).reshape(-1, SEQ, D)
    zeros = tuple((jnp.zeros_like(item) for item in params))

    def one_seq(totals, pieces):
        sequence, cot_seq = pieces
        output, pull = jax.vjp(block, sequence, *params)
        grads = pull(cot_seq)
        summed = tuple((left + right for left, right in zip(totals, grads[1:])))
        return (summed, (output.astype(jnp.bfloat16), grads[0].astype(jnp.bfloat16)))
    totals, (outputs, input_grads) = lax.scan(one_seq, zeros, (sequences, cot_seqs))
    rounded = tuple((item.astype(jnp.bfloat16) for item in totals))
    return (outputs.reshape(TOKENS, D), input_grads.reshape(TOKENS, D), rounded[0], rounded[1], rounded[2], rounded[3], rounded[4], rounded[5], rounded[6], rounded[7], rounded[8], rounded[9], rounded[10], rounded[11], rounded[12])
```

```python
import functools

import jax
import jax.numpy as jnp
from jax import lax
from jax.experimental import pallas as pl
from jax.experimental.pallas import tpu as pltpu
from jax.sharding import PartitionSpec as P

EPSILON = 1e-5
CHUNK = 128
HEAD = 64
GROUP_HEADS = 4
WIDTH = HEAD * GROUP_HEADS
LANES = 128
SLOT = 32
HIGHEST = lax.Precision.HIGHEST
F32, BF16 = jnp.float32, jnp.bfloat16
MIB = 1024 * 1024


def nn(left, right):
    return lax.dot_general(left, right, (((1,), (0,)), ((), ())), preferred_element_type=F32)


def nt(left, right):
    return lax.dot_general(left, right, (((1,), (1,)), ((), ())), preferred_element_type=F32)


def tn(left, right):
    return lax.dot_general(left, right, (((0,), (0,)), ((), ())), preferred_element_type=F32)


def sigmoid(v):
    return 1.0 / (1.0 + jnp.exp(-v))


def split3(v):
    high = v.astype(BF16).astype(F32)
    rest = v - high
    mid = rest.astype(BF16).astype(F32)
    low = rest - mid
    return (high + pltpu.roll(mid, SLOT, 1) + pltpu.roll(low, 2 * SLOT, 1)).astype(BF16)


def spread(group, lanes_each):
    shape = (LANES, GROUP_HEADS * lanes_each)
    slot = lax.broadcasted_iota(jnp.int32, shape, 0)
    lane = lax.broadcasted_iota(jnp.int32, shape, 1)
    hit = (slot % SLOT == group * GROUP_HEADS + lane // lanes_each) & (slot < 3 * SLOT)
    return jnp.where(hit, 1.0, 0.0).astype(BF16)


def gather_heads(group):
    shape = (WIDTH, LANES)
    lane = lax.broadcasted_iota(jnp.int32, shape, 0)
    head = lax.broadcasted_iota(jnp.int32, shape, 1)
    return jnp.where(head == group * GROUP_HEADS + lane // HEAD, 1.0, 0.0).astype(BF16)


def head_sums(v, chooser):
    high = v.astype(BF16)
    low = (v - high.astype(F32)).astype(BF16)
    return nn(high, chooser) + nn(low, chooser)


def fold(v):
    return jnp.sum(v.reshape(v.shape[0] // 8, 8, v.shape[1]), axis=0)


def prologue_kernel(
    heads,
    tokens_ref, gain_ref, state_w_ref, step_w_ref, taps_ref, bias_ref, step_bias_ref, rate_ref,
    normed_ref, normed_t_ref, state_pre_ref, b_ref, c_ref, b_t_ref, c_t_ref, scores_ref,
    step_pre_ref, step_ref, step3_ref, cum3_ref, ecum3_ref, toend3_ref, cum_t_ref,
    halo,
):
    rows = tokens_ref.shape[0]

    @pl.when(pl.program_id(0) == 0)
    def _():
        halo[0:8, :] = jnp.zeros((8, halo.shape[1]), F32)

    @pl.when(pl.program_id(0) > 0)
    def _():
        halo[0:8, :] = halo[rows : rows + 8, :]

    values = tokens_ref[...].astype(F32)
    inverse = lax.rsqrt(jnp.mean(values * values, axis=1, keepdims=True) + EPSILON)
    normed_wide = values * inverse * gain_ref[...]
    normed = normed_wide.astype(BF16)
    normed_ref[...] = normed
    normed_t_ref[...] = normed.T
    state_pre = nn(normed, state_w_ref[...])
    state_pre_ref[...] = state_pre
    halo[8 : 8 + rows, :] = state_pre
    summed = bias_ref[...] + sum(taps_ref[k : k + 1, :] * halo[5 + k : 5 + k + rows, :] for k in range(4))
    act = summed * sigmoid(summed)
    state = act.shape[1] // 2
    b_wide, c_wide = act[:, :state], act[:, state:]
    b_low, c_low = b_wide.astype(BF16), c_wide.astype(BF16)
    b_ref[...] = b_low
    c_ref[...] = c_low
    step_pre = nn(normed, step_w_ref[...]) + step_bias_ref[...]
    step_pre_ref[...] = step_pre
    lane = lax.broadcasted_iota(jnp.int32, step_pre.shape, 1)
    step = jnp.maximum(step_pre, 0.0) + jnp.log1p(jnp.exp(-jnp.abs(step_pre)))
    step = jnp.where(lane < heads, step, 0.0)
    step_ref[...] = step
    step3_ref[...] = split3(step)
    decay = step * rate_ref[...]
    low_tri = (
        lax.broadcasted_iota(jnp.int32, (CHUNK, CHUNK), 0) >= lax.broadcasted_iota(jnp.int32, (CHUNK, CHUNK), 1)
    ).astype(F32)
    place = lax.broadcasted_iota(jnp.int32, (LANES, LANES), 0)
    head = lax.broadcasted_iota(jnp.int32, (LANES, LANES), 1)
    places = ((place % 8 < GROUP_HEADS) & (head == place // 8 * GROUP_HEADS + place % 8)).astype(F32)
    for part in range(rows // CHUNK):
        at = slice(part * CHUNK, (part + 1) * CHUNK)
        b_t_ref[part] = b_wide[at].T.astype(BF16)
        c_t_ref[part] = c_wide[at].T.astype(BF16)
        scores_ref[part] = nt(c_low[at], b_low[at])
        cum = jnp.dot(low_tri, decay[at], precision=HIGHEST, preferred_element_type=F32)
        keep = lane[at] < heads
        cum3_ref[at, :] = split3(cum)
        ecum3_ref[at, :] = split3(jnp.where(keep, jnp.exp(cum), 0.0))
        toend3_ref[at, :] = split3(jnp.where(keep, jnp.exp(cum[CHUNK - 1 :, :] - cum), 0.0))
        cum_t_ref[:, at] = lax.dot_general(
            places, cum, (((1,), (1,)), ((), ())), precision=HIGHEST, preferred_element_type=F32
        )


def prologue(tokens, norm_gain, state_weight, step_weight, state_conv_weight, state_conv_bias, step_bias, log_rate):
    seq, model = tokens.shape
    heads = step_bias.shape[0]
    pad = LANES - heads
    step_w = jnp.pad(step_weight, ((0, 0), (0, pad)))
    step_b = jnp.pad(step_bias, (0, pad)).reshape(1, LANES)
    rate = jnp.pad(-jnp.exp(log_rate), (0, pad)).reshape(1, LANES)
    rows = 2 * CHUNK
    blocks = seq // rows
    chunks = seq // CHUNK
    two = state_weight.shape[1]
    state = two // 2
    by_rows = lambda width: pl.BlockSpec((rows, width), lambda i: (i, 0))
    whole = lambda shape: pl.BlockSpec(shape, lambda i: (0,) * len(shape), pipeline_mode=pl.Buffered(1))
    per_chunk = lambda a, b: pl.BlockSpec((rows // CHUNK, a, b), lambda i: (i, 0, 0))
    shape = jax.ShapeDtypeStruct
    outs = pl.pallas_call(
        functools.partial(prologue_kernel, heads),
        grid=(blocks,),
        in_specs=[
            by_rows(model), whole((1, model)), whole((model, two)), whole((model, LANES)), whole((4, two)), whole((1, two)),
            whole((1, LANES)), whole((1, LANES)),
        ],
        out_specs=[
            by_rows(model), pl.BlockSpec((model, rows), lambda i: (0, i)), by_rows(two), by_rows(state), by_rows(state),
            per_chunk(state, CHUNK), per_chunk(state, CHUNK), per_chunk(CHUNK, CHUNK),
            by_rows(LANES), by_rows(LANES), by_rows(LANES), by_rows(LANES), by_rows(LANES), by_rows(LANES),
            pl.BlockSpec((LANES, rows), lambda i: (0, i)),
        ],
        out_shape=[
            shape((seq, model), BF16), shape((model, seq), BF16), shape((seq, two), F32), shape((seq, state), BF16),
            shape((seq, state), BF16), shape((chunks, state, CHUNK), BF16), shape((chunks, state, CHUNK), BF16),
            shape((chunks, CHUNK, CHUNK), F32), shape((seq, LANES), F32), shape((seq, LANES), F32), shape((seq, LANES), BF16),
            shape((seq, LANES), BF16), shape((seq, LANES), BF16), shape((seq, LANES), BF16), shape((LANES, seq), F32),
        ],
        scratch_shapes=[pltpu.VMEM((8 + rows, two), F32)],
        compiler_params=pltpu.CompilerParams(vmem_limit_bytes=40 * MIB),
        name="prologue",
    )(
        tokens, norm_gain.reshape(1, model), state_weight, step_w, state_conv_weight, state_conv_bias.reshape(1, two), step_b, rate,
    )
    names = (
        "normed", "normed_t", "state_pre", "b", "c", "b_t", "c_t", "scores", "step_pre", "step", "step3", "cum3", "ecum3",
        "toend3", "cum_t",
    )
    made = dict(zip(names, outs))
    made["rate"] = rate
    return made


def masks():
    row = lax.broadcasted_iota(jnp.int32, (CHUNK, CHUNK), 0)
    col = lax.broadcasted_iota(jnp.int32, (CHUNK, CHUNK), 1)
    return row >= col, col < HEAD


def both_halves(v, first):
    zero = jnp.zeros_like(v)
    return jnp.concatenate([jnp.where(first, v, zero), jnp.where(first, zero, v)], axis=0)


def decay_of(cum_b, cum_t_ref, head, at, lower):
    across = cum_t_ref[head : head + 1, at]
    return jnp.exp(jnp.where(lower, cum_b - across, -1e30))


def forward_kernel(
    normed_ref, cot_ref, w_ref, ow_ref, taps_ref, bias_ref, skip_ref, gain_ref,
    b_t_ref, c_ref, scores_ref, step3_ref, cum3_ref, ecum3_ref, toend3_ref, cum_t_ref,
    gate_ref, mix_ref, y_ref, gs_ref, entering_ref, sums_ref,
    carry, square, dots,
):
    group = pl.program_id(0)
    seq = normed_ref.shape[0]
    chunks = seq // CHUNK

    @pl.when(group == 0)
    def _():
        square[...] = jnp.zeros_like(square)
        dots[...] = jnp.zeros_like(dots)

    mix_ref[0:8, :] = jnp.zeros((8, WIDTH), F32)
    mix_ref[8:, :] = nn(normed_ref[...], w_ref[1])
    gate_ref[...] = nn(normed_ref[...], w_ref[0])
    gs_ref[...] = nt(cot_ref[...], ow_ref[...])
    carry[...] = jnp.zeros_like(carry)
    each, wide = spread(group, HEAD), spread(group, LANES)
    lower, first = masks()

    def chunk(c, _):
        start = pl.multiple_of(c * CHUNK, CHUNK)
        at = pl.ds(start, CHUNK)
        around = mix_ref.at[pl.ds(start, CHUNK + 8), :]
        summed = bias_ref[...] + sum(
            taps_ref[k : k + 1, :] * around[5 + k : 5 + k + CHUNK, :] for k in range(4)
        )
        x = summed * sigmoid(summed)
        xs = x * nn(step3_ref[at, :], each)
        ecum = nn(ecum3_ref[at, :], each)
        weighted = (xs * nn(toend3_ref[at, :], each)).astype(BF16)
        u = xs.astype(BF16)
        cum_b = nn(cum3_ref[at, :], wide)
        scores = scores_ref[c]
        state = carry[...]
        state_low = state.astype(BF16)
        entering_ref[0, c] = state_low
        y = nn(c_ref[at, :], state_low) * ecum + skip_ref[...] * x
        carry[...] = state * ecum[CHUNK - 1 :, :] + nn(b_t_ref[c], weighted)
        parts = []
        for pair in range(GROUP_HEADS // 2):
            mixing = jnp.concatenate(
                [
                    (
                        scores
                        * decay_of(cum_b[:, h * LANES : (h + 1) * LANES], cum_t_ref, h, at, lower)
                    ).astype(BF16)
                    for h in (2 * pair, 2 * pair + 1)
                ],
                axis=1,
            )
            parts.append(nn(mixing, both_halves(u[:, pair * LANES : (pair + 1) * LANES], first)))
        y = y + jnp.concatenate(parts, axis=1)
        y_ref[at, :] = y
        gate = gate_ref[at, :]
        gated = y * gate * sigmoid(gate)
        squares = gated * gated
        product = gs_ref[at, :] * gain_ref[...] * gated
        square[at, :] += squares[:, :LANES] + squares[:, LANES:]
        dots[at, :] += product[:, :LANES] + product[:, LANES:]
        return 0

    lax.fori_loop(0, chunks, chunk, 0)

    @pl.when(group == pl.num_programs(0) - 1)
    def _():
        sums_ref[0] = jnp.broadcast_to(jnp.sum(square[...], axis=1, keepdims=True), square.shape)
        sums_ref[1] = jnp.broadcast_to(jnp.sum(dots[...], axis=1, keepdims=True), dots.shape)


def whole_spec(shape):
    return pl.BlockSpec(shape, lambda g: (0,) * len(shape), pipeline_mode=pl.Buffered(1))


def column(rows):
    return pl.BlockSpec((rows, WIDTH), lambda g: (0, g))


def forward(made, cotangent, both, out_weight, conv_weight, conv_bias, skip, gate_gain):
    seq, model = cotangent.shape
    inner = out_weight.shape[0]
    groups = inner // WIDTH
    chunks = seq // CHUNK
    state = made["b"].shape[1]
    shape = jax.ShapeDtypeStruct
    names = "b_t", "c", "scores", "step3", "cum3", "ecum3", "toend3", "cum_t"
    return pl.pallas_call(
        forward_kernel,
        grid=(groups,),
        in_specs=[
            whole_spec((seq, model)), whole_spec((seq, model)), pl.BlockSpec((2, model, WIDTH), lambda g: (0, 0, g)),
            pl.BlockSpec((WIDTH, model), lambda g: (g, 0)), column(4), column(1), column(1), column(1),
        ] + [whole_spec(made[n].shape) for n in names[:-1]] + [pl.BlockSpec((8, seq), lambda g: (g, 0))],
        out_specs=[
            column(seq), column(seq + 8), column(seq), column(seq),
            pl.BlockSpec((1, chunks, state, WIDTH), lambda g: (g, 0, 0, 0)),
            pl.BlockSpec((2, seq, LANES), lambda g: (0, 0, 0)),
        ],
        out_shape=[
            shape((seq, inner), F32), shape((seq + 8, inner), F32), shape((seq, inner), F32), shape((seq, inner), F32),
            shape((groups, chunks, state, WIDTH), BF16), shape((2, seq, LANES), F32),
        ],
        scratch_shapes=[
            pltpu.VMEM((state, WIDTH), F32), pltpu.VMEM((seq, LANES), F32), pltpu.VMEM((seq, LANES), F32),
        ],
        compiler_params=pltpu.CompilerParams(vmem_limit_bytes=56 * MIB),
        name="forward",
    )(
        made["normed"], cotangent, both, out_weight, conv_weight, conv_bias.reshape(1, inner), skip,
        gate_gain.reshape(1, inner), *[made[n] for n in names],
    )


def backward_kernel(
    normed_t_ref, cot_ref, gate_ref, mix_ref, y_ref, gs_ref, entering_ref, factor_ref,
    taps_ref, bias_ref, skip_ref, gain_ref,
    b_ref, c_ref, c_t_ref, scores_ref, step3_ref, cum3_ref, ecum3_ref, toend3_ref,
    step_pre_ref, step_ref, rate_ref, cum_t_ref,
    gout_ref, ggate_w_ref, gmix_w_ref, gate_low_ref, mix_low_ref, scaled_ref, columns_ref,
    gbc_ref, gstep_ref, heads_ref,
    dy, dz, carry, partial, gscores, decay_sums, step_sums,
):
    group = pl.program_id(0)
    seq = normed_t_ref.shape[1]
    chunks = seq // CHUNK
    state = b_ref.shape[1]

    @pl.when(group == 0)
    def _():
        gscores[...] = jnp.zeros_like(gscores)
        decay_sums[...] = jnp.zeros_like(decay_sums)
        step_sums[...] = jnp.zeros_like(step_sums)
        gbc_ref[...] = jnp.zeros_like(gbc_ref)

    partial[...] = jnp.zeros_like(partial)

    def gating(c, _):
        at = pl.ds(pl.multiple_of(c * CHUNK, CHUNK), CHUNK)
        inverse = jnp.concatenate([factor_ref[0, at, :]] * 2, axis=1)
        coefficient = jnp.concatenate([factor_ref[1, at, :]] * 2, axis=1)
        gate, y, gs, gain = gate_ref[at, :], y_ref[at, :], gs_ref[at, :], gain_ref[...]
        sig = sigmoid(gate)
        silu = gate * sig
        gated = y * silu
        hat = gated * inverse
        scaled_ref[at, :] = (hat * gain).astype(BF16)
        partial[0] += fold(gs * hat)
        ggated = inverse * (gs * gain) - gated * coefficient
        dy[at, :] = ggated * silu
        gate_low_ref[at, :] = (ggated * y * (sig + silu * (1.0 - sig))).astype(BF16)
        return 0

    lax.fori_loop(0, chunks, gating, 0)
    gout_ref[...] = tn(scaled_ref[...], cot_ref[...]).astype(BF16)
    ggate_w_ref[...] = nn(normed_t_ref[...], gate_low_ref[...]).astype(BF16)

    each, wide, chooser = spread(group, HEAD), spread(group, LANES), gather_heads(group)
    lower, first = masks()
    carry[...] = jnp.zeros_like(carry)
    dz[seq:, :] = jnp.zeros((8, WIDTH), F32)

    def chunk(step, _):
        c = chunks - 1 - step
        start = pl.multiple_of(c * CHUNK, CHUNK)
        at = pl.ds(start, CHUNK)
        around = mix_ref.at[pl.ds(start, CHUNK + 8), :]
        shifted = [around[5 + k : 5 + k + CHUNK, :] for k in range(4)]
        summed = bias_ref[...] + sum(taps_ref[k : k + 1, :] * shifted[k] for k in range(4))
        sig = sigmoid(summed)
        x = summed * sig
        step_e = nn(step3_ref[at, :], each)
        ecum = nn(ecum3_ref[at, :], each)
        toend = nn(toend3_ref[at, :], each)
        cum_b = nn(cum3_ref[at, :], wide)
        xs = x * step_e
        u = xs.astype(BF16)
        weighted = (xs * toend).astype(BF16)
        gy = dy[at, :]
        gy_low = gy.astype(BF16)
        gy_across = (gy * ecum).astype(BF16)
        gstate = carry[...]
        gstate_low = gstate.astype(BF16)
        entering = entering_ref[0, c]
        last = ecum[CHUNK - 1 :, :]
        gbc_ref[at, state:] += nt(gy_across, entering)
        gbc_ref[at, :state] += nt(weighted, gstate_low)
        from_state = nn(b_ref[at, :], gstate_low)
        to_output = nn(c_ref[at, :], entering)
        kept = weighted.astype(F32) * from_state
        state_dot = jnp.sum(kept, axis=0, keepdims=True) + last * jnp.sum(
            entering.astype(F32) * gstate, axis=0, keepdims=True
        )
        carry[...] = gstate * last + nn(c_t_ref[c], gy_across)
        scores = scores_ref[c]
        gscore = jnp.zeros((CHUNK, CHUNK), F32)
        parts = []
        for pair in range(GROUP_HEADS // 2):
            lanes = slice(pair * LANES, (pair + 1) * LANES)
            gmixing = nt(gy_low[:, lanes], both_halves(u[:, lanes], first))
            mixing = []
            for j in range(2):
                h = 2 * pair + j
                decay = decay_of(cum_b[:, h * LANES : (h + 1) * LANES], cum_t_ref, h, at, lower)
                gscore = gscore + gmixing[:, j * CHUNK : (j + 1) * CHUNK] * decay
                mixing.append((scores * decay).astype(BF16))
            back = tn(jnp.concatenate(mixing, axis=1), gy_low[:, lanes])
            parts.append(jnp.where(first, back[:CHUNK], back[CHUNK:]))
        gscores[c] += gscore
        gu = jnp.concatenate(parts, axis=1)
        skip = skip_ref[...]
        change = (
            gy_low.astype(F32) * (y_ref[at, :] - skip * x - ecum * to_output)
            + gy_across.astype(F32) * to_output
            - u.astype(F32) * gu
            - kept
        )
        gu = gu + from_state * toend
        row = lax.broadcasted_iota(jnp.int32, change.shape, 0)
        change = change + jnp.where(row == CHUNK - 1, state_dot, 0.0)
        decay_sums[at, :] += head_sums(change, chooser)
        step_sums[at, :] += head_sums(x * gu, chooser)
        gx = gu * step_e + skip * gy
        gsum = gx * (sig + x * (1.0 - sig))
        dz[at, :] = gsum
        partial[1] += fold(gy * x)
        partial[2] += fold(gsum)
        for k in range(4):
            partial[3 + k] += fold(gsum * shifted[k])
        after = dz.at[pl.ds(start, CHUNK + 8), :]
        gmix = sum(taps_ref[k : k + 1, :] * after[3 - k : 3 - k + CHUNK, :] for k in range(4))
        mix_low_ref[at, :] = gmix.astype(BF16)
        return 0

    lax.fori_loop(0, chunks, chunk, 0)
    gmix_w_ref[...] = nn(normed_t_ref[...], mix_low_ref[...]).astype(BF16)
    columns_ref[...] = jnp.concatenate(
        [jnp.sum(partial[i], axis=0, keepdims=True) for i in range(7)] + [jnp.zeros((1, WIDTH), F32)], axis=0
    )

    @pl.when(group == pl.num_programs(0) - 1)
    def _():
        upper = (
            lax.broadcasted_iota(jnp.int32, (CHUNK, CHUNK), 0) <= lax.broadcasted_iota(jnp.int32, (CHUNK, CHUNK), 1)
        ).astype(F32)
        heads_ref[...] = jnp.zeros_like(heads_ref)

        def finish(c, _):
            at = pl.ds(pl.multiple_of(c * CHUNK, CHUNK), CHUNK)
            gscore = gscores[c].astype(BF16)
            gbc_ref[at, state:] += nn(gscore, b_ref[at, :])
            gbc_ref[at, :state] += tn(gscore, c_ref[at, :])
            gdecay = jnp.dot(upper, decay_sums[at, :], precision=HIGHEST, preferred_element_type=F32)
            gstep = (gdecay * rate_ref[...] + step_sums[at, :]) * sigmoid(step_pre_ref[at, :])
            heads_ref[0] += fold(gstep)
            heads_ref[1] += fold(gdecay * step_ref[at, :] * rate_ref[...])
            gstep_ref[at, :] = gstep.astype(BF16)
            return 0

        lax.fori_loop(0, chunks, finish, 0)


def backward(made, cotangent, fwd, factors, conv_weight, conv_bias, skip, gate_gain):
    seq, model = cotangent.shape
    inner = skip.shape[1]
    groups = inner // WIDTH
    chunks = seq // CHUNK
    state = made["b"].shape[1]
    gate, mix, y, gs, entering = fwd
    shape = jax.ShapeDtypeStruct
    names = (
        "b", "c", "c_t", "scores", "step3", "cum3", "ecum3", "toend3", "step_pre", "step", "rate", "cum_t",
    )
    rows_of_out = pl.BlockSpec((WIDTH, model), lambda g: (g, 0))
    keep = lambda *dims: pl.BlockSpec(dims, lambda g: (0,) * len(dims))
    return pl.pallas_call(
        backward_kernel,
        grid=(groups,),
        in_specs=[
            whole_spec((model, seq)), whole_spec((seq, model)), column(seq), column(seq + 8), column(seq), column(seq),
            pl.BlockSpec((1, chunks, state, WIDTH), lambda g: (g, 0, 0, 0)), whole_spec((2, seq, LANES)),
            column(4), column(1), column(1), column(1),
        ] + [whole_spec(made[n].shape) for n in names[:-1]] + [pl.BlockSpec((8, seq), lambda g: (g, 0))],
        out_specs=[
            rows_of_out, column(model), column(model), column(seq), column(seq), column(seq), column(8),
            keep(seq, 2 * state), keep(seq, LANES), keep(2, 8, LANES),
        ],
        out_shape=[
            shape((inner, model), BF16), shape((model, inner), BF16), shape((model, inner), BF16),
            shape((seq, inner), BF16), shape((seq, inner), BF16), shape((seq, inner), BF16), shape((8, inner), F32),
            shape((seq, 2 * state), F32), shape((seq, LANES), BF16), shape((2, 8, LANES), F32),
        ],
        scratch_shapes=[
            pltpu.VMEM((seq, WIDTH), F32), pltpu.VMEM((seq + 8, WIDTH), F32), pltpu.VMEM((state, WIDTH), F32),
            pltpu.VMEM((7, 8, WIDTH), F32), pltpu.VMEM((chunks, CHUNK, CHUNK), F32), pltpu.VMEM((seq, LANES), F32),
            pltpu.VMEM((seq, LANES), F32),
        ],
        compiler_params=pltpu.CompilerParams(vmem_limit_bytes=60 * MIB),
        name="backward",
    )(
        made["normed_t"], cotangent, gate, mix, y, gs, entering, factors, conv_weight, conv_bias.reshape(1, inner), skip,
        gate_gain.reshape(1, inner), *[made[n] for n in names],
    )


SCHEDULE = (
    ("X8", 8), ("G2", 1), ("M3", 2), ("O5", 3), ("M1", 1), ("O6", 3), ("O4", 2), ("O0", 0), ("G0", 0), ("O8", 6), ("O1", 0), ("G1", 0), ("X4", 2), ("O2", 1), ("O7", 4), ("X6", 3), ("X7", 6), ("G3", 1), ("M2", 1), ("M0", 0), ("O3", 1), ("X5", 2),
)


class Route:
    def __init__(self, bits, rows):
        me = lax.axis_index("dp")
        self.bits = bits
        self.mine = [(me // b) % 2 for b in bits]
        self.partner = [me + b - 2 * b * v for b, v in zip(bits, self.mine)]
        self.size = [rows // 2 ** (s + 1) for s in range(len(bits))]
        self.base = [0]
        for s, v in enumerate(self.mine):
            self.base.append(self.base[-1] + v * self.size[s])
        self.away = [self.base[s] + (1 - self.mine[s]) * self.size[s] for s in range(len(bits))]

def mult(v, m):
    return v if isinstance(v, int) else pl.multiple_of(v, m)

def ar_kernel(schedule, groups, ring, order_o, order_x,
    o_in, g_in, m_in, o_out, x_out,
    o_src, g_src, m_src, o_r0,o_r1,o_r2,o_r3, g_r0,g_r1,g_r2,g_r3, m_r0,m_r1,m_r2,m_r3, x_own,
    load_sem, send_sem, recv_sem, copy_sem, ag_send, ag_recv):
    k = pl.program_id(0)
    me = lax.axis_index("dp")
    @pl.when(k == 0)
    def _():
        bar = pltpu.get_barrier_semaphore()
        for b in (1,2,4,8):
            v = (me // b) % 2
            pl.semaphore_signal(bar, inc=1, device_id={"dp": me + b - 2*b*v}, device_id_type=pl.DeviceIdType.MESH)
        pl.semaphore_wait(bar, 4)
    ro = Route(order_o, o_src.shape[1]); rx = Route(order_x, g_src.shape[1])
    kinds = {"O": (0, ro, o_src, (o_r0,o_r1,o_r2,o_r3)), "G": (1, rx, g_src, (g_r0,g_r1,g_r2,g_r3)), "M": (2, rx, m_src, (m_r0,m_r1,m_r2,m_r3))}
    def rs(kind, s, slot):
        i, r, src, recv = kinds[kind]
        n = r.size[s]
        return pltpu.make_async_remote_copy(
            src_ref=src.at[slot, pl.ds(mult(r.away[s], 16), n), :], dst_ref=recv[s].at[slot],
            send_sem=send_sem.at[i, s, slot], recv_sem=recv_sem.at[i, s, slot],
            device_id={"dp": r.partner[s]}, device_id_type=pl.DeviceIdType.MESH)
    def add(kind, s, slot):
        i, r, src, recv = kinds[kind]
        n = r.size[s]
        step = min(n, 96 if src.shape[2] == WIDTH else 16)
        if n <= step:
            at = pl.ds(mult(r.base[s+1], 16), n)
            src[slot, at, :] = (src[slot, at, :].astype(F32) + recv[s][slot].astype(F32)).astype(BF16)
        else:
            def body(j, _):
                at = pl.ds(pl.multiple_of(r.base[s+1] + j*step, 16), step)
                src[slot, at, :] = (src[slot, at, :].astype(F32) + recv[s][slot, pl.ds(pl.multiple_of(j*step,16), step), :].astype(F32)).astype(BF16)
                return 0
            lax.fori_loop(0, n//step, body, 0)
    def ag(kind, s, g, slot):
        if kind == "O":
            r, out, i = ro, o_out, 0
            at = pl.ds(mult(g*WIDTH + r.base[s+1], 16), r.size[s])
            dst = out.at[at, :]
            src = o_src.at[slot, pl.ds(mult(r.base[s+1],16), r.size[s]), :] if s == 3 else dst
        else:
            r, out, i = rx, x_out, 1
            dst = out.at[pl.ds(r.base[s+1], r.size[s]), :, pl.ds(pl.multiple_of(g*WIDTH, WIDTH), WIDTH)]
            src = x_own.at[slot] if s == 3 else dst
        return pltpu.make_async_remote_copy(src_ref=src, dst_ref=dst, send_sem=ag_send.at[i, s, g], recv_sem=ag_recv.at[i, s, g],
            device_id={"dp": r.partner[s]}, device_id_type=pl.DeviceIdType.MESH)
    def own(kind, g, slot):
        if kind == "O":
            return pltpu.make_async_copy(o_src.at[slot, pl.ds(mult(ro.base[4],16), ro.size[3]), :], o_out.at[pl.ds(mult(g*WIDTH + ro.base[4],16), ro.size[3]), :], copy_sem.at[0, slot])
        return pltpu.make_async_copy(x_own.at[slot], x_out.at[pl.ds(rx.base[4], rx.size[3]), :, pl.ds(pl.multiple_of(g*WIDTH,WIDTH), WIDTH)], copy_sem.at[1, slot])
    def event(name, g, slot):
        kind, st = name[0], int(name[1:])
        if st == 0:
            src_h = {"O": lambda: o_in.at[pl.ds(pl.multiple_of(g*WIDTH,WIDTH), WIDTH), :], "G": lambda: g_in.at[:, pl.ds(pl.multiple_of(g*WIDTH,WIDTH), WIDTH)], "M": lambda: m_in.at[:, pl.ds(pl.multiple_of(g*WIDTH,WIDTH), WIDTH)]}[kind]()
            i = kinds[kind][0]
            cp = pltpu.make_async_copy(src_h, kinds[kind][2].at[slot], load_sem.at[i, slot]); cp.start(); cp.wait()
            rs(kind, 0, slot).start()
        elif st < 4:
            rs(kind, st-1, slot).wait()
            add(kind, st-1, slot)
            rs(kind, st, slot).start()
        elif st == 4:
            if kind == "O":
                rs("O", 3, slot).wait(); add("O", 3, slot)
            else:
                for q in "GM":
                    rs(q, 3, slot).wait(); add(q, 3, slot)
                at = pl.ds(mult(rx.base[4],16), rx.size[3])
                x_own[slot, :, 0, :] = g_src[slot, at, :]
                x_own[slot, :, 1, :] = m_src[slot, at, :]
            own(kind, g, slot).start()
            ag(kind, 3, g, slot).start()
        else:
            s = 8 - st
            ag(kind, s, g, slot).wait()
            if st == 5: own(kind, g, slot).wait()
            if s > 0: ag(kind, s-1, g, slot).start()
    for name, d in schedule:
        g = k - d
        @pl.when((g >= 0) & (g < groups))
        def _():
            event(name, g, lax.rem(g, ring))

def all_reduce(schedule, o, g, m, ring=3, order_o=(1,4,2,8), order_x=(1,2,4,8)):
    inner, model = o.shape
    groups = inner // WIDTH
    depth = max(d for _, d in schedule)
    V = pltpu.VMEM
    sizes = lambda r: [r//2, r//4, r//8, r//16]
    scr = [V((ring, WIDTH, model), BF16), V((ring, model, WIDTH), BF16), V((ring, model, WIDTH), BF16)]
    scr += [V((ring, n, model), BF16) for n in sizes(WIDTH)]
    scr += [V((ring, n, WIDTH), BF16) for n in sizes(model)]*2
    scr += [V((ring, model//16, 2, WIDTH), BF16)]
    D = pltpu.SemaphoreType.DMA
    scr += [D((3, ring)), D((3,4,ring)), D((3,4,ring)), D((2,ring)), D((2,4,groups)), D((2,4,groups))]
    any_ = pl.BlockSpec(memory_space=pl.ANY)
    return pl.pallas_call(functools.partial(ar_kernel, schedule, groups, ring, order_o, order_x),
        grid=(groups+depth,), in_specs=[any_]*3, out_specs=[any_]*2,
        out_shape=[jax.ShapeDtypeStruct((inner, model), BF16), jax.ShapeDtypeStruct((model, 2, inner), BF16)],
        scratch_shapes=scr, compiler_params=pltpu.CompilerParams(collective_id=0, has_side_effects=True, vmem_limit_bytes=60*MIB), name="weight_reduce")(o,g,m)


def weight_reduce(o, g, m):
    gout, gmix = all_reduce(SCHEDULE, o, g, m)
    size = lax.axis_size("dp")
    if size > 16:
        rows = [[i + 16 * j for j in range(size // 16)] for i in range(16)]
        gout, gmix = lax.psum((gout, gmix), "dp", axis_index_groups=rows)
    return gout, gmix


def swap(values):
    size = lax.axis_size("tensor")
    return lax.ppermute(values, "tensor", [(i, (i + 1) % size) for i in range(size)])


def conv_silu(values, kernel, offset):
    padded = jnp.pad(values, ((3, 0), (0, 0)))
    summed = offset + sum(padded[k : k + values.shape[0]] * kernel[k] for k in range(4))
    return jax.nn.silu(summed)


def on_device(
    tokens, norm_gain, mix_weight, state_weight, step_weight, conv_weight, conv_bias, state_conv_weight, state_conv_bias,
    step_bias, log_rate, skip_gain, gate_gain, out_weight, cotangent,
):
    seq, model = tokens.shape
    inner = out_weight.shape[0]
    heads = step_bias.shape[0]
    full_width = inner * lax.axis_size("tensor")
    both = jnp.transpose(mix_weight, (1, 0, 2))
    made = prologue(tokens, norm_gain, state_weight, step_weight, state_conv_weight, state_conv_bias, step_bias, log_rate)
    skip = jnp.repeat(skip_gain, HEAD).reshape(1, inner)
    *fwd, sums = forward(made, cotangent, both, out_weight, conv_weight, conv_bias, skip, gate_gain)
    sums = sums[:, :, 0]
    sums = sums + swap(sums)
    inverse = lax.rsqrt(sums[0] / full_width + EPSILON)
    coefficient = inverse**3 * (sums[1] / full_width)
    factors = jnp.broadcast_to(jnp.stack([inverse, coefficient])[:, :, None], (2, seq, LANES))
    gout, ggate_w, gmix_w, gate_low, mix_low, scaled, columns, gbc, gstep, head_rows = backward(
        made, cotangent, fwd, factors, conv_weight, conv_bias, skip, gate_gain
    )
    product = nn(scaled, out_weight).astype(BF16)
    block_out = (tokens.astype(F32) + (product.astype(F32) + swap(product).astype(F32))).astype(BF16)

    gbc_low = gbc.astype(BF16)
    gbc_sum = gbc_low.astype(F32) + swap(gbc_low).astype(F32)
    _, state_pull = jax.vjp(conv_silu, made["state_pre"], state_conv_weight, state_conv_bias)
    gstate, gstate_taps, gstate_bias = state_pull(gbc_sum)
    gstate_low = gstate.astype(BF16)
    gstep_low = gstep[:, :heads]
    normed_t = made["normed_t"]
    gstate_w = nn(normed_t, gstate_low).astype(BF16)
    gstep_w = nn(normed_t, gstep_low).astype(BF16)
    part = (nt(gate_low, both[0]) + nt(mix_low, both[1]) + nt(gstep_low, step_weight)).astype(BF16)
    gnormed = part.astype(F32) + swap(part).astype(F32) + nt(gstate_low, state_weight)
    wide = tokens.astype(F32)
    rms = lax.rsqrt(jnp.mean(wide * wide, axis=1, keepdims=True) + EPSILON)
    scaled_grad = gnormed * norm_gain
    pull = rms * scaled_grad - wide * rms**3 * (jnp.sum(scaled_grad * wide, axis=1, keepdims=True) / model)
    grad_tokens = (cotangent.astype(F32) + pull).astype(BF16)
    gnorm_gain = jnp.sum(gnormed * wide * rms, axis=0)

    gout, gmix_weight = weight_reduce(gout, ggate_w, gmix_w)
    gstate_w, gstep_w = lax.psum((gstate_w, gstep_w), "dp")
    small = (
        gnorm_gain, columns[3:7], columns[2], gstate_taps, gstate_bias, jnp.sum(head_rows[0], axis=0)[:heads],
        jnp.sum(head_rows[1], axis=0)[:heads], jnp.sum(columns[1].reshape(heads, HEAD), axis=1), columns[0],
    )
    small = tuple(item.astype(BF16) for item in lax.psum(small, "dp"))
    return (
        block_out, grad_tokens, small[0], gmix_weight, gstate_w, gstep_w, small[1], small[2], small[3],
        small[4], small[5], small[6], small[7], small[8], gout,
    )


def solution(mesh):
    rows, halves = P("dp", None), P("tensor")
    return jax.shard_map(
        on_device,
        mesh=mesh,
        in_specs=(
            rows, P(), P(None, None, "tensor"), P(), P(None, "tensor"), P(None, "tensor"), halves, P(), P(), halves, halves,
            halves, halves, P("tensor", None), rows,
        ),
        out_specs=(
            rows, rows, P(), P(None, None, "tensor"), P(), P(None, "tensor"), P(None, "tensor"), halves, P(), P(), halves,
            halves, halves, halves, P("tensor", None),
        ),
        check_vma=False,
    )
```

```python
import functools
import types
import typing

import jax
import jax.numpy as jnp
from jax import lax
from jax.experimental import pallas as pl
from jax.experimental.pallas import tpu as pltpu
from jax.sharding import PartitionSpec as P

EPSILON = 1e-5
CHUNK = 128
HEAD = 64
GROUP_HEADS = 4
WIDTH = HEAD * GROUP_HEADS
LANES = 128
SLOT = 32
HIGHEST = lax.Precision.HIGHEST
F32, BF16 = jnp.float32, jnp.bfloat16
MIB = 1024 * 1024


def nn(left, right):
    return lax.dot_general(left, right, (((1,), (0,)), ((), ())), preferred_element_type=F32)


def nt(left, right):
    return lax.dot_general(left, right, (((1,), (1,)), ((), ())), preferred_element_type=F32)


def tn(left, right):
    return lax.dot_general(left, right, (((0,), (0,)), ((), ())), preferred_element_type=F32)


def sigmoid(v):
    return jax.nn.sigmoid(v)


def softplus(v):
    return jnp.maximum(v, 0.0) + jnp.log1p(jnp.exp(-jnp.abs(v)))


def split3(v):
    high = v.astype(BF16).astype(F32)
    rest = v - high
    mid = rest.astype(BF16).astype(F32)
    low = rest - mid
    return (high + pltpu.roll(mid, SLOT, 1) + pltpu.roll(low, 2 * SLOT, 1)).astype(BF16)


def spread(group, lanes_each):
    shape = (LANES, GROUP_HEADS * lanes_each)
    slot = lax.broadcasted_iota(jnp.int32, shape, 0)
    lane = lax.broadcasted_iota(jnp.int32, shape, 1)
    hit = (slot % SLOT == group * GROUP_HEADS + lane // lanes_each) & (slot < 3 * SLOT)
    return jnp.where(hit, 1.0, 0.0).astype(BF16)


def gather_heads(group):
    shape = (4 * WIDTH, LANES)
    row = lax.broadcasted_iota(jnp.int32, shape, 0)
    lane = lax.broadcasted_iota(jnp.int32, shape, 1)
    head = group * GROUP_HEADS + row % WIDTH // HEAD
    return jnp.where(lane == head + row // (2 * WIDTH) * (LANES // 2), 1.0, 0.0).astype(BF16)


def two_parts(v):
    high = v.astype(BF16)
    return high, (v - high.astype(F32)).astype(BF16)


def row_sums(v):
    ones = jnp.ones((8, LANES), BF16)
    high, low = two_parts(v)
    return nt(ones, high) + nt(ones, low)


def fold(v):
    return jnp.sum(v.reshape(v.shape[0] // 8, 8, v.shape[1]), axis=0)


def prologue_kernel(
    heads,
    tokens_ref, gain_ref, state_w_ref, step_w_ref, taps_ref, bias_ref, step_bias_ref, rate_ref,
    normed_ref, normed_t_ref, state_pre_ref, b_ref, c_ref, b_t_ref, c_t_ref, scores_ref,
    step_pre_ref, step3_ref, cum3_ref, cum_t_ref, rms_ref,
    halo,
):
    rows = tokens_ref.shape[0]

    @pl.when(pl.program_id(0) == 0)
    def _():
        halo[0:8, :] = jnp.zeros((8, halo.shape[1]), F32)

    @pl.when(pl.program_id(0) > 0)
    def _():
        halo[0:8, :] = halo[rows : rows + 8, :]

    values = tokens_ref[...].astype(F32)
    inverse = lax.rsqrt(jnp.mean(values * values, axis=1, keepdims=True) + EPSILON)
    rms_ref[...] = jnp.broadcast_to(inverse, rms_ref.shape)
    normed_wide = values * inverse * gain_ref[...]
    normed = normed_wide.astype(BF16)
    normed_ref[...] = normed
    normed_t_ref[...] = normed.T
    state_pre = nn(normed, state_w_ref[...])
    state_pre_ref[...] = state_pre
    halo[8 : 8 + rows, :] = state_pre
    summed = bias_ref[...] + sum(taps_ref[k : k + 1, :] * halo[5 + k : 5 + k + rows, :] for k in range(4))
    act = summed * sigmoid(summed)
    state = act.shape[1] // 2
    b_wide, c_wide = act[:, :state], act[:, state:]
    b_low, c_low = b_wide.astype(BF16), c_wide.astype(BF16)
    b_ref[...] = b_low
    c_ref[...] = c_low
    step_pre = nn(normed, step_w_ref[...]) + step_bias_ref[...]
    step_pre_ref[...] = step_pre
    lane = lax.broadcasted_iota(jnp.int32, step_pre.shape, 1)
    step = jnp.where(lane < heads, softplus(step_pre), 0.0)
    step3_ref[...] = split3(step)
    decay = step * rate_ref[...]
    low_tri = (
        lax.broadcasted_iota(jnp.int32, (CHUNK, CHUNK), 0) >= lax.broadcasted_iota(jnp.int32, (CHUNK, CHUNK), 1)
    ).astype(F32)
    place = lax.broadcasted_iota(jnp.int32, (LANES, LANES), 0)
    head = lax.broadcasted_iota(jnp.int32, (LANES, LANES), 1)
    places = ((place % 8 < GROUP_HEADS) & (head == place // 8 * GROUP_HEADS + place % 8)).astype(F32)
    for part in range(rows // CHUNK):
        at = slice(part * CHUNK, (part + 1) * CHUNK)
        b_t_ref[part] = b_wide[at].T.astype(BF16)
        c_t_ref[part] = c_wide[at].T.astype(BF16)
        scores_ref[part] = lax.dot_general(
            c_wide[at], b_wide[at], (((1,), (1,)), ((), ())), precision=HIGHEST, preferred_element_type=F32
        )
        cum = jnp.dot(low_tri, decay[at], precision=HIGHEST, preferred_element_type=F32)
        cum3_ref[at, :] = split3(cum)
        cum_t_ref[:, at] = lax.dot_general(
            places, cum, (((1,), (1,)), ((), ())), precision=HIGHEST, preferred_element_type=F32
        )


def prologue(tokens, norm_gain, state_weight, step_weight, state_conv_weight, state_conv_bias, step_bias, log_rate):
    seq, model = tokens.shape
    heads = step_bias.shape[0]
    pad = LANES - heads
    step_w = jnp.pad(step_weight, ((0, 0), (0, pad)))
    step_b = jnp.pad(step_bias, (0, pad)).reshape(1, LANES)
    rate = jnp.pad(-jnp.exp(log_rate), (0, pad)).reshape(1, LANES)
    rows = 2 * CHUNK
    blocks = seq // rows
    chunks = seq // CHUNK
    two = state_weight.shape[1]
    state = two // 2
    by_rows = lambda width: pl.BlockSpec((rows, width), lambda i: (i, 0))
    whole = lambda shape: pl.BlockSpec(shape, lambda i: (0,) * len(shape), pipeline_mode=pl.Buffered(1))
    per_chunk = lambda a, b: pl.BlockSpec((rows // CHUNK, a, b), lambda i: (i, 0, 0))
    shape = jax.ShapeDtypeStruct
    outs = pl.pallas_call(
        functools.partial(prologue_kernel, heads),
        grid=(blocks,),
        in_specs=[
            by_rows(model), whole((1, model)), whole((model, two)), whole((model, LANES)), whole((4, two)), whole((1, two)),
            whole((1, LANES)), whole((1, LANES)),
        ],
        out_specs=[
            by_rows(model), pl.BlockSpec((model, rows), lambda i: (0, i)), by_rows(two), by_rows(state), by_rows(state),
            per_chunk(state, CHUNK), per_chunk(state, CHUNK), per_chunk(CHUNK, CHUNK),
            by_rows(LANES), by_rows(LANES), by_rows(LANES),
            pl.BlockSpec((LANES, rows), lambda i: (0, i)), by_rows(LANES),
        ],
        out_shape=[
            shape((seq, model), BF16), shape((model, seq), BF16), shape((seq, two), F32), shape((seq, state), BF16),
            shape((seq, state), BF16), shape((chunks, state, CHUNK), BF16), shape((chunks, state, CHUNK), BF16),
            shape((chunks, CHUNK, CHUNK), F32), shape((seq, LANES), F32), shape((seq, LANES), BF16),
            shape((seq, LANES), BF16), shape((LANES, seq), F32), shape((seq, LANES), F32),
        ],
        scratch_shapes=[pltpu.VMEM((8 + rows, two), F32)],
        compiler_params=pltpu.CompilerParams(vmem_limit_bytes=62 * MIB),
        name="prologue",
    )(
        tokens, norm_gain.reshape(1, model), state_weight, step_w, state_conv_weight, state_conv_bias.reshape(1, two), step_b, rate,
    )
    names = (
        "normed", "normed_t", "state_pre", "b", "c", "b_t", "c_t", "scores", "step_pre", "step3", "cum3", "cum_t", "rms",
    )
    return dict(zip(names, outs), rate=rate, step_w=step_w, step_bias=step_b)


def masks():
    row = lax.broadcasted_iota(jnp.int32, (CHUNK, CHUNK), 0)
    col = lax.broadcasted_iota(jnp.int32, (CHUNK, CHUNK), 1)
    return row >= col, col < HEAD


def both_halves(v, first):
    zero = jnp.zeros_like(v)
    return jnp.concatenate([jnp.where(first, v, zero), jnp.where(first, zero, v)], axis=0)


def decay_of(cum_b, cum_t_ref, head, at, lower):
    across = cum_t_ref[head : head + 1, at]
    return jnp.exp(jnp.where(lower, cum_b - across, -1e30))


def pairwise(cum_b, at, first):
    heads = [cum_b[at, h * LANES : (h + 1) * LANES] for h in range(GROUP_HEADS)]
    return jnp.concatenate([jnp.where(first, heads[h], heads[h + 1]) for h in range(0, GROUP_HEADS, 2)], axis=1)


def forward_kernel(
    normed_ref, cot_ref, w_ref, ow_ref, taps_ref, bias_ref, skip_ref, gain_ref,
    b_t_ref, c_ref, scores_ref, step3_ref, cum3_ref, cum_t_ref,
    gate_ref, mix_ref, y_ref, entering_ref, product_ref, sums_ref,
    carry, square, gained, cum_b, step_e,
):
    group = pl.program_id(0)
    seq = normed_ref.shape[0]
    chunks = seq // CHUNK

    @pl.when(group == 0)
    def _():
        square[...] = jnp.zeros_like(square)

    mix_ref[0:8, :] = jnp.zeros((8, WIDTH), F32)
    mix_ref[8:, :] = nn(normed_ref[...], w_ref[1])
    gate_ref[...] = nn(normed_ref[...], w_ref[0])
    carry[...] = jnp.zeros_like(carry)
    lanes_of_group = pl.ds(pl.multiple_of(group * WIDTH, WIDTH), WIDTH)
    each, wide = spread(group, HEAD), spread(group, LANES)
    lower, first = masks()
    cum_b[...] = nn(cum3_ref[...], wide)
    step_e[...] = nn(step3_ref[...], each)

    def chunk(c, _):
        start = pl.multiple_of(c * CHUNK, CHUNK)
        at = pl.ds(start, CHUNK)
        around = mix_ref.at[pl.ds(start, CHUNK + 8), :]
        summed = bias_ref[...] + sum(
            taps_ref[k : k + 1, :] * around[5 + k : 5 + k + CHUNK, :] for k in range(4)
        )
        x = summed * sigmoid(summed)
        xs = x * step_e[at, :]
        cum = pairwise(cum_b, at, first)
        ecum = jnp.exp(cum)
        weighted = (xs * jnp.exp(cum[CHUNK - 1 :, :] - cum)).astype(BF16)
        u = xs.astype(BF16)
        scores = scores_ref[c]
        state = carry[...]
        state_low = state.astype(BF16)
        entering_ref[0, c] = state_low
        y = nn(c_ref[at, :], state_low) * ecum + skip_ref[...] * x
        carry[...] = state * ecum[CHUNK - 1 :, :] + nn(b_t_ref[c], weighted)
        parts = []
        for pair in range(GROUP_HEADS // 2):
            mixing = jnp.concatenate(
                [
                    (
                        scores
                        * decay_of(cum_b[at, h * LANES : (h + 1) * LANES], cum_t_ref, h, at, lower)
                    ).astype(BF16)
                    for h in (2 * pair, 2 * pair + 1)
                ],
                axis=1,
            )
            parts.append(nn(mixing, both_halves(u[:, pair * LANES : (pair + 1) * LANES], first)))
        y = y + jnp.concatenate(parts, axis=1)
        y_ref[at, :] = y
        gate = gate_ref[at, :]
        gated = y * gate * sigmoid(gate)
        squares = gated * gated
        square[at, :] += squares[:, :LANES] + squares[:, LANES:]
        gained[at, lanes_of_group] = (gated * gain_ref[...]).astype(BF16)
        return 0

    lax.fori_loop(0, chunks, chunk, 0, unroll=8)

    @pl.when(group == pl.num_programs(0) - 1)
    def _():
        def project(r, _):
            at = pl.ds(pl.multiple_of(r * 2 * CHUNK, CHUNK), 2 * CHUNK)
            product = nn(gained[at, :], ow_ref[...])
            product_ref[at, :] = product.astype(BF16)
            dots = product * cot_ref[at, :].astype(F32)
            dots = sum(dots[:, n * LANES : (n + 1) * LANES] for n in range(dots.shape[1] // LANES))
            sums_ref[0:8, at] = row_sums(square[at, :])
            sums_ref[8:16, at] = row_sums(dots)
            return 0

        lax.fori_loop(0, seq // (2 * CHUNK), project, 0)


def whole_spec(shape):
    return pl.BlockSpec(shape, lambda g: (0,) * len(shape), pipeline_mode=pl.Buffered(1))


def column(rows):
    return pl.BlockSpec((rows, WIDTH), lambda g: (0, g))


def forward(made, cotangent, both, out_weight, conv_weight, conv_bias, skip, gate_gain):
    seq, model = cotangent.shape
    inner = out_weight.shape[0]
    groups = inner // WIDTH
    chunks = seq // CHUNK
    state = made["b"].shape[1]
    shape = jax.ShapeDtypeStruct
    names = "b_t", "c", "scores", "step3", "cum3", "cum_t"
    return pl.pallas_call(
        forward_kernel,
        grid=(groups,),
        in_specs=[
            whole_spec((seq, model)), whole_spec((seq, model)), pl.BlockSpec((2, model, WIDTH), lambda g: (0, 0, g)),
            whole_spec((inner, model)), column(4), column(1), column(1), column(1),
        ] + [whole_spec(made[n].shape) for n in names[:-1]] + [pl.BlockSpec((8, seq), lambda g: (g, 0))],
        out_specs=[
            column(seq), column(seq + 8), column(seq),
            pl.BlockSpec((1, chunks, state, WIDTH), lambda g: (g, 0, 0, 0)),
            pl.BlockSpec((seq, model), lambda g: (0, 0)), pl.BlockSpec((16, seq), lambda g: (0, 0)),
        ],
        out_shape=[
            shape((seq, inner), F32), shape((seq + 8, inner), F32), shape((seq, inner), F32),
            shape((groups, chunks, state, WIDTH), BF16), shape((seq, model), BF16), shape((16, seq), F32),
        ],
        scratch_shapes=[
            pltpu.VMEM((state, WIDTH), F32), pltpu.VMEM((seq, LANES), F32), pltpu.VMEM((seq, inner), BF16),
            pltpu.VMEM((seq, GROUP_HEADS * LANES), F32), pltpu.VMEM((seq, WIDTH), F32),
        ],
        compiler_params=pltpu.CompilerParams(vmem_limit_bytes=56 * MIB),
        name="forward",
    )(
        made["normed"], cotangent, both, out_weight, conv_weight, conv_bias.reshape(1, inner), skip,
        gate_gain.reshape(1, inner), *[made[n] for n in names],
    )


class Inputs(typing.NamedTuple):
    normed_t: object
    cot: object
    gate: object
    mix: object
    y: object
    entering: object
    ow: object
    taps: object
    bias: object
    skip: object
    gain: object
    b: object
    c: object
    c_t: object
    scores: object
    step3: object
    cum3: object
    step_pre: object
    rate: object
    step_bias: object
    rms: object
    state_pre: object
    state_taps: object
    state_bias: object
    state_w: object
    step_w: object
    norm_gain: object
    cum_t: object
    w: object
    tokens: object
    sums: object
    product: object


class Outputs(typing.NamedTuple):
    gout: object
    gmix: object
    gstate_w: object
    gstep_w: object
    gtokens: object
    there: object
    mine: object
    block_out: object
    product_there: object
    small: object


class Scratch(typing.NamedTuple):
    gs: object
    dz: object
    cum_b: object
    step_e: object
    saved: object
    kept_carry: object
    kept_partial: object
    dy: object
    factor: object
    sums_there: object
    gscores: object
    decay_sums: object
    inner_sums: object
    gbc: object
    scaled: object
    gate_low: object
    mix_low: object
    gbc_low: object
    gbc_there: object
    inner_row: object
    inner_there: object
    gstep_low: object
    w_block: object
    token_block: object
    stage: object
    o_src: object
    g_src: object
    m_src: object
    s_src: object
    t_src: object
    o_r0: object
    o_r1: object
    o_r2: object
    o_r3: object
    g_r0: object
    g_r1: object
    g_r2: object
    g_r3: object
    m_r0: object
    m_r1: object
    m_r2: object
    m_r3: object
    s_r0: object
    s_r1: object
    s_r2: object
    s_r3: object
    t_r0: object
    t_r1: object
    t_r2: object
    t_r3: object
    g_own: object
    x_own: object
    o_own: object
    small_there: object
    small_last: object
    send_sem: object
    recv_sem: object
    copy_sem: object
    ag_send: object
    ag_recv: object
    near_send: object
    near_recv: object
    part_send: object
    part_recv: object
    small_send: object
    small_recv: object
    load_sem: object
    store_sem: object
    sums_send: object
    sums_recv: object
    product_send: object
    product_recv: object
    row_sem: object
    stage_sem: object
    gate_now: object
    ow_now: object
    now_sem: object
    state_block: object
    step_block: object
    narrow_sem: object


RING = 3
LANDINGS = 2
BITS = (1, 2, 4, 8)
O, G, M, S, T, X, MEET, PART, FINAL, SMALL, BLOCK = range(11)
MESH = pl.DeviceIdType.MESH


WHOLE, EARLY = 3, 9
X_FIRST, Z_FIRST = (1, 2, 4, 8), (1, 4, 2, 8)
O_TURNS, X_TURNS, S_TURNS = (1, 1, 0, 0, 0, 1,), (0, 0, 0, 0, 0, 1,), (0,)
MAIN = (
    (0, 3, ((O, 1, 0),)),
    (0, 4, ((G, 1, 0),)),
    (1, 4, ((O, 2, 0),)),
    (2, 0, ((G, 2, 0),)),
    (2, 1, ((M, 1, 0), (O, 3, 0),)),
    (2, 2, ((G, 3, 0),)),
    (2, 3, ((O, 1, 1),)),
    (2, 4, ((O, 4, 0), (G, 1, 1), (G, 4, 0), (M, 2, 0),)),
    (3, 4, ((O, 5, 0),)),
    (3, 5, ((G, 2, 1),)),
    (4, 1, ((M, 1, 1), (O, 6, 0),)),
    (4, 2, ((G, 3, 1),)),
    (4, 3, ((O, 1, 2), (O, 3, 1), (G, 1, 2), (M, 4, 0),)),
    (4, 4, ((G, 4, 1),)),
    (4, 6, ((M, 3, 0), (O, 2, 1),)),
    (5, 3, ((O, 7, 0), (M, 2, 1),)),
    (5, 4, ((O, 4, 1),)),
    (5, 5, ((O, 8, 0), (X, 5, 0),)),
    (6, 1, ((O, 5, 1), (M, 1, 2),)),
    (6, 3, ((O, 1, 3),)),
    (6, 4, ((G, 1, 3), (O, 6, 1), (M, 4, 1),)),
    (6, 6, ((G, 2, 2), (M, 3, 1), (O, 2, 2),)),
    (7, 3, ((M, 2, 2),)),
    (7, 6, ((X, 6, 0), (G, 3, 2), (O, 3, 2),)),
    (8, 1, ((M, 3, 2), (O, 8, 1), (G, 2, 3), (G, 1, 4),)),
    (8, 2, ((O, 5, 2),)),
    (8, 6, ((O, 4, 2), (X, 5, 1), (O, 7, 1), (G, 4, 2), (O, 2, 3), (O, 1, 4),)),
    (9, 0, ((M, 4, 2),)),
    (9, 3, ((O, 3, 3),)),
    (9, 4, ((X, 6, 1), (X, 7, 0), (G, 3, 3), (O, 6, 2), (O, 2, 4), (O, 1, 5), (G, 2, 4), (G, 1, 5),)),
    (10, 0, ((X, 8, 0), (O, 4, 3), (M, 1, 3), (X, 5, 2), (O, 7, 2), (G, 4, 3), (G, 3, 4), (O, 3, 4),)),
    (10, 3, ((X, 7, 1), (O, 8, 2),)),
    (10, 5, ((X, 8, 1), (M, 2, 3),)),
    (11, 0, ((O, 5, 3), (O, 2, 5),)),
    (11, 3, ((O, 4, 4), (M, 1, 4), (G, 2, 5), (G, 4, 4),)),
    (11, 4, ((O, 3, 5),)),
)
TAIL = (
    (O, 5, 4), (G, 3, 5), (X, 6, 2), (M, 3, 3), (O, 6, 3), (O, 4, 5), (M, 2, 4), (M, 1, 5), (G, 4, 5), (M, 4, 3),
    (O, 5, 5), (O, 6, 4), (O, 7, 3), (M, 3, 4), (O, 8, 3), (X, 5, 3), (O, 6, 5), (M, 2, 5), (M, 4, 4), (MEET, 0, 0),
    (PART, 0, 0), (PART, 1, 0), (S, 1, 0), (X, 5, 4), (X, 7, 2), (O, 7, 4), (M, 3, 5), (PART, 2, 0), (PART, 3, 0),
    (O, 8, 4), (PART, 4, 0), (X, 6, 3), (X, 8, 2), (PART, 5, 0), (SMALL, 0, 0), (O, 7, 5), (M, 4, 5), (BLOCK, 0, 0),
    (SMALL, 1, 0), (S, 2, 0), (X, 6, 4), (O, 8, 5), (BLOCK, 1, 0), (BLOCK, 2, 0), (X, 5, 5), (BLOCK, 3, 0), (S, 3, 0),
    (SMALL, 2, 0), (S, 4, 0), (FINAL, 0, 0), (SMALL, 3, 0), (S, 5, 0), (FINAL, 1, 0), (X, 6, 5), (X, 7, 3),
    (SMALL, 4, 0), (X, 8, 3), (X, 7, 4), (FINAL, 2, 0), (S, 6, 0), (FINAL, 3, 0), (SMALL, 5, 0), (X, 8, 4),
    (FINAL, 4, 0), (FINAL, 5, 0), (X, 7, 5), (S, 7, 0), (X, 8, 5), (S, 8, 0),
)


class Route:
    def __init__(self, bits, rows):
        me = lax.axis_index("dp")
        mine = [(me // bit) % 2 for bit in bits]
        self.partner = [me + bit - 2 * bit * v for bit, v in zip(bits, mine)]
        self.size = [rows // 2 ** (stage + 1) for stage in range(len(bits))]
        self.base = [0]
        for n, v in zip(self.size, mine):
            self.base.append(self.base[-1] + v * n)
        self.away = [self.base[s] + (1 - mine[s]) * self.size[s] for s in range(len(bits))]


def even(v):
    return v if isinstance(v, int) else pl.multiple_of(v, 16)


def block(index):
    return pl.ds(index * WIDTH if isinstance(index, int) else pl.multiple_of(index * WIDTH, WIDTH), WIDTH)


class Reduction:
    def __init__(self, r):
        self.r = r
        self.src = (r.o_src, r.g_src, r.m_src, r.s_src, r.t_src)
        self.came = (
            (r.o_r0, r.o_r1, r.o_r2, r.o_r3), (r.g_r0, r.g_r1, r.g_r2, r.g_r3), (r.m_r0, r.m_r1, r.m_r2, r.m_r3),
            (r.s_r0, r.s_r1, r.s_r2, r.s_r3), (r.t_r0, r.t_r1, r.t_r2, r.t_r3),
        )
        model = r.g_src.shape[1]
        self.routes = {order: (Route(order, r.o_src.shape[1]), Route(order, model)) for order in (X_FIRST, Z_FIRST)}

    def route(self, kind, g):
        turns = {O: O_TURNS, S: S_TURNS, T: S_TURNS}.get(kind, X_TURNS)
        order = Z_FIRST if isinstance(g, int) and turns[g] else X_FIRST
        return self.routes[order][0 if kind == O else 1]

    def slot(self, kind, g):
        return 0 if kind in (S, T) else (g % RING if isinstance(g, int) else lax.rem(g, RING))

    def landing(self, kind, g):
        return 0 if kind in (S, T) else (g % LANDINGS if isinstance(g, int) else lax.rem(g, LANDINGS))

    def place(self, kind, g):
        return g if kind in (O, X) else 0

    def halve(self, kind, s, g):
        r, route, slot, landing = self.r, self.route(kind, g), self.slot(kind, g), self.landing(kind, g)
        return pltpu.make_async_remote_copy(
            src_ref=self.src[kind].at[slot, pl.ds(even(route.away[s]), route.size[s]), :],
            dst_ref=self.came[kind][s].at[landing],
            send_sem=r.send_sem.at[kind, s, landing], recv_sem=r.recv_sem.at[kind, s, landing],
            device_id={"dp": route.partner[s]}, device_id_type=MESH,
        )

    def add(self, kind, s, g):
        route, slot, landing = self.route(kind, g), self.slot(kind, g), self.landing(kind, g)
        src, came = self.src[kind], self.came[kind][s]
        n = route.size[s]
        step = 16 if kind == O else 96

        def some(j, _):
            here = pl.ds(pl.multiple_of(route.base[s + 1] + j * step, 16), step)
            there = pl.ds(pl.multiple_of(j * step, 16), step)
            src[slot, here, :] += came[landing, there, :]
            return 0

        lax.fori_loop(0, n // step, some, 0)

    def target(self, kind, s, g):
        r, route = self.r, self.route(kind, g)
        if kind == O:
            return r.gout.at[pl.ds(even(g * WIDTH + route.base[s + 1]), route.size[s]), :]
        if kind == X:
            return r.gmix.at[pl.ds(route.base[s + 1], route.size[s]), :, block(g)]
        return (r.gstate_w if kind == S else r.gstep_w).at[pl.ds(even(route.base[s + 1]), route.size[s]), :]

    def reduced(self, kind, g):
        if kind in (O, X):
            return (self.r.o_own if kind == O else self.r.x_own).at[g]
        route = self.route(kind, g)
        return self.src[kind].at[0, pl.ds(even(route.base[4]), route.size[3]), :]

    def gather(self, kind, s, g):
        i, place = (O, X, S, T).index(kind), self.place(kind, g)
        return pltpu.make_async_remote_copy(
            src_ref=self.reduced(kind, g) if s == 3 else self.target(kind, s, g), dst_ref=self.target(kind, s, g),
            send_sem=self.r.ag_send.at[i, s, place], recv_sem=self.r.ag_recv.at[i, s, place],
            device_id={"dp": self.route(kind, g).partner[s]}, device_id_type=MESH,
        )

    def keep(self, kind, g):
        sem = self.r.copy_sem.at[(O, X, S, T).index(kind), self.place(kind, g)]
        return pltpu.make_async_copy(self.reduced(kind, g), self.target(kind, 3, g), sem)

    def event(self, kind, n, g):
        for each in (S, T) if kind == S else (kind,):
            self.piece(each, n, g)

    def piece(self, kind, n, g):
        r = self.r
        if n == 0:
            self.halve(kind, 0, g).start()
        elif n < 4:
            self.halve(kind, n - 1, g).wait()
            self.add(kind, n - 1, g)
            self.halve(kind, n, g).start()
        elif n == 4:
            self.halve(kind, 3, g).wait()
            self.add(kind, 3, g)
            slot = self.slot(kind, g)
            route = self.route(kind, g)
            at = pl.ds(even(route.base[4]), route.size[3])
            if kind == G:
                r.g_own[g] = r.g_src[slot, at, :]
            else:
                if kind == M:
                    r.x_own[g, :, 0, :] = r.g_own[g]
                    r.x_own[g, :, 1, :] = r.m_src[slot, at, :]
                    kind = X
                if kind == O:
                    r.o_own[g] = r.o_src[slot, at, :]
                self.keep(kind, g).start()
                self.gather(kind, 3, g).start()
        else:
            s = 8 - n
            self.gather(kind, s, g).wait()
            if s == 3:
                self.keep(kind, g).wait()
            if s > 0:
                self.gather(kind, s - 1, g).start()


def by_rows(rows, step, body):
    def some(i, _):
        body(pl.ds(pl.multiple_of(i * step, step), step))
        return 0

    lax.fori_loop(0, rows // step, some, 0)


def twice(v):
    return jnp.concatenate([v, v], axis=1)


def to_column(v, chooser):
    high, low = two_parts(v)
    return tn(high, chooser) + tn(low, chooser)


def group_at(k, groups):
    late, others = k - 2 * WHOLE, groups - WHOLE
    g = jnp.where(late < 0, k // 2, WHOLE + lax.rem(jnp.maximum(late, 0), others))
    return g, jnp.where(late < 0, lax.rem(k, 2) == 0, late < others)


def backward_kernel(groups, *refs):
    a, b = len(Inputs._fields), len(Inputs._fields) + len(Outputs._fields)
    parts = Inputs(*refs[:a]), Outputs(*refs[a:b]), Scratch(*refs[b:])
    r = types.SimpleNamespace(**{name: ref for part in parts for name, ref in part._asdict().items()})
    k = pl.program_id(0)
    group, opens = group_at(k, groups)
    seq = r.normed_t.shape[1]
    model = r.cot.shape[1]
    chunks = seq // CHUNK
    state = r.b.shape[1]
    blocks = model // WIDTH
    me = lax.axis_index("dp")
    near = lax.axis_index("tensor")
    reduction = Reduction(r)

    def beside(src, dst, send, recv):
        return pltpu.make_async_remote_copy(
            src_ref=src, dst_ref=dst, send_sem=send, recv_sem=recv, device_id={"tensor": 1 - near}, device_id_type=MESH
        )

    def rows_of(half):
        return pl.ds(half * (seq // 2), seq // 2)

    def bc_copy(half):
        at = rows_of(half)
        return beside(r.gbc_low.at[at, :], r.gbc_there.at[at, :], r.near_send.at[0, half], r.near_recv.at[0, half])

    def inner_copy(half):
        at = rows_of(half)
        return beside(r.inner_row.at[:, at], r.inner_there.at[:, at], r.near_send.at[1, half], r.near_recv.at[1, half])

    def sums_copy():
        return beside(r.sums, r.sums_there, r.sums_send, r.sums_recv)

    def product_copy():
        return beside(r.product, r.product_there, r.product_send, r.product_recv)

    def part_copy(j, half):
        at = rows_of(half)
        return beside(r.mine.at[j, at, :], r.there.at[j, at, :], r.part_send.at[half, j], r.part_recv.at[half, j])

    def part_store(j, half):
        return pltpu.make_async_copy(r.stage.at[turn(j)], r.mine.at[j, rows_of(half), :], r.stage_sem.at[turn(j)])

    def turn(j):
        return j % 2 if isinstance(j, int) else lax.rem(j, 2)

    def load_w(j):
        return pltpu.make_async_copy(r.w.at[:, block(j), :], r.w_block.at[turn(j)], r.load_sem.at[0, turn(j)])

    def load_narrow(j):
        return [
            pltpu.make_async_copy(src.at[block(j), :], dst.at[turn(j)], r.narrow_sem.at[n, turn(j)])
            for n, (src, dst) in enumerate(((r.state_w, r.state_block), (r.step_w, r.step_block)))
        ]

    def load_tokens(j):
        return pltpu.make_async_copy(r.tokens.at[:, block(j)], r.token_block.at[turn(j)], r.load_sem.at[1, turn(j)])

    def start_loads(j):
        load_w(j).start()
        load_tokens(j).start()
        for load in load_narrow(j):
            load.start()

    def load_there(j):
        return pltpu.make_async_copy(r.there.at[j], r.scaled, r.load_sem.at[2, 0])

    def load_gate(g):
        return pltpu.make_async_copy(r.gate.at[:, block(g)], r.gate_now, r.now_sem.at[0])

    def load_ow(g):
        return pltpu.make_async_copy(r.ow.at[block(g), :], r.ow_now, r.now_sem.at[1])

    def load_mine(j):
        return pltpu.make_async_copy(r.mine.at[j], r.gate_low.at[:, block(j)], r.load_sem.at[2, 1])

    def load_state():
        return pltpu.make_async_copy(r.state_pre, r.gs.at[8:, :], r.load_sem.at[2, 1])

    def store_tokens(j):
        return pltpu.make_async_copy(r.mix_low.at[:, block(j)], r.gtokens.at[:, block(j)], r.store_sem.at[j])

    def small_copy(i):
        bit = BITS[i]
        return pltpu.make_async_remote_copy(
            src_ref=r.small, dst_ref=r.small_there.at[i], send_sem=r.small_send.at[i], recv_sem=r.small_recv.at[i],
            device_id={"dp": me + bit - 2 * bit * ((me // bit) % 2)}, device_id_type=MESH,
        )

    def small_near():
        return beside(r.small.at[8:16, :], r.small_last, r.small_send.at[4], r.small_recv.at[4])

    def poll(place):
        for step, where, events in MAIN:
            if where == place:

                @pl.when(k == step)
                def _():
                    for kind, n, g in events:
                        reduction.event(kind, n, g)

    def first_step():
        load_ow(0).start()
        load_gate(0).start()
        barrier = pltpu.get_barrier_semaphore()
        for bit in BITS:
            partner = me + bit - 2 * bit * ((me // bit) % 2)
            pl.semaphore_signal(barrier, inc=1, device_id={"dp": partner}, device_id_type=MESH)
        pl.semaphore_signal(barrier, inc=1, device_id={"tensor": 1 - near}, device_id_type=MESH)
        for ref in (r.gscores, r.decay_sums, r.inner_sums, r.gbc, r.small, r.saved, r.kept_carry, r.kept_partial):
            ref[...] = jnp.zeros_like(ref)
        pl.semaphore_wait(barrier, 5)
        sums_copy().start()
        product_copy().start()
        sums_copy().wait()
        row = lax.broadcasted_iota(jnp.int32, (16, 2 * LANES), 0)
        lane = lax.broadcasted_iota(jnp.int32, (16, 2 * LANES), 1)
        chooser = (row == lane // LANES * 8).astype(BF16)
        full = 2 * groups * WIDTH

        def factors(at):
            both = to_column(r.sums[:, at] + r.sums_there[:, at], chooser) * (1.0 / full)
            inverse = lax.rsqrt(both[:, :LANES] + EPSILON)
            r.factor[0, at, :] = inverse
            r.factor[1, at, :] = inverse * inverse * inverse * both[:, LANES:]

        by_rows(seq, CHUNK, factors)

    def gating(at, dy):
        lanes = block(group)
        inverse, coefficient = twice(r.factor[0, at, :]), twice(r.factor[1, at, :])
        gate, y, gs, gain = r.gate_now[at, :], r.y[at, :], r.gs[at, :], r.gain[...]
        sig = sigmoid(gate)
        silu = gate * sig
        gated = y * silu
        hat = gated * inverse
        r.scaled[at, :] = (hat * gain).astype(BF16)
        r.kept_partial[group, 0] += fold(gs * hat)
        ggated = inverse * (gs * gain) - gated * coefficient
        dy[...] = (ggated * silu).astype(BF16)
        ggate = ggated * y * (sig + silu * (1.0 - sig))
        r.gate_low[at, lanes] = ggate.astype(BF16)
        inner = ggate * gate
        r.inner_sums[at, :] += inner[:, :LANES] + inner[:, LANES:]

    def scan_chunk(c, here, dy, g, chooser, lower, first):
        start = pl.multiple_of(c * CHUNK, CHUNK)
        at = pl.ds(start, CHUNK)
        around = r.mix.at[pl.ds(start, CHUNK + 8), :]
        shifted = [around[5 + t : 5 + t + CHUNK, :] for t in range(4)]
        summed = r.bias[...] + sum(r.taps[t : t + 1, :] * shifted[t] for t in range(4))
        sig = sigmoid(summed)
        x = summed * sig
        step_e = r.step_e[here, :]
        cum = pairwise(r.cum_b, here, first)
        ecum = jnp.exp(cum)
        toend = jnp.exp(cum[CHUNK - 1 :, :] - cum)
        xs = x * step_e
        u = xs.astype(BF16)
        weighted = (xs * toend).astype(BF16)
        gy_low = dy[...]
        gy = gy_low.astype(F32)
        gy_across = (gy * ecum).astype(BF16)
        gstate = r.kept_carry[g]
        gstate_low = gstate.astype(BF16)
        entering = r.entering[0, lax.rem(c, chunks // 2)]
        last = ecum[CHUNK - 1 :, :]
        r.gbc[at, state:] += nt(gy_across, entering)
        r.gbc[at, :state] += nt(weighted, gstate_low)
        from_state = nn(r.b[at, :], gstate_low)
        to_output = nn(r.c[at, :], entering)
        kept = weighted.astype(F32) * from_state
        state_dot = jnp.sum(kept, axis=0, keepdims=True) + last * jnp.sum(
            entering.astype(F32) * gstate, axis=0, keepdims=True
        )
        r.kept_carry[g] = gstate * last + nn(r.c_t[c], gy_across)
        scores = r.scores[c]
        gscore = jnp.zeros((CHUNK, CHUNK), F32)
        parts = []
        for pair in range(GROUP_HEADS // 2):
            lanes = slice(pair * LANES, (pair + 1) * LANES)
            gmixing = nt(gy_low[:, lanes], both_halves(u[:, lanes], first))
            mixing = []
            for j in range(2):
                h = 2 * pair + j
                decay = decay_of(r.cum_b[here, h * LANES : (h + 1) * LANES], r.cum_t, h, at, lower)
                gscore = gscore + gmixing[:, j * CHUNK : (j + 1) * CHUNK] * decay
                mixing.append((scores * decay).astype(BF16))
            back = tn(jnp.concatenate(mixing, axis=1), gy_low[:, lanes])
            parts.append(jnp.where(first, back[:CHUNK], back[CHUNK:]))
        r.gscores[c] += gscore
        gu = jnp.concatenate(parts, axis=1)
        skip = r.skip[...]
        change = (
            gy * (r.y[at, :] - skip * x - ecum * to_output)
            + gy_across.astype(F32) * to_output
            - u.astype(F32) * gu
            - kept
        )
        gu = gu + from_state * toend
        row = lax.broadcasted_iota(jnp.int32, change.shape, 0)
        change = change + jnp.where(row == CHUNK - 1, state_dot, 0.0)
        r.decay_sums[at, :] += nn(jnp.concatenate([*two_parts(change), *two_parts(x * gu)], axis=1), chooser)
        gx = gu * step_e + skip * gy
        gsum = gx * (sig + x * (1.0 - sig))
        r.dz[at, :] = gsum
        r.kept_partial[g, 1] += fold(gy * x)
        r.kept_partial[g, 2] += fold(gsum)
        for t in range(4):
            r.kept_partial[g, 3 + t] += fold(gsum * shifted[t])
        after = r.dz.at[pl.ds(start, CHUNK + 8), :]
        gmix = sum(r.taps[t : t + 1, :] * after[3 - t : 3 - t + CHUNK, :] for t in range(4))
        r.mix_low[at, block(g)] = gmix.astype(BF16)
        inner = gmix * shifted[3]
        r.inner_sums[at, :] += inner[:, :LANES] + inner[:, LANES:]

    def early_room(g):
        return jnp.maximum(g - WHOLE + 1, 0)

    def gate_step():
        slot = lax.rem(group, RING)

        load_ow(group).wait()

        def grad_scaled(at):
            r.gs[at, :] = nt(r.cot[at, :], r.ow_now[...])

        by_rows(seq, 4 * CHUNK, grad_scaled)
        more = group + 1 < groups
        pl.when(more)(lambda: load_ow(group + 1).start())
        poll(6)
        load_gate(group).wait()
        for half, place in ((0, early_room(group)), (1, groups - WHOLE + 1)):

            def some(i, _):
                start = pl.multiple_of(i * CHUNK, CHUNK)
                at = pl.ds(pl.multiple_of(half * (seq // 2) + start, CHUNK), CHUNK)
                gating(at, r.dy.at[place, pl.ds(start, CHUNK), :])
                return 0

            lax.fori_loop(0, chunks // 2, some, 0)
        pl.when(more)(lambda: load_gate(group + 1).start())
        r.o_src[slot] = tn(r.scaled[...], r.cot[...]).astype(BF16)
        reduction.event(O, 0, group)
        poll(1)
        r.g_src[slot] = nn(r.normed_t[...], r.gate_low[:, block(group)]).astype(BF16)
        reduction.event(G, 0, group)

    def scan_step():
        g = group
        half = jnp.where(opens, 1, 0)
        each, wide, chooser = spread(g, HEAD), spread(g, LANES), gather_heads(g)
        lower, first = masks()
        edge = pl.ds(pl.multiple_of((half + 1) * (seq // 2), 8), 8)
        r.dz[edge, :] = r.saved[g]
        place = jnp.where(opens, groups - WHOLE + 1, early_room(g))

        def chunk(i, _):
            pair = chunks // 4 - 1 - i
            both = pl.ds(pl.multiple_of(half * (seq // 2) + pair * 2 * CHUNK, CHUNK), 2 * CHUNK)
            r.cum_b[...] = nn(r.cum3[both, :], wide)
            r.step_e[...] = nn(r.step3[both, :], each)
            for j in (1, 0):
                dy = r.dy.at[place, pl.ds(pl.multiple_of((2 * pair + j) * CHUNK, CHUNK), CHUNK), :]
                here = slice(j * CHUNK, (j + 1) * CHUNK)
                scan_chunk(half * (chunks // 2) + 2 * pair + j, here, dy, g, chooser, lower, first)

            @pl.when(i == 0)
            def _():
                poll(3)

            return 0

        lax.fori_loop(0, chunks // 4, chunk, 0)
        r.saved[g] = r.dz[pl.ds(pl.multiple_of(half * (seq // 2), 8), 8), :]

    def mix_step():
        g = group
        r.m_src[lax.rem(g, RING)] = nn(r.normed_t[...], r.mix_low[:, block(g)]).astype(BF16)
        reduction.event(M, 0, g)
        r.small[0:8, block(g)] = jnp.concatenate(
            [jnp.sum(r.kept_partial[g, i], axis=0, keepdims=True) for i in range(7)] + [jnp.zeros((1, WIDTH), F32)], axis=0
        )

    def finish(half):
        upper = (
            lax.broadcasted_iota(jnp.int32, (CHUNK, CHUNK), 0) <= lax.broadcasted_iota(jnp.int32, (CHUNK, CHUNK), 1)
        ).astype(F32)
        lane = lax.broadcasted_iota(jnp.int32, (CHUNK, LANES), 1)
        zero = jnp.zeros((8, LANES), F32)

        def some(i, totals):
            c = half * (chunks // 2) + i
            at = pl.ds(pl.multiple_of(c * CHUNK, CHUNK), CHUNK)
            gscore = r.gscores[c]
            high = gscore.astype(BF16)
            low = (gscore - high.astype(F32)).astype(BF16)
            r.gbc_low[at, state:] = (r.gbc[at, state:] + nn(high, r.b[at, :]) + nn(low, r.b[at, :])).astype(BF16)
            r.gbc_low[at, :state] = (r.gbc[at, :state] + tn(high, r.c[at, :]) + tn(low, r.c[at, :])).astype(BF16)
            sums = r.decay_sums[at, :]
            of_step = jnp.where(lane < LANES // 2, pltpu.roll(sums, LANES // 2, 1), 0.0)
            gdecay = jnp.dot(
                upper, jnp.where(lane < LANES // 2, sums, 0.0), precision=HIGHEST, preferred_element_type=F32
            )
            gstep = (gdecay * r.rate[...] + of_step) * sigmoid(r.step_pre[at, :])
            totals = (
                totals[0] + fold(gstep),
                totals[1] + fold(gdecay * softplus(r.step_pre[at, :]) * r.rate[...]),
            )
            r.gstep_low[at, :] = gstep.astype(BF16)
            inner = r.inner_sums[at, :] + gstep * (r.step_pre[at, :] - r.step_bias[...])
            r.inner_row[:, at] = row_sums(inner)
            return totals

        totals = lax.fori_loop(0, chunks // 2, some, (zero, zero))
        bc_copy(half).start()
        inner_copy(half).start()
        if half == 1:
            load_state().start()
        for j in range(2):
            start_loads(j)
        r.small[13:15, :LANES] += jnp.concatenate([jnp.sum(total, axis=0, keepdims=True) for total in totals], axis=0)

    def meet(half):
        bc_copy(half).wait()
        inner_copy(half).wait()
        padded = r.gs
        if half == 1:
            load_state().wait()
            padded[0:8, :] = jnp.zeros((8, WIDTH), F32)
        edge = pl.ds((half + 1) * (seq // 2), 8)
        r.dz[edge, :] = r.saved[groups]
        top = (lax.broadcasted_iota(jnp.int32, (8, LANES), 0) == 0).astype(BF16)
        zero = jnp.zeros((8, WIDTH), F32)

        def some(i, totals):
            c = (half + 1) * (chunks // 2) - 1 - i
            start = pl.multiple_of(c * CHUNK, CHUNK)
            at = pl.ds(start, CHUNK)
            around = padded.at[pl.ds(start, CHUNK + 8), :]
            shifted = [around[5 + t : 5 + t + CHUNK, :] for t in range(4)]
            summed = r.state_bias[...] + sum(r.state_taps[t : t + 1, :] * shifted[t] for t in range(4))
            sig = sigmoid(summed)
            gact = r.gbc_low[at, :].astype(F32) + r.gbc_there[at, :].astype(F32)
            gsum = gact * (sig + summed * sig * (1.0 - sig))
            r.dz[at, :] = gsum
            totals = tuple(total + fold(gsum * v) for total, v in zip(totals, shifted)) + (totals[4] + fold(gsum),)
            after = r.dz.at[pl.ds(start, CHUNK + 8), :]
            gstate = sum(r.state_taps[t : t + 1, :] * after[3 - t : 3 - t + CHUNK, :] for t in range(4))
            r.gbc_low[at, :] = gstate.astype(BF16)
            column_of = to_column(r.inner_row[:, at] + r.inner_there[:, at], top)
            column_of = column_of + jnp.sum(gstate * shifted[3], axis=1, keepdims=True)
            rms = r.rms[at, :]
            r.decay_sums[at, :] = rms * rms * column_of * (1.0 / model)
            return totals

        totals = lax.fori_loop(0, chunks // 2, some, (zero,) * 5)
        r.saved[groups] = r.dz[pl.ds(half * (seq // 2), 8), :]
        r.small[8:13, :WIDTH] += jnp.concatenate([jnp.sum(total, axis=0, keepdims=True) for total in totals], axis=0)
        if half == 0:
            r.s_src[0] = nn(r.normed_t[...], r.gbc_low[...]).astype(BF16)
            r.t_src[0] = nn(r.normed_t[...], r.gstep_low[...]).astype(BF16)
            reduction.event(S, 0, 0)

    def grad_normed(j, half):
        load_w(j).wait()
        load_tokens(j).wait()
        for load in load_narrow(j):
            load.wait()
        share = pl.ds(pl.multiple_of(near * state, LANES), state)
        at = rows_of(half)
        part = (
            nt(r.gate_low[at, :], r.w_block[turn(j), 0])
            + nt(r.mix_low[at, :], r.w_block[turn(j), 1])
            + nt(r.gstep_low[at, :], r.step_block[turn(j)])
            + nt(r.gbc_low[at, share], r.state_block[turn(j), :, share])
        )
        r.stage[turn(j)] = part.astype(BF16)
        part_store(j, half).start()
        total = fold(part * r.token_block[turn(j), at, :].astype(F32) * twice(r.rms[at, :]))
        r.small[15:16, block(j)] += jnp.sum(total, axis=0, keepdims=True)
        part_store(j, half).wait()
        part_copy(j, half).start()
        if isinstance(j, int):
            if j + 2 < blocks:
                start_loads(j + 2)
            else:
                load_tokens(j + 2 - blocks).start()
        else:
            pl.when(j + 2 < blocks)(lambda: start_loads(j + 2))

    def grad_tokens(j):
        for half in (1, 0):
            part_copy(j, half).wait()
        load_there(j).start()
        load_mine(j).start()
        load_tokens(j).wait()
        load_there(j).wait()
        load_mine(j).wait()

        def some(at):
            whole = r.gate_low[at, block(j)].astype(F32) + r.scaled[at, :].astype(F32)
            pulled = twice(r.rms[at, :]) * (whole * r.norm_gain[:, block(j)])
            pulled = pulled - r.token_block[turn(j), at, :].astype(F32) * twice(r.decay_sums[at, :])
            r.mix_low[at, block(j)] = (r.cot[at, block(j)].astype(F32) + pulled).astype(BF16)

        by_rows(seq, CHUNK, some)
        store_tokens(j).start()
        if j + 2 < blocks:
            load_tokens(j + 2).start()

    def small_event(n):
        if 0 < n < 5:
            small_copy(n - 1).wait()
            r.small[...] += r.small_there[n - 1]
        if n < 4:
            small_copy(n).start()
        elif n == 4:
            small_near().start()
        else:
            small_near().wait()
            row = lax.broadcasted_iota(jnp.int32, r.small_last.shape, 0)
            r.small[8:16, :] = r.small[8:16, :] + jnp.where(row == 7, r.small_last[...], 0.0)

    def block_rows(i):
        rows = pl.ds(i * WIDTH, WIDTH)
        room = [r.w_block.at[0, 0, :, :model], r.w_block.at[0, 1, :, :model], r.w_block.at[1, 0, :, :model]]
        made = r.w_block.at[1, 1, :, :model]
        if i == 0:
            product_copy().wait()
        loads = [
            pltpu.make_async_copy(src.at[rows, :], dst, r.row_sem.at[n])
            for n, (src, dst) in enumerate(zip((r.product, r.product_there, r.tokens), room))
        ]
        for load in loads:
            load.start()
        store = lambda n: pltpu.make_async_copy(made, r.block_out.at[pl.ds(n * WIDTH, WIDTH), :], r.row_sem.at[3])
        if i > 0:
            store(i - 1).wait()
        for load in loads:
            load.wait()

        def some(at):
            whole = room[0][at, :].astype(F32) + room[1][at, :].astype(F32)
            factor = r.factor[0, pl.ds(pl.multiple_of(i * WIDTH + at.start, 32), 32), :]
            scale = jnp.concatenate([factor] * (model // LANES), axis=1)
            made[at, :] = (room[2][at, :].astype(F32) + scale * whole).astype(BF16)

        by_rows(WIDTH, 32, some)
        store(i).start()
        if (i + 1) * WIDTH == seq:
            store(i).wait()

    def end():
        parts = {FINAL: grad_tokens, SMALL: small_event, BLOCK: block_rows}
        for kind, n, g in TAIL:
            if kind == MEET:
                meet(0)
            elif kind == PART:
                grad_normed(n, 0)
            elif kind in parts:
                parts[kind](n)
            else:
                reduction.event(kind, n, g)
        for j in range(blocks):
            store_tokens(j).wait()

    def early_part():
        meet(1)

        def some(j, _):
            grad_normed(j, 1)
            return 0

        lax.fori_loop(0, blocks, some, 0)

    pl.when(k == 0)(first_step)

    @pl.when(k < 2 * groups)
    def _():
        poll(0)
        pl.when(opens)(gate_step)
        poll(2)
        scan_step()
        poll(4)
        pl.when(jnp.logical_not(opens))(mix_step)
        poll(5)

    pl.when(k == groups + WHOLE - 1)(lambda: finish(1))
    pl.when(k == EARLY)(early_part)
    pl.when(k == 2 * groups - 1)(lambda: finish(0))
    pl.when(k == 2 * groups)(end)


def backward(made, tokens, cotangent, both, out_weight, fwd, weights):
    seq, model = cotangent.shape
    inner = out_weight.shape[0]
    groups = inner // WIDTH
    chunks = seq // CHUNK
    state = made["b"].shape[1]
    two = 2 * state
    blocks = model // WIDTH
    gate, mix, y, entering, product, sums = fwd
    at = lambda k: group_at(jnp.minimum(k, 2 * groups - 1), groups)[0]
    half_at = lambda k: jnp.where(group_at(jnp.minimum(k, 2 * groups - 1), groups)[1], 1, 0)
    once = lambda k: jnp.where(k < 2 * WHOLE, k // 2, jnp.minimum(k - WHOLE, groups - 1))
    shape, vmem, dma = jax.ShapeDtypeStruct, pltpu.VMEM, pltpu.SemaphoreType.DMA
    stream = lambda rows: pl.BlockSpec((rows, WIDTH), lambda k: (0, at(k)))
    outside = pl.BlockSpec(memory_space=pl.ANY)
    values = dict(
        made, cot=cotangent, gate=gate, mix=mix, y=y, entering=entering, ow=out_weight, w=both, tokens=tokens,
        product=product, sums=sums, **weights,
    )
    specs = {
        "gate": outside, "ow": outside, "mix": stream(seq + 8), "y": stream(seq), "taps": stream(4), "bias": stream(1), "skip": stream(1),
        "gain": pl.BlockSpec((1, WIDTH), lambda k: (0, once(k))), "entering": pl.BlockSpec((1, chunks // 2, state, WIDTH), lambda k: (at(k), half_at(k), 0, 0)),
        "cum_t": pl.BlockSpec((8, seq), lambda k: (at(k), 0)),
        "w": outside, "tokens": outside, "state_pre": outside, "product": outside, "state_w": outside, "step_w": outside,
    }
    wide = max(inner, model)
    halves = lambda rows: [rows // 2, rows // 4, rows // 8, rows // 16]
    ring = lambda rows, width, count=LANDINGS: [vmem((count, n, width), BF16) for n in halves(rows)]
    scratch = [
        vmem((seq + 8, WIDTH), F32), vmem((seq + 8, WIDTH), F32),
        vmem((2 * CHUNK, GROUP_HEADS * LANES), F32), vmem((2 * CHUNK, WIDTH), F32), vmem((groups + 1, 8, WIDTH), F32),
        vmem((groups, state, WIDTH), F32), vmem((groups, 7, 8, WIDTH), F32), vmem((groups - WHOLE + 2, seq // 2, WIDTH), BF16),
        vmem((2, seq, LANES), F32), vmem((16, seq), F32),
        vmem((chunks, CHUNK, CHUNK), F32), vmem((seq, LANES), F32), vmem((seq, LANES), F32), vmem((seq, two), F32),
        vmem((seq, WIDTH), BF16), vmem((seq, inner), BF16), vmem((seq, inner), BF16), vmem((seq, two), BF16),
        vmem((seq, two), BF16), vmem((8, seq), F32), vmem((8, seq), F32), vmem((seq, LANES), BF16),
        vmem((2, 2, WIDTH, inner), BF16), vmem((2, seq, WIDTH), BF16), vmem((2, seq // 2, WIDTH), BF16),
        vmem((RING, WIDTH, model), BF16), vmem((RING, model, WIDTH), BF16), vmem((RING, model, WIDTH), BF16),
        vmem((1, model, two), BF16), vmem((1, model, LANES), BF16),
        *ring(WIDTH, model), *ring(model, WIDTH), *ring(model, WIDTH), *ring(model, two, 1), *ring(model, LANES, 1),
        vmem((groups, model // 16, WIDTH), BF16), vmem((groups, model // 16, 2, WIDTH), BF16), vmem((groups, WIDTH // 16, model), BF16), vmem((4, 16, wide), F32),
        vmem((8, wide), F32),
        dma((5, 4, LANDINGS)), dma((5, 4, LANDINGS)), dma((4, groups)), dma((4, 4, groups)), dma((4, 4, groups)), dma((2, 2)), dma((2, 2)),
        dma((2, blocks)), dma((2, blocks)), dma((5,)), dma((5,)), dma((3, 2)), dma((blocks,)),
        dma, dma, dma, dma, dma((4,)), dma((2,)), vmem((seq, WIDTH), F32), vmem((WIDTH, model), BF16), dma((2,)),
        vmem((2, WIDTH, two), BF16), vmem((2, WIDTH, LANES), BF16), dma((2, 2)),
    ]
    return pl.pallas_call(
        functools.partial(backward_kernel, groups),
        grid=(2 * groups + 1,),
        in_specs=[specs.get(name, whole_spec(values[name].shape)) for name in Inputs._fields],
        out_specs=[outside] * 9 + [pl.BlockSpec((16, wide), lambda k: (0, 0))],
        out_shape=[
            shape((inner, model), BF16), shape((model, 2, inner), BF16), shape((model, two), BF16), shape((model, LANES), BF16),
            shape((seq, model), BF16), shape((blocks, seq, WIDTH), BF16), shape((blocks, seq, WIDTH), BF16),
            shape((seq, model), BF16), shape((seq, model), BF16),
            shape((16, wide), F32),
        ],
        scratch_shapes=scratch,
        compiler_params=pltpu.CompilerParams(collective_id=0, has_side_effects=True, vmem_limit_bytes=60 * MIB),
        name="backward",
    )(*[values[name] for name in Inputs._fields])


def on_device(
    tokens, norm_gain, mix_weight, state_weight, step_weight, conv_weight, conv_bias, state_conv_weight, state_conv_bias,
    step_bias, log_rate, skip_gain, gate_gain, out_weight, cotangent,
):
    seq, model = tokens.shape
    inner = out_weight.shape[0]
    heads = step_bias.shape[0]
    two = state_weight.shape[1]
    both = jnp.transpose(mix_weight, (1, 0, 2))
    made = prologue(tokens, norm_gain, state_weight, step_weight, state_conv_weight, state_conv_bias, step_bias, log_rate)
    skip = jnp.repeat(skip_gain, HEAD).reshape(1, inner)
    fwd = forward(made, cotangent, both, out_weight, conv_weight, conv_bias, skip, gate_gain)
    weights = {
        "taps": conv_weight, "bias": conv_bias.reshape(1, inner), "skip": skip, "gain": gate_gain.reshape(1, inner),
        "state_taps": state_conv_weight, "state_bias": state_conv_bias.reshape(1, two), "state_w": state_weight,
        "norm_gain": norm_gain.reshape(1, model),
    }
    gout, gmix, gstate_w, gstep_w, grad_tokens, _, _, block_out, _, small = backward(
        made, tokens, cotangent, both, out_weight, fwd, weights
    )
    size = lax.axis_size("dp")
    if size > 16:
        rows = [[i + 16 * j for j in range(size // 16)] for i in range(16)]
        gout, gmix, gstate_w, gstep_w, small = lax.psum((gout, gmix, gstate_w, gstep_w, small), "dp", axis_index_groups=rows)
    low = small.astype(BF16)
    return (
        block_out, grad_tokens, low[15, :model], gmix, gstate_w, gstep_w[:, :heads], low[3:7, :inner], low[2, :inner],
        low[8:12, :two], low[12, :two], low[13, :heads], low[14, :heads],
        jnp.sum(small[1, :inner].reshape(heads, HEAD), axis=1).astype(BF16), low[0, :inner], gout,
    )


def solution(mesh):
    rows, halves = P("dp", None), P("tensor")
    return jax.shard_map(
        on_device,
        mesh=mesh,
        in_specs=(
            rows, P(), P(None, None, "tensor"), P(), P(None, "tensor"), P(None, "tensor"), halves, P(), P(), halves, halves,
            halves, halves, P("tensor", None), rows,
        ),
        out_specs=(
            rows, rows, P(), P(None, None, "tensor"), P(), P(None, "tensor"), P(None, "tensor"), halves, P(), P(), halves,
            halves, halves, halves, P("tensor", None),
        ),
        check_vma=False,
    )
```

```python
import functools
import types
import typing

import jax
import jax.numpy as jnp
from jax import lax
from jax.experimental import pallas as pl
from jax.experimental.pallas import tpu as pltpu
from jax.sharding import PartitionSpec as P

EPSILON = 1e-5
CHUNK = 128
HEAD = 64
GROUP_HEADS = 4
WIDTH = HEAD * GROUP_HEADS
LANES = 128
SLOT = 32
F32, BF16 = jnp.float32, jnp.bfloat16
MIB = 1024 * 1024


def nn(left, right):
    return lax.dot_general(left, right, (((1,), (0,)), ((), ())), preferred_element_type=F32)


def nt(left, right):
    return lax.dot_general(left, right, (((1,), (1,)), ((), ())), preferred_element_type=F32)


def tn(left, right):
    return lax.dot_general(left, right, (((0,), (0,)), ((), ())), preferred_element_type=F32)


def sigmoid(v):
    return jax.nn.sigmoid(v)


def softplus(v):
    return jnp.maximum(v, 0.0) + jnp.log1p(jnp.exp(-jnp.abs(v)))


def split3(v):
    high = v.astype(BF16).astype(F32)
    rest = v - high
    mid = rest.astype(BF16).astype(F32)
    low = rest - mid
    return (high + pltpu.roll(mid, SLOT, 1) + pltpu.roll(low, 2 * SLOT, 1)).astype(BF16)


def spread(group, lanes_each):
    shape = (LANES, GROUP_HEADS * lanes_each)
    slot = lax.broadcasted_iota(jnp.int32, shape, 0)
    lane = lax.broadcasted_iota(jnp.int32, shape, 1)
    hit = (slot % SLOT == group * GROUP_HEADS + lane // lanes_each) & (slot < 3 * SLOT)
    return jnp.where(hit, 1.0, 0.0).astype(BF16)


def gather_heads(group):
    shape = (4 * WIDTH, LANES)
    row = lax.broadcasted_iota(jnp.int32, shape, 0)
    lane = lax.broadcasted_iota(jnp.int32, shape, 1)
    head = group * GROUP_HEADS + row % WIDTH // HEAD
    return jnp.where(lane == head + row // (2 * WIDTH) * (LANES // 2), 1.0, 0.0).astype(BF16)


def two_parts(v):
    high = v.astype(BF16)
    return high, (v - high.astype(F32)).astype(BF16)


def row_sums(v):
    ones = jnp.ones((8, LANES), BF16)
    high, low = two_parts(v)
    return nt(ones, high) + nt(ones, low)


def fold(v):
    return jnp.sum(v.reshape(v.shape[0] // 8, 8, v.shape[1]), axis=0)


class Held(typing.NamedTuple):
    normed_t: object
    state_pre: object
    b: object
    c: object
    c_t: object
    scores: object
    step_pre: object
    step3: object
    cum3: object
    cum_t: object
    rms: object
    vectors: object
    state_rows: object
    heads: object


TAPS, BIAS, GATE_GAIN, NORM_GAIN = 0, 4, 5, 6
RATE, STEP_BIAS, SKIP = 0, 1, 2


def masks():
    row = lax.broadcasted_iota(jnp.int32, (CHUNK, CHUNK), 0)
    col = lax.broadcasted_iota(jnp.int32, (CHUNK, CHUNK), 1)
    return row >= col, col < HEAD


def both_halves(v, first):
    zero = jnp.zeros_like(v)
    return jnp.concatenate([jnp.where(first, v, zero), jnp.where(first, zero, v)], axis=0)


def decay_of(cum_b, cum_t_ref, head, at, lower):
    across = cum_t_ref[head : head + 1, at]
    return jnp.exp(jnp.where(lower, cum_b - across, -1e30))


def pairwise(cum_b, at, first):
    heads = [cum_b[at, h * LANES : (h + 1) * LANES] for h in range(GROUP_HEADS)]
    return jnp.concatenate([jnp.where(first, heads[h], heads[h + 1]) for h in range(0, GROUP_HEADS, 2)], axis=1)


def skip_row(heads_ref, each):
    return nn(split3(heads_ref[...]), each)[SKIP : SKIP + 1, :]


def pack(vectors, state_rows, heads, conv_w, conv_b, gate_gain, norm_gain, state_conv_w, state_conv_b, step_bias, log_rate, skip):
    for ref in (vectors, state_rows, heads):
        ref[...] = jnp.zeros_like(ref)
    count = step_bias.shape[0]
    vectors[TAPS : TAPS + 4, : conv_w.shape[1]] = conv_w[...]
    vectors[BIAS, : conv_b.shape[0]] = conv_b[...]
    vectors[GATE_GAIN, : gate_gain.shape[0]] = gate_gain[...]
    vectors[NORM_GAIN, : norm_gain.shape[0]] = norm_gain[...]
    state_rows[0:4, :] = state_conv_w[...]
    state_rows[4, :] = state_conv_b[...]
    heads[RATE, :count] = -jnp.exp(log_rate[...])
    heads[STEP_BIAS, :count] = step_bias[...]
    heads[SKIP, :count] = skip[...]


def prepare(heads, tokens_ref, state_w_ref, step_t_ref, normed, b_t, halo, step_w, held):
    seq, model = tokens_ref.shape
    vectors_ref, state_rows_ref, heads_ref = held.vectors, held.state_rows, held.heads
    rows = 2 * CHUNK
    halo[0:8, :] = jnp.zeros((8, halo.shape[1]), F32)
    step_w[...] = jnp.zeros_like(step_w)
    step_w[0:heads, :] = step_t_ref[...]
    row = lax.broadcasted_iota(jnp.int32, (CHUNK, CHUNK), 0)
    col = lax.broadcasted_iota(jnp.int32, (CHUNK, CHUNK), 1)
    low_tri = jnp.where(row >= col, 1.0, 0.0).astype(BF16)
    hit = (row % 8 < GROUP_HEADS) & (col % SLOT == row // 8 * GROUP_HEADS + row % 8) & (col < 3 * SLOT)
    places = jnp.where(hit, 1.0, 0.0).astype(BF16)

    def some(i, _):
        start = pl.multiple_of(i * rows, rows)
        here = pl.ds(start, rows)
        values = tokens_ref[here, :].astype(F32)
        inverse = lax.rsqrt(jnp.mean(values * values, axis=1, keepdims=True) + EPSILON)
        held.rms[here, :] = jnp.broadcast_to(inverse, (rows, LANES))
        low = (values * inverse * vectors_ref[NORM_GAIN : NORM_GAIN + 1, :model]).astype(BF16)
        normed[here, :] = low
        held.normed_t[:, here] = low.T
        state_pre = nn(low, state_w_ref[...])
        held.state_pre[here, :] = state_pre
        halo[8 : 8 + rows, :] = state_pre
        summed = state_rows_ref[4:5, :] + sum(state_rows_ref[t : t + 1, :] * halo[5 + t : 5 + t + rows, :] for t in range(4))
        halo[0:8, :] = halo[rows : rows + 8, :]
        act = summed * sigmoid(summed)
        state = act.shape[1] // 2
        b_wide, c_wide = act[:, :state], act[:, state:]
        (b_high, b_low), (c_high, c_low) = two_parts(b_wide), two_parts(c_wide)
        held.b[here, :] = b_high
        held.c[here, :] = c_high
        b_parts = jnp.concatenate([b_high, b_low, b_high], axis=1)
        c_parts = jnp.concatenate([c_high, c_high, c_low], axis=1)
        step_pre = nt(low, step_w[...]) + heads_ref[STEP_BIAS : STEP_BIAS + 1, :]
        held.step_pre[here, :] = step_pre
        lane = lax.broadcasted_iota(jnp.int32, (CHUNK, LANES), 1)
        for part in range(rows // CHUNK):
            at = slice(part * CHUNK, (part + 1) * CHUNK)
            there = pl.ds(pl.multiple_of(start + part * CHUNK, CHUNK), CHUNK)
            c = i * (rows // CHUNK) + part
            b_t[c] = b_wide[at].T.astype(BF16)
            held.c_t[c] = c_wide[at].T.astype(BF16)
            held.scores[c] = nt(c_parts[at], b_parts[at])
            step = jnp.where(lane < heads, softplus(step_pre[at]), 0.0)
            held.step3[there, :] = split3(step)
            sums = nn(low_tri, split3(step * heads_ref[RATE : RATE + 1, :]))
            sums = sums + pltpu.roll(sums, LANES - SLOT, 1) + pltpu.roll(sums, LANES - 2 * SLOT, 1)
            cum3 = split3(jnp.where(lane < heads, sums, 0.0))
            held.cum3[there, :] = cum3
            held.cum_t[:, there] = nt(places, cum3)
        return 0

    lax.fori_loop(0, seq // rows, some, 0)


def forward_kernel(
    heads,
    tokens_ref, state_w_ref, step_t_ref, *rest,
):
    narrow, (w_ref, cot_ref, ow_ref), rest = rest[:9], rest[9:12], rest[12:]
    (
    gate_ref, mix_ref, y_ref, entering_ref, sums_ref, product_ref, *rest
    ) = rest
    n = len(Held._fields)
    outs, held = Held(*rest[:n]), Held(*rest[n : 2 * n])
    normed, b_t, halo, step_w, carry, square, gained, cum_b, step_e, cot, ow, product, sem, held_sem, product_sem = rest[2 * n :]
    group = pl.program_id(0)
    seq = normed.shape[0]
    chunks = seq // CHUNK
    late = [pltpu.make_async_copy(src, dst, sem.at[i]) for i, (src, dst) in enumerate(((cot_ref, cot), (ow_ref, ow)))]
    keeps = [pltpu.make_async_copy(src, dst, held_sem.at[i]) for i, (src, dst) in enumerate(zip(held, outs))]

    @pl.when(group == 0)
    def _():
        for copy in late:
            copy.start()
        square[...] = jnp.zeros_like(square)
        pack(held.vectors, held.state_rows, held.heads, *narrow)
        prepare(heads, tokens_ref, state_w_ref, step_t_ref, normed, b_t, halo, step_w, held)
        for copy in keeps:
            copy.start()

    mix_ref[0:8, :] = jnp.zeros((8, WIDTH), F32)
    mix_ref[8:, :] = nn(normed[...], w_ref[1])
    gate_ref[...] = nn(normed[...], w_ref[0])
    carry[...] = jnp.zeros_like(carry)
    lanes = pl.ds(pl.multiple_of(group * WIDTH, WIDTH), WIDTH)
    vector = lambda row: held.vectors[row : row + 1, lanes]
    each, wide = spread(group, HEAD), spread(group, LANES)
    lower, first = masks()
    cum_b[...] = nn(held.cum3[...], wide)
    step_e[...] = nn(held.step3[...], each)
    skip = skip_row(held.heads, each)
    cum_t = held.cum_t.at[pl.ds(pl.multiple_of(group * 8, 8), 8), :]

    def chunk(c, _):
        start = pl.multiple_of(c * CHUNK, CHUNK)
        at = pl.ds(start, CHUNK)
        around = mix_ref.at[pl.ds(start, CHUNK + 8), :]
        summed = vector(BIAS) + sum(vector(TAPS + t) * around[5 + t : 5 + t + CHUNK, :] for t in range(4))
        x = summed * sigmoid(summed)
        xs = x * step_e[at, :]
        cum = pairwise(cum_b, at, first)
        ecum = jnp.exp(cum)
        weighted = (xs * jnp.exp(cum[CHUNK - 1 :, :] - cum)).astype(BF16)
        u = xs.astype(BF16)
        scores = held.scores[c]
        state = carry[...]
        state_low = state.astype(BF16)
        entering_ref[0, c] = state_low
        y = nn(held.c[at, :], state_low) * ecum + skip * x
        carry[...] = state * ecum[CHUNK - 1 :, :] + nn(b_t[c], weighted)
        parts = []
        for pair in range(GROUP_HEADS // 2):
            mixing = [
                (scores * decay_of(cum_b[at, h * LANES : (h + 1) * LANES], cum_t, h, at, lower)).astype(BF16)
                for h in (2 * pair, 2 * pair + 1)
            ]
            parts.append(nn(jnp.concatenate(mixing, axis=1), both_halves(u[:, pair * LANES : (pair + 1) * LANES], first)))
        y = y + jnp.concatenate(parts, axis=1)
        y_ref[at, :] = y
        gate = gate_ref[at, :]
        gated = y * gate * sigmoid(gate)
        squares = gated * gated
        square[at, :] += squares[:, :LANES] + squares[:, LANES:]
        gained[at, lanes] = (gated * vector(GATE_GAIN)).astype(BF16)
        return 0

    lax.fori_loop(0, chunks, chunk, 0, unroll=chunks)

    @pl.when(group == pl.num_programs(0) - 1)
    def _():
        for copy in late:
            copy.wait()

        def project(i, _):
            at = pl.ds(pl.multiple_of(i * 2 * CHUNK, CHUNK), 2 * CHUNK)
            wide = nn(gained[at, :], ow[...])
            product[at, :] = wide.astype(BF16)
            pltpu.make_async_copy(product.at[at, :], product_ref.at[at, :], product_sem.at[i]).start()
            dots = wide * cot[at, :].astype(F32)
            dots = sum(dots[:, m * LANES : (m + 1) * LANES] for m in range(dots.shape[1] // LANES))
            sums_ref[0:8, at] = row_sums(square[at, :])
            sums_ref[8:16, at] = row_sums(dots)
            return 0

        lax.fori_loop(0, seq // (2 * CHUNK), project, 0)
        for i in range(seq // (2 * CHUNK)):
            at = pl.ds(i * 2 * CHUNK, 2 * CHUNK)
            pltpu.make_async_copy(product.at[at, :], product_ref.at[at, :], product_sem.at[i]).wait()
        for copy in keeps:
            copy.wait()


def whole_spec(shape):
    return pl.BlockSpec(shape, lambda g: (0,) * len(shape), pipeline_mode=pl.Buffered(1))


def column(rows):
    return pl.BlockSpec((rows, WIDTH), lambda g: (0, g))


def forward(tokens, state_weight, step_t, narrow, both, cotangent, out_weight):
    seq, model = cotangent.shape
    inner = out_weight.shape[0]
    groups = inner // WIDTH
    chunks = seq // CHUNK
    two = state_weight.shape[1]
    state = two // 2
    shape, vmem, dma = jax.ShapeDtypeStruct, pltpu.VMEM, pltpu.SemaphoreType.DMA
    held = Held(
        normed_t=((model, seq), BF16), state_pre=((seq, two), F32), b=((seq, state), BF16), c=((seq, state), BF16),
        c_t=((chunks, state, CHUNK), BF16), scores=((chunks, CHUNK, CHUNK), F32), step_pre=((seq, LANES), F32),
        step3=((seq, LANES), BF16), cum3=((seq, LANES), BF16), cum_t=((LANES, seq), F32), rms=((seq, LANES), F32), vectors=((8, max(inner, model)), F32),
        state_rows=((8, two), F32), heads=((8, LANES), F32),
    )
    whole = [tokens, state_weight, step_t, *narrow]
    outside = pl.BlockSpec(memory_space=pl.ANY)
    outs = pl.pallas_call(
        functools.partial(forward_kernel, step_t.shape[0]),
        grid=(groups,),
        in_specs=[whole_spec(item.shape) for item in whole]
        + [pl.BlockSpec((2, model, WIDTH), lambda g: (0, 0, g)), outside, outside],
        out_specs=[
            column(seq), column(seq + 8), column(seq),
            pl.BlockSpec((1, chunks, state, WIDTH), lambda g: (g, 0, 0, 0)), pl.BlockSpec((16, seq), lambda g: (0, 0)),
            outside, *[outside] * len(held),
        ],
        out_shape=[
            shape((seq, inner), F32), shape((seq + 8, inner), F32), shape((seq, inner), F32),
            shape((groups, chunks, state, WIDTH), BF16), shape((16, seq), F32), shape((seq, model), BF16),
            *[shape(*item) for item in held],
        ],
        scratch_shapes=[
            *[vmem(*item) for item in held],
            vmem((seq, model), BF16), vmem((chunks, state, CHUNK), BF16), vmem((8 + 2 * CHUNK, two), F32), vmem((LANES, model), BF16),
            vmem((state, WIDTH), F32), vmem((seq, LANES), F32), vmem((seq, inner), BF16),
            vmem((seq, GROUP_HEADS * LANES), F32), vmem((seq, WIDTH), F32),
            vmem((seq, model), BF16), vmem((inner, model), BF16), vmem((seq, model), BF16),
            dma((2,)), dma((len(held),)), dma((seq // (2 * CHUNK),)),
        ],
        compiler_params=pltpu.CompilerParams(vmem_limit_bytes=56 * MIB),
        name="forward",
    )(*whole, both, cotangent, out_weight)
    return outs[:6], Held(*outs[6:])


class Inputs(typing.NamedTuple):
    normed_t: object
    cot: object
    gate: object
    mix: object
    y: object
    entering: object
    ow: object
    b: object
    c: object
    c_t: object
    scores: object
    step3: object
    cum3: object
    step_pre: object
    rms: object
    state_pre: object
    state_w: object
    step_t: object
    vectors: object
    state_rows: object
    heads: object
    cum_t: object
    w: object
    tokens: object
    sums: object
    product: object


class Outputs(typing.NamedTuple):
    gout: object
    gmix: object
    gstate_w: object
    gstep_w: object
    gtokens: object
    there: object
    mine: object
    block_out: object
    product_there: object
    small: object


class Scratch(typing.NamedTuple):
    gs: object
    dz: object
    cum_b: object
    step_e: object
    saved: object
    kept_carry: object
    kept_partial: object
    dy: object
    factor: object
    sums_there: object
    gscores: object
    decay_sums: object
    inner_sums: object
    gbc: object
    scaled: object
    gate_low: object
    mix_low: object
    gbc_low: object
    gbc_there: object
    inner_row: object
    inner_there: object
    gstep_low: object
    w_block: object
    token_block: object
    stage: object
    o_src: object
    g_src: object
    m_src: object
    s_src: object
    t_src: object
    o_r0: object
    o_r1: object
    o_r2: object
    o_r3: object
    g_r0: object
    g_r1: object
    g_r2: object
    g_r3: object
    m_r0: object
    m_r1: object
    m_r2: object
    m_r3: object
    s_r0: object
    s_r1: object
    s_r2: object
    s_r3: object
    t_r0: object
    t_r1: object
    t_r2: object
    t_r3: object
    g_own: object
    x_own: object
    o_own: object
    small_there: object
    small_last: object
    send_sem: object
    recv_sem: object
    copy_sem: object
    ag_send: object
    ag_recv: object
    near_send: object
    near_recv: object
    part_send: object
    part_recv: object
    small_send: object
    small_recv: object
    load_sem: object
    store_sem: object
    sums_send: object
    sums_recv: object
    product_send: object
    product_recv: object
    row_sem: object
    stage_sem: object
    gate_now: object
    ow_now: object
    now_sem: object
    state_block: object
    step_w: object
    skip: object
    normed_now: object
    cot_now: object
    narrow_sem: object


RING = 3
LANDINGS = 2
BITS = (1, 2, 4, 8)
O, G, M, S, T, X, MEET, PART, FINAL, SMALL, BLOCK = range(11)
MESH = pl.DeviceIdType.MESH


STEPS = ((0, 0), (1, 0), (2, 0), (0, 1), (3, 0), (1, 1), (4, 0), (5, 0), (2, 1), (3, 1), (4, 1), (5, 1))
LAST_OPENING = 7
ROOMS = (0, 1, 2, 0, 1, 3,)
X_FIRST, Z_FIRST = (1, 2, 4, 8), (1, 4, 2, 8)
O_TURNS, X_TURNS, S_TURNS = (0, 0, 0, 1, 1, 1,), (0, 0, 0, 0, 0, 0,), (0,)
MAIN = (
    (0, 3, ((O, 1, 0), (G, 1, 0),)),
    (1, 4, ((G, 2, 0), (G, 1, 1), (O, 2, 0), (O, 1, 1),)),
    (2, 2, ((G, 3, 0), (O, 3, 0),)),
    (2, 4, ((G, 2, 1), (G, 1, 2), (O, 2, 1), (O, 1, 2), (O, 4, 0), (G, 4, 0),)),
    (3, 4, ((O, 5, 0), (G, 3, 1),)),
    (3, 5, ((O, 3, 1),)),
    (4, 6, ((M, 1, 0), (G, 2, 2), (G, 4, 1), (O, 2, 2),)),
    (4, 1, ((O, 6, 0), (O, 4, 1),)),
    (4, 3, ((O, 1, 3), (G, 1, 3),)),
    (4, 4, ((G, 3, 2), (O, 3, 2), (O, 5, 1), (M, 2, 0),)),
    (5, 3, ((O, 7, 0),)),
    (5, 4, ((O, 8, 0), (G, 2, 3),)),
    (5, 5, ((O, 4, 2), (G, 4, 2),)),
    (6, 6, ((O, 2, 3), (M, 1, 1),)),
    (6, 1, ((O, 6, 1), (M, 3, 0),)),
    (6, 2, ((G, 3, 3), (O, 1, 4), (O, 5, 2),)),
    (6, 3, ((O, 3, 3), (G, 1, 4), (M, 4, 0),)),
    (7, 0, ((G, 4, 3),)),
    (7, 1, ((O, 4, 3), (M, 2, 1),)),
    (7, 2, ((O, 6, 2), (O, 7, 1),)),
    (7, 3, ((X, 5, 0),)),
    (7, 4, ((O, 8, 1), (O, 5, 3), (G, 2, 4), (G, 1, 5),)),
    (8, 0, ((O, 7, 2), (M, 3, 1), (O, 2, 4), (O, 1, 5),)),
    (8, 3, ((O, 8, 2), (O, 6, 3),)),
    (8, 4, ((G, 3, 4), (M, 4, 1),)),
    (8, 5, ((O, 3, 4), (G, 2, 5),)),
    (9, 0, ((MEET, 0, 1), (M, 1, 2), (X, 6, 0),)),
    (9, 3, ((G, 4, 4), (PART, 0, 1), (O, 4, 4),)),
    (9, 5, ((X, 5, 1), (PART, 1, 1), (G, 3, 5), (O, 5, 4), (O, 2, 5), (M, 2, 2), (M, 1, 3),)),
    (10, 2, ((PART, 2, 1), (O, 7, 3),)),
    (10, 3, ((O, 8, 3), (G, 4, 5),)),
    (10, 4, ((M, 3, 2), (X, 6, 1), (PART, 3, 1), (O, 3, 5), (O, 6, 4), (X, 7, 0),)),
    (10, 5, ((M, 4, 2),)),
    (11, 0, ((PART, 4, 1), (X, 8, 0), (O, 4, 5), (M, 2, 3), (M, 1, 4),)),
    (11, 3, ((PART, 5, 1), (X, 5, 2),)),
    (11, 4, ((O, 5, 5),)),
    (11, 5, ((O, 7, 4), (M, 3, 3),)),
)
TAIL = (
    (X, 7, 1), (O, 8, 4), (M, 2, 4), (M, 1, 5), (M, 4, 3), (O, 6, 5), (X, 6, 2), (X, 8, 1), (M, 3, 4), (X, 5, 3),
    (M, 2, 5), (MEET, 0, 0), (M, 4, 4), (PART, 0, 0), (S, 1, 0), (O, 7, 5), (X, 7, 2), (PART, 1, 0), (M, 3, 5),
    (O, 8, 5), (PART, 2, 0), (X, 8, 2), (X, 5, 4), (X, 6, 3), (PART, 3, 0), (M, 4, 5), (PART, 4, 0), (S, 2, 0),
    (PART, 5, 0), (SMALL, 0, 0), (BLOCK, 0, 0), (SMALL, 1, 0), (X, 5, 5), (X, 6, 4), (FINAL, 0, 0), (S, 3, 0),
    (BLOCK, 1, 0), (X, 7, 3), (BLOCK, 2, 0), (SMALL, 2, 0), (S, 4, 0), (BLOCK, 3, 0), (X, 8, 3), (X, 6, 5), (S, 5, 0),
    (SMALL, 3, 0), (FINAL, 1, 0), (X, 7, 4), (FINAL, 2, 0), (S, 6, 0), (SMALL, 4, 0), (X, 8, 4), (FINAL, 3, 0),
    (FINAL, 4, 0), (SMALL, 5, 0), (FINAL, 5, 0), (X, 7, 5), (X, 8, 5), (S, 7, 0), (S, 8, 0),
)


class Route:
    def __init__(self, bits, rows):
        me = lax.axis_index("dp")
        mine = [(me // bit) % 2 for bit in bits]
        self.partner = [me + bit - 2 * bit * v for bit, v in zip(bits, mine)]
        self.size = [rows // 2 ** (stage + 1) for stage in range(len(bits))]
        self.base = [0]
        for n, v in zip(self.size, mine):
            self.base.append(self.base[-1] + v * n)
        self.away = [self.base[s] + (1 - mine[s]) * self.size[s] for s in range(len(bits))]


def even(v):
    return v if isinstance(v, int) else pl.multiple_of(v, 16)


def block(index):
    return pl.ds(index * WIDTH if isinstance(index, int) else pl.multiple_of(index * WIDTH, WIDTH), WIDTH)


class Reduction:
    def __init__(self, r):
        self.r = r
        self.src = (r.o_src, r.g_src, r.m_src, r.s_src, r.t_src)
        self.came = (
            (r.o_r0, r.o_r1, r.o_r2, r.o_r3), (r.g_r0, r.g_r1, r.g_r2, r.g_r3), (r.m_r0, r.m_r1, r.m_r2, r.m_r3),
            (r.s_r0, r.s_r1, r.s_r2, r.s_r3), (r.t_r0, r.t_r1, r.t_r2, r.t_r3),
        )
        model = r.g_src.shape[1]
        self.routes = {order: (Route(order, r.o_src.shape[1]), Route(order, model)) for order in (X_FIRST, Z_FIRST)}

    def route(self, kind, g):
        turns = {O: O_TURNS, S: S_TURNS, T: S_TURNS}.get(kind, X_TURNS)
        order = Z_FIRST if isinstance(g, int) and turns[g] else X_FIRST
        return self.routes[order][0 if kind == O else 1]

    def slot(self, kind, g):
        return 0 if kind in (S, T) else (g % RING if isinstance(g, int) else lax.rem(g, RING))

    def landing(self, kind, g):
        return 0 if kind in (S, T) else (g % LANDINGS if isinstance(g, int) else lax.rem(g, LANDINGS))

    def place(self, kind, g):
        return g if kind in (O, X) else 0

    def halve(self, kind, s, g):
        r, route, slot, landing = self.r, self.route(kind, g), self.slot(kind, g), self.landing(kind, g)
        return pltpu.make_async_remote_copy(
            src_ref=self.src[kind].at[slot, pl.ds(even(route.away[s]), route.size[s]), :],
            dst_ref=self.came[kind][s].at[landing],
            send_sem=r.send_sem.at[kind, s, landing], recv_sem=r.recv_sem.at[kind, s, landing],
            device_id={"dp": route.partner[s]}, device_id_type=MESH,
        )

    def add(self, kind, s, g):
        route, slot, landing = self.route(kind, g), self.slot(kind, g), self.landing(kind, g)
        src, came = self.src[kind], self.came[kind][s]
        n = route.size[s]
        step = min(n, 64 if kind == O else 384)

        def some(j, _):
            here = pl.ds(pl.multiple_of(route.base[s + 1] + j * step, 16), step)
            there = pl.ds(pl.multiple_of(j * step, 16), step)
            src[slot, here, :] += came[landing, there, :]
            return 0

        lax.fori_loop(0, n // step, some, 0)

    def target(self, kind, s, g):
        r, route = self.r, self.route(kind, g)
        if kind == O:
            return r.gout.at[pl.ds(even(g * WIDTH + route.base[s + 1]), route.size[s]), :]
        if kind == X:
            return r.gmix.at[pl.ds(route.base[s + 1], route.size[s]), :, block(g)]
        return (r.gstate_w if kind == S else r.gstep_w).at[pl.ds(even(route.base[s + 1]), route.size[s]), :]

    def reduced(self, kind, g):
        if kind in (O, X):
            return (self.r.o_own if kind == O else self.r.x_own).at[g]
        route = self.route(kind, g)
        return self.src[kind].at[0, pl.ds(even(route.base[4]), route.size[3]), :]

    def gather(self, kind, s, g):
        i, place = (O, X, S, T).index(kind), self.place(kind, g)
        return pltpu.make_async_remote_copy(
            src_ref=self.reduced(kind, g) if s == 3 else self.target(kind, s, g), dst_ref=self.target(kind, s, g),
            send_sem=self.r.ag_send.at[i, s, place], recv_sem=self.r.ag_recv.at[i, s, place],
            device_id={"dp": self.route(kind, g).partner[s]}, device_id_type=MESH,
        )

    def keep(self, kind, g):
        sem = self.r.copy_sem.at[(O, X, S, T).index(kind), self.place(kind, g)]
        return pltpu.make_async_copy(self.reduced(kind, g), self.target(kind, 3, g), sem)

    def event(self, kind, n, g):
        for each in (S, T) if kind == S else (kind,):
            self.piece(each, n, g)

    def piece(self, kind, n, g):
        r = self.r
        if n == 0:
            self.halve(kind, 0, g).start()
        elif n < 4:
            self.halve(kind, n - 1, g).wait()
            self.add(kind, n - 1, g)
            self.halve(kind, n, g).start()
        elif n == 4:
            self.halve(kind, 3, g).wait()
            self.add(kind, 3, g)
            slot = self.slot(kind, g)
            route = self.route(kind, g)
            at = pl.ds(even(route.base[4]), route.size[3])
            if kind == G:
                r.g_own[g] = r.g_src[slot, at, :]
            else:
                if kind == M:
                    r.x_own[g, :, 0, :] = r.g_own[g]
                    r.x_own[g, :, 1, :] = r.m_src[slot, at, :]
                    kind = X
                if kind == O:
                    r.o_own[g] = r.o_src[slot, at, :]
                self.keep(kind, g).start()
                self.gather(kind, 3, g).start()
        else:
            s = 8 - n
            self.gather(kind, s, g).wait()
            if s == 3:
                self.keep(kind, g).wait()
            if s > 0:
                self.gather(kind, s - 1, g).start()


def by_rows(rows, step, body):
    def some(i, _):
        body(pl.ds(pl.multiple_of(i * step, step), step))
        return 0

    lax.fori_loop(0, rows // step, some, 0)


def twice(v):
    return jnp.concatenate([v, v], axis=1)


def to_column(v, chooser):
    high, low = two_parts(v)
    return tn(high, chooser) + tn(low, chooser)


def group_at(k):
    g, opens = 0, 0
    for step, (group, second) in enumerate(STEPS):
        g = jnp.where(k == step, group, g)
        opens = jnp.where(k == step, 1 - second, opens)
    return g, opens == 1


def backward_kernel(groups, *refs):
    a, b = len(Inputs._fields), len(Inputs._fields) + len(Outputs._fields)
    parts = Inputs(*refs[:a]), Outputs(*refs[a:b]), Scratch(*refs[b:])
    r = types.SimpleNamespace(**{name: ref for part in parts for name, ref in part._asdict().items()})
    k = pl.program_id(0)
    group, opens = group_at(k)
    seq = r.normed_t.shape[1]
    model = r.cot.shape[1]
    chunks = seq // CHUNK
    state = r.b.shape[1]
    blocks = model // WIDTH
    me = lax.axis_index("dp")
    near = lax.axis_index("tensor")
    reduction = Reduction(r)

    def vector(row):
        return r.vectors[row : row + 1, block(group)]

    def beside(src, dst, send, recv):
        return pltpu.make_async_remote_copy(
            src_ref=src, dst_ref=dst, send_sem=send, recv_sem=recv, device_id={"tensor": 1 - near}, device_id_type=MESH
        )

    def rows_of(half):
        return pl.ds(half * (seq // 2), seq // 2)

    def bc_copy(half):
        at = rows_of(half)
        return beside(r.gbc_low.at[at, :], r.gbc_there.at[at, :], r.near_send.at[0, half], r.near_recv.at[0, half])

    def inner_copy(half):
        at = rows_of(half)
        return beside(r.inner_row.at[:, at], r.inner_there.at[:, at], r.near_send.at[1, half], r.near_recv.at[1, half])

    def sums_copy():
        return beside(r.sums, r.sums_there, r.sums_send, r.sums_recv)

    def product_copy():
        return beside(r.product, r.product_there, r.product_send, r.product_recv)

    def part_copy(j, half):
        at = rows_of(half)
        return beside(r.mine.at[j, at, :], r.there.at[j, at, :], r.part_send.at[half, j], r.part_recv.at[half, j])

    def part_store(j, half):
        return pltpu.make_async_copy(r.stage.at[j % 2], r.mine.at[j, rows_of(half), :], r.stage_sem.at[j % 2])

    def load_w(j):
        return pltpu.make_async_copy(r.w.at[:, block(j), :], r.w_block.at[j % 2], r.load_sem.at[0, j % 2])

    def load_narrow(j):
        return pltpu.make_async_copy(r.state_w.at[block(j), :], r.state_block.at[j % 2], r.narrow_sem.at[j % 2])

    def load_tokens(j):
        return pltpu.make_async_copy(r.tokens.at[:, block(j)], r.token_block.at[j % 2], r.load_sem.at[1, j % 2])

    def start_loads(j):
        load_w(j).start()
        load_tokens(j).start()
        load_narrow(j).start()

    def load_there(j):
        return pltpu.make_async_copy(r.there.at[j], r.scaled, r.load_sem.at[2, 0])

    def load_gate(g):
        return pltpu.make_async_copy(r.gate.at[:, block(g)], r.gate_now, r.now_sem.at[0])

    def load_ow(g):
        return pltpu.make_async_copy(r.ow.at[block(g), :], r.ow_now, r.now_sem.at[1])

    def load_cot():
        return pltpu.make_async_copy(r.cot, r.cot_now, r.now_sem.at[2])

    def load_normed():
        return pltpu.make_async_copy(r.normed_t, r.normed_now, r.now_sem.at[3])

    def load_mine(j):
        return pltpu.make_async_copy(r.mine.at[j], r.gate_low.at[:, block(j)], r.load_sem.at[2, 1])

    def load_state():
        return pltpu.make_async_copy(r.state_pre, r.gs.at[8:, :], r.load_sem.at[2, 1])

    def store_tokens(j):
        return pltpu.make_async_copy(r.mix_low.at[:, block(j)], r.gtokens.at[:, block(j)], r.store_sem.at[j])

    def small_copy(i):
        bit = BITS[i]
        return pltpu.make_async_remote_copy(
            src_ref=r.small, dst_ref=r.small_there.at[i], send_sem=r.small_send.at[i], recv_sem=r.small_recv.at[i],
            device_id={"dp": me + bit - 2 * bit * ((me // bit) % 2)}, device_id_type=MESH,
        )

    def small_near():
        return beside(r.small.at[8:16, :], r.small_last, r.small_send.at[4], r.small_recv.at[4])

    def poll(place):
        for step, where, events in MAIN:
            if where == place:

                @pl.when(k == step)
                def _():
                    for kind, n, g in events:
                        if kind == MEET:
                            meet(1)
                        elif kind == PART:
                            grad_normed(n, 1)
                        else:
                            reduction.event(kind, n, g)

    def first_step():
        load_ow(0).start()
        load_cot().start()
        load_gate(0).start()
        load_normed().start()
        r.step_w[...] = jnp.zeros_like(r.step_w)
        r.step_w[0 : r.step_t.shape[0], :] = r.step_t[...]
        barrier = pltpu.get_barrier_semaphore()
        for bit in BITS:
            partner = me + bit - 2 * bit * ((me // bit) % 2)
            pl.semaphore_signal(barrier, inc=1, device_id={"dp": partner}, device_id_type=MESH)
        pl.semaphore_signal(barrier, inc=1, device_id={"tensor": 1 - near}, device_id_type=MESH)
        for ref in (r.gscores, r.decay_sums, r.inner_sums, r.gbc, r.small, r.saved, r.kept_carry, r.kept_partial):
            ref[...] = jnp.zeros_like(ref)
        pl.semaphore_wait(barrier, 5)
        sums_copy().start()
        product_copy().start()
        load_ow(0).wait()
        load_cot().wait()
        grad_scaled()
        sums_copy().wait()
        row = lax.broadcasted_iota(jnp.int32, (16, 2 * LANES), 0)
        lane = lax.broadcasted_iota(jnp.int32, (16, 2 * LANES), 1)
        chooser = (row == lane // LANES * 8).astype(BF16)
        full = 2 * groups * WIDTH

        def factors(at):
            both = to_column(r.sums[:, at] + r.sums_there[:, at], chooser) * (1.0 / full)
            inverse = lax.rsqrt(both[:, :LANES] + EPSILON)
            r.factor[0, at, :] = inverse
            r.factor[1, at, :] = inverse * inverse * inverse * both[:, LANES:]

        by_rows(seq, CHUNK, factors)

    def gating(at, dy):
        lanes = block(group)
        inverse, coefficient = twice(r.factor[0, at, :]), twice(r.factor[1, at, :])
        gate, y, gs, gain = r.gate_now[at, :], r.y[at, :], r.gs[at, :], vector(GATE_GAIN)
        sig = sigmoid(gate)
        silu = gate * sig
        gated = y * silu
        hat = gated * inverse
        r.scaled[at, :] = (hat * gain).astype(BF16)
        r.kept_partial[group, 0] += fold(gs * hat)
        ggated = inverse * (gs * gain) - gated * coefficient
        dy[...] = (ggated * silu).astype(BF16)
        ggate = ggated * y * (sig + silu * (1.0 - sig))
        r.gate_low[at, lanes] = ggate.astype(BF16)
        inner = ggate * gate
        r.inner_sums[at, :] += inner[:, :LANES] + inner[:, LANES:]

    def scan_chunk(c, here, dy, g, chooser, lower, first):
        start = pl.multiple_of(c * CHUNK, CHUNK)
        at = pl.ds(start, CHUNK)
        around = r.mix.at[pl.ds(start, CHUNK + 8), :]
        shifted = [around[5 + t : 5 + t + CHUNK, :] for t in range(4)]
        summed = vector(BIAS) + sum(vector(TAPS + t) * shifted[t] for t in range(4))
        sig = sigmoid(summed)
        x = summed * sig
        step_e = r.step_e[here, :]
        cum = pairwise(r.cum_b, here, first)
        ecum = jnp.exp(cum)
        toend = jnp.exp(cum[CHUNK - 1 :, :] - cum)
        xs = x * step_e
        u = xs.astype(BF16)
        weighted = (xs * toend).astype(BF16)
        gy_low = dy[...]
        gy = gy_low.astype(F32)
        gy_across = (gy * ecum).astype(BF16)
        gstate = r.kept_carry[g]
        gstate_low = gstate.astype(BF16)
        entering = r.entering[0, lax.rem(c, chunks // 2)]
        last = ecum[CHUNK - 1 :, :]
        r.gbc[at, state:] += nt(gy_across, entering)
        r.gbc[at, :state] += nt(weighted, gstate_low)
        from_state = nn(r.b[at, :], gstate_low)
        to_output = nn(r.c[at, :], entering)
        kept = weighted.astype(F32) * from_state
        state_dot = jnp.sum(kept, axis=0, keepdims=True) + last * jnp.sum(
            entering.astype(F32) * gstate, axis=0, keepdims=True
        )
        r.kept_carry[g] = gstate * last + nn(r.c_t[c], gy_across)
        scores = r.scores[c]
        gscore = jnp.zeros((CHUNK, CHUNK), F32)
        parts = []
        for pair in range(GROUP_HEADS // 2):
            lanes = slice(pair * LANES, (pair + 1) * LANES)
            gmixing = nt(gy_low[:, lanes], both_halves(u[:, lanes], first))
            mixing = []
            for j in range(2):
                h = 2 * pair + j
                decay = decay_of(r.cum_b[here, h * LANES : (h + 1) * LANES], r.cum_t, h, at, lower)
                gscore = gscore + gmixing[:, j * CHUNK : (j + 1) * CHUNK] * decay
                mixing.append((scores * decay).astype(BF16))
            back = tn(jnp.concatenate(mixing, axis=1), gy_low[:, lanes])
            parts.append(jnp.where(first, back[:CHUNK], back[CHUNK:]))
        r.gscores[c] += gscore
        gu = jnp.concatenate(parts, axis=1)
        skip = r.skip[0:1, :]
        change = (
            gy * (r.y[at, :] - skip * x - ecum * to_output)
            + gy_across.astype(F32) * to_output
            - u.astype(F32) * gu
            - kept
        )
        gu = gu + from_state * toend
        row = lax.broadcasted_iota(jnp.int32, change.shape, 0)
        change = change + jnp.where(row == CHUNK - 1, state_dot, 0.0)
        r.decay_sums[at, :] += nn(jnp.concatenate([*two_parts(change), *two_parts(x * gu)], axis=1), chooser)
        gx = gu * step_e + skip * gy
        gsum = gx * (sig + x * (1.0 - sig))
        r.dz[at, :] = gsum
        r.kept_partial[g, 1] += fold(gy * x)
        r.kept_partial[g, 2] += fold(gsum)
        for t in range(4):
            r.kept_partial[g, 3 + t] += fold(gsum * shifted[t])
        after = r.dz.at[pl.ds(start, CHUNK + 8), :]
        gmix = sum(vector(TAPS + t) * after[3 - t : 3 - t + CHUNK, :] for t in range(4))
        r.mix_low[at, block(g)] = gmix.astype(BF16)
        inner = gmix * shifted[3]
        r.inner_sums[at, :] += inner[:, :LANES] + inner[:, LANES:]

    def early_room(g):
        room = 0
        for each, number in enumerate(ROOMS):
            room = jnp.where(g == each, number, room)
        return room

    def grad_scaled():
        def some(at):
            r.gs[at, :] = nt(r.cot_now[at, :], r.ow_now[...])

        by_rows(seq, 4 * CHUNK, some)

    def gate_step():
        slot = lax.rem(group, RING)


        @pl.when(k > 0)
        def _():
            load_ow(group).wait()
            grad_scaled()

        more = group + 1 < groups
        pl.when(more)(lambda: load_ow(group + 1).start())
        poll(6)
        load_gate(group).wait()
        for half, place in ((0, early_room(group)), (1, max(ROOMS) + 1)):

            def some(i, _):
                start = pl.multiple_of(i * CHUNK, CHUNK)
                at = pl.ds(pl.multiple_of(half * (seq // 2) + start, CHUNK), CHUNK)
                gating(at, r.dy.at[place, pl.ds(start, CHUNK), :])
                return 0

            lax.fori_loop(0, chunks // 2, some, 0)
        pl.when(more)(lambda: load_gate(group + 1).start())
        r.o_src[slot] = tn(r.scaled[...], r.cot_now[...]).astype(BF16)
        reduction.event(O, 0, group)
        poll(1)
        pl.when(k == 0)(lambda: load_normed().wait())
        r.g_src[slot] = nn(r.normed_now[...], r.gate_low[:, block(group)]).astype(BF16)
        reduction.event(G, 0, group)

    def scan_step():
        g = group
        half = jnp.where(opens, 1, 0)
        each, wide, chooser = spread(g, HEAD), spread(g, LANES), gather_heads(g)
        lower, first = masks()
        r.skip[...] = jnp.broadcast_to(skip_row(r.heads, each), (8, WIDTH))
        edge = pl.ds(pl.multiple_of((half + 1) * (seq // 2), 8), 8)
        r.dz[edge, :] = r.saved[g]
        place = jnp.where(opens, max(ROOMS) + 1, early_room(g))

        def chunk(i, _):
            pair = chunks // 4 - 1 - i
            both = pl.ds(pl.multiple_of(half * (seq // 2) + pair * 2 * CHUNK, CHUNK), 2 * CHUNK)
            r.cum_b[...] = nn(r.cum3[both, :], wide)
            r.step_e[...] = nn(r.step3[both, :], each)
            for j in (1, 0):
                dy = r.dy.at[place, pl.ds(pl.multiple_of((2 * pair + j) * CHUNK, CHUNK), CHUNK), :]
                here = slice(j * CHUNK, (j + 1) * CHUNK)
                scan_chunk(half * (chunks // 2) + 2 * pair + j, here, dy, g, chooser, lower, first)

            @pl.when(i == 0)
            def _():
                poll(3)

            return 0

        lax.fori_loop(0, chunks // 4, chunk, 0)
        r.saved[g] = r.dz[pl.ds(pl.multiple_of(half * (seq // 2), 8), 8), :]

    def mix_step():
        g = group
        r.m_src[lax.rem(g, RING)] = nn(r.normed_now[...], r.mix_low[:, block(g)]).astype(BF16)
        reduction.event(M, 0, g)
        r.small[0:8, block(g)] = jnp.concatenate(
            [jnp.sum(r.kept_partial[g, i], axis=0, keepdims=True) for i in range(7)] + [jnp.zeros((1, WIDTH), F32)], axis=0
        )

    def finish(half):
        upper = (
            lax.broadcasted_iota(jnp.int32, (CHUNK, CHUNK), 0) <= lax.broadcasted_iota(jnp.int32, (CHUNK, CHUNK), 1)
        ).astype(BF16)
        lane = lax.broadcasted_iota(jnp.int32, (CHUNK, LANES), 1)
        zero = jnp.zeros((8, LANES), F32)

        def some(i, totals):
            c = half * (chunks // 2) + i
            at = pl.ds(pl.multiple_of(c * CHUNK, CHUNK), CHUNK)
            gscore = r.gscores[c]
            high = gscore.astype(BF16)
            low = (gscore - high.astype(F32)).astype(BF16)
            r.gbc_low[at, state:] = (r.gbc[at, state:] + nn(high, r.b[at, :]) + nn(low, r.b[at, :])).astype(BF16)
            r.gbc_low[at, :state] = (r.gbc[at, :state] + tn(high, r.c[at, :]) + tn(low, r.c[at, :])).astype(BF16)
            sums = r.decay_sums[at, :]
            of_step = jnp.where(lane < LANES // 2, pltpu.roll(sums, LANES // 2, 1), 0.0)
            gdecay = nn(upper, split3(jnp.where(lane < SLOT, sums, 0.0)))
            gdecay = gdecay + pltpu.roll(gdecay, LANES - SLOT, 1) + pltpu.roll(gdecay, LANES - 2 * SLOT, 1)
            gdecay = jnp.where(lane < SLOT, gdecay, 0.0)
            gstep = (gdecay * r.heads[RATE : RATE + 1, :] + of_step) * sigmoid(r.step_pre[at, :])
            totals = (
                totals[0] + fold(gstep),
                totals[1] + fold(gdecay * softplus(r.step_pre[at, :]) * r.heads[RATE : RATE + 1, :]),
            )
            r.gstep_low[at, :] = gstep.astype(BF16)
            inner = r.inner_sums[at, :] + gstep * (r.step_pre[at, :] - r.heads[STEP_BIAS : STEP_BIAS + 1, :])
            r.inner_row[:, at] = row_sums(inner)
            return totals

        totals = lax.fori_loop(0, chunks // 2, some, (zero, zero))
        bc_copy(half).start()
        inner_copy(half).start()
        if half == 1:
            load_state().start()
        for j in range(2):
            start_loads(j)
        r.small[13:15, :LANES] += jnp.concatenate([jnp.sum(total, axis=0, keepdims=True) for total in totals], axis=0)

    def meet(half):
        bc_copy(half).wait()
        inner_copy(half).wait()
        padded = r.gs
        if half == 1:
            load_state().wait()
            padded[0:8, :] = jnp.zeros((8, WIDTH), F32)
        edge = pl.ds((half + 1) * (seq // 2), 8)
        r.dz[edge, :] = r.saved[groups]
        top = (lax.broadcasted_iota(jnp.int32, (8, LANES), 0) == 0).astype(BF16)
        zero = jnp.zeros((8, WIDTH), F32)

        def some(i, totals):
            c = (half + 1) * (chunks // 2) - 1 - i
            start = pl.multiple_of(c * CHUNK, CHUNK)
            at = pl.ds(start, CHUNK)
            around = padded.at[pl.ds(start, CHUNK + 8), :]
            shifted = [around[5 + t : 5 + t + CHUNK, :] for t in range(4)]
            summed = r.state_rows[4:5, :] + sum(r.state_rows[t : t + 1, :] * shifted[t] for t in range(4))
            sig = sigmoid(summed)
            gact = r.gbc_low[at, :].astype(F32) + r.gbc_there[at, :].astype(F32)
            gsum = gact * (sig + summed * sig * (1.0 - sig))
            r.dz[at, :] = gsum
            totals = tuple(total + fold(gsum * v) for total, v in zip(totals, shifted)) + (totals[4] + fold(gsum),)
            after = r.dz.at[pl.ds(start, CHUNK + 8), :]
            gstate = sum(r.state_rows[t : t + 1, :] * after[3 - t : 3 - t + CHUNK, :] for t in range(4))
            r.gbc_low[at, :] = gstate.astype(BF16)
            column_of = to_column(r.inner_row[:, at] + r.inner_there[:, at], top)
            column_of = column_of + jnp.sum(gstate * shifted[3], axis=1, keepdims=True)
            rms = r.rms[at, :]
            r.decay_sums[at, :] = rms * rms * column_of * (1.0 / model)
            return totals

        totals = lax.fori_loop(0, chunks // 2, some, (zero,) * 5)
        r.saved[groups] = r.dz[pl.ds(half * (seq // 2), 8), :]
        r.small[8:13, :WIDTH] += jnp.concatenate([jnp.sum(total, axis=0, keepdims=True) for total in totals], axis=0)
        if half == 0:
            r.s_src[0] = nn(r.normed_now[...], r.gbc_low[...]).astype(BF16)
            r.t_src[0] = nn(r.normed_now[...], r.gstep_low[...]).astype(BF16)
            reduction.event(S, 0, 0)

    def grad_normed(j, half):
        load_w(j).wait()
        load_tokens(j).wait()
        load_narrow(j).wait()
        share = pl.ds(pl.multiple_of(near * state, LANES), state)
        at = rows_of(half)
        part = (
            nt(r.gate_low[at, :], r.w_block[j % 2, 0])
            + nt(r.mix_low[at, :], r.w_block[j % 2, 1])
            + nn(r.gstep_low[at, :], r.step_w[:, block(j)])
            + nt(r.gbc_low[at, share], r.state_block[j % 2, :, share])
        )
        r.stage[j % 2] = part.astype(BF16)
        part_store(j, half).start()
        total = fold(part * r.token_block[j % 2, at, :].astype(F32) * twice(r.rms[at, :]))
        r.small[15:16, block(j)] += jnp.sum(total, axis=0, keepdims=True)
        part_store(j, half).wait()
        part_copy(j, half).start()
        if j + 2 < blocks:
            start_loads(j + 2)
        elif half == 0:
            load_tokens(j + 2 - blocks).start()

    def grad_tokens(j):
        for half in (1, 0):
            part_copy(j, half).wait()
        load_there(j).start()
        load_mine(j).start()
        load_tokens(j).wait()
        load_there(j).wait()
        load_mine(j).wait()

        def some(at):
            whole = r.gate_low[at, block(j)].astype(F32) + r.scaled[at, :].astype(F32)
            pulled = twice(r.rms[at, :]) * (whole * r.vectors[NORM_GAIN : NORM_GAIN + 1, block(j)])
            pulled = pulled - r.token_block[j % 2, at, :].astype(F32) * twice(r.decay_sums[at, :])
            r.mix_low[at, block(j)] = (r.cot_now[at, block(j)].astype(F32) + pulled).astype(BF16)

        by_rows(seq, CHUNK, some)
        store_tokens(j).start()
        if j + 2 < blocks:
            load_tokens(j + 2).start()

    def small_event(n):
        if 0 < n < 5:
            small_copy(n - 1).wait()
            r.small[...] += r.small_there[n - 1]
        if n < 4:
            small_copy(n).start()
        elif n == 4:
            small_near().start()
        else:
            small_near().wait()
            row = lax.broadcasted_iota(jnp.int32, r.small_last.shape, 0)
            r.small[8:16, :] = r.small[8:16, :] + jnp.where(row == 7, r.small_last[...], 0.0)

    def block_rows(i):
        rows = pl.ds(i * WIDTH, WIDTH)
        room = [r.w_block.at[0, 0, :, :model], r.w_block.at[0, 1, :, :model], r.w_block.at[1, 0, :, :model]]
        made = r.w_block.at[1, 1, :, :model]
        if i == 0:
            product_copy().wait()
        loads = [
            pltpu.make_async_copy(src.at[rows, :], dst, r.row_sem.at[n])
            for n, (src, dst) in enumerate(zip((r.product, r.product_there, r.tokens), room))
        ]
        for load in loads:
            load.start()
        store = lambda n: pltpu.make_async_copy(made, r.block_out.at[pl.ds(n * WIDTH, WIDTH), :], r.row_sem.at[3])
        if i > 0:
            store(i - 1).wait()
        for load in loads:
            load.wait()

        def some(at):
            whole = room[0][at, :].astype(F32) + room[1][at, :].astype(F32)
            factor = r.factor[0, pl.ds(pl.multiple_of(i * WIDTH + at.start, 32), 32), :]
            scale = jnp.concatenate([factor] * (model // LANES), axis=1)
            made[at, :] = (room[2][at, :].astype(F32) + scale * whole).astype(BF16)

        by_rows(WIDTH, 32, some)
        store(i).start()
        if (i + 1) * WIDTH == seq:
            store(i).wait()

    def end():
        parts = {FINAL: grad_tokens, SMALL: small_event, BLOCK: block_rows}
        for kind, n, g in TAIL:
            if kind == MEET:
                meet(0)
            elif kind == PART:
                grad_normed(n, 0)
            elif kind in parts:
                parts[kind](n)
            else:
                reduction.event(kind, n, g)
        for j in range(blocks):
            store_tokens(j).wait()

    pl.when(k == 0)(first_step)

    @pl.when(k < 2 * groups)
    def _():
        poll(0)
        pl.when(opens)(gate_step)
        poll(2)
        scan_step()
        poll(4)
        pl.when(jnp.logical_not(opens))(mix_step)
        poll(5)

    pl.when(k == LAST_OPENING)(lambda: finish(1))
    pl.when(k == 2 * groups - 1)(lambda: finish(0))
    pl.when(k == 2 * groups)(end)


def backward(fwd, held, given):
    gate, mix, y, entering, sums, product = fwd
    seq, model = given["cot"].shape
    inner = given["ow"].shape[0]
    groups = inner // WIDTH
    chunks = seq // CHUNK
    two = given["state_w"].shape[1]
    state = two // 2
    blocks = model // WIDTH
    at = lambda k: group_at(jnp.minimum(k, 2 * groups - 1))[0]
    half_at = lambda k: jnp.where(group_at(jnp.minimum(k, 2 * groups - 1))[1], 1, 0)
    shape, vmem, dma = jax.ShapeDtypeStruct, pltpu.VMEM, pltpu.SemaphoreType.DMA
    stream = lambda rows: pl.BlockSpec((rows, WIDTH), lambda k: (0, at(k)))
    outside = pl.BlockSpec(memory_space=pl.ANY)
    values = dict(
        given, **held._asdict(), gate=gate, mix=mix, y=y, entering=entering, sums=sums, product=product
    )
    specs = {
        "mix": stream(seq + 8), "y": stream(seq), "cum_t": pl.BlockSpec((8, seq), lambda k: (at(k), 0)),
        "entering": pl.BlockSpec((1, chunks // 2, state, WIDTH), lambda k: (at(k), half_at(k), 0, 0)),
        **{name: outside for name in ("gate", "ow", "w", "tokens", "state_pre", "product", "state_w", "cot", "normed_t")},
    }
    wide = max(inner, model)
    halves = lambda rows: [rows // 2, rows // 4, rows // 8, rows // 16]
    ring = lambda rows, width, count=LANDINGS: [vmem((count, n, width), BF16) for n in halves(rows)]
    scratch = [
        vmem((seq + 8, WIDTH), F32), vmem((seq + 8, WIDTH), F32),
        vmem((2 * CHUNK, GROUP_HEADS * LANES), F32), vmem((2 * CHUNK, WIDTH), F32), vmem((groups + 1, 8, WIDTH), F32),
        vmem((groups, state, WIDTH), F32), vmem((groups, 7, 8, WIDTH), F32), vmem((max(ROOMS) + 2, seq // 2, WIDTH), BF16),
        vmem((2, seq, LANES), F32), vmem((16, seq), F32),
        vmem((chunks, CHUNK, CHUNK), F32), vmem((seq, LANES), F32), vmem((seq, LANES), F32), vmem((seq, two), F32),
        vmem((seq, WIDTH), BF16), vmem((seq, inner), BF16), vmem((seq, inner), BF16), vmem((seq, two), BF16),
        vmem((seq, two), BF16), vmem((8, seq), F32), vmem((8, seq), F32), vmem((seq, LANES), BF16),
        vmem((2, 2, WIDTH, inner), BF16), vmem((2, seq, WIDTH), BF16), vmem((2, seq // 2, WIDTH), BF16),
        vmem((RING, WIDTH, model), BF16), vmem((RING, model, WIDTH), BF16), vmem((RING, model, WIDTH), BF16),
        vmem((1, model, two), BF16), vmem((1, model, LANES), BF16),
        *ring(WIDTH, model), *ring(model, WIDTH), *ring(model, WIDTH), *ring(model, two, 1), *ring(model, LANES, 1),
        vmem((groups, model // 16, WIDTH), BF16), vmem((groups, model // 16, 2, WIDTH), BF16), vmem((groups, WIDTH // 16, model), BF16), vmem((4, 16, wide), F32),
        vmem((8, wide), F32),
        dma((5, 4, LANDINGS)), dma((5, 4, LANDINGS)), dma((4, groups)), dma((4, 4, groups)), dma((4, 4, groups)), dma((2, 2)), dma((2, 2)),
        dma((2, blocks)), dma((2, blocks)), dma((5,)), dma((5,)), dma((3, 2)), dma((blocks,)),
        dma, dma, dma, dma, dma((4,)), dma((2,)), vmem((seq, WIDTH), F32), vmem((WIDTH, model), BF16), dma((4,)),
        vmem((2, WIDTH, two), BF16), vmem((LANES, model), BF16), vmem((8, WIDTH), F32), vmem((model, seq), BF16),
        vmem((seq, model), BF16), dma((2,)),
    ]
    return pl.pallas_call(
        functools.partial(backward_kernel, groups),
        grid=(2 * groups + 1,),
        in_specs=[specs.get(name, whole_spec(values[name].shape)) for name in Inputs._fields],
        out_specs=[outside] * 9 + [pl.BlockSpec((16, wide), lambda k: (0, 0))],
        out_shape=[
            shape((inner, model), BF16), shape((model, 2, inner), BF16), shape((model, two), BF16), shape((model, LANES), BF16),
            shape((seq, model), BF16), shape((blocks, seq, WIDTH), BF16), shape((blocks, seq, WIDTH), BF16),
            shape((seq, model), BF16), shape((seq, model), BF16),
            shape((16, wide), F32),
        ],
        scratch_shapes=scratch,
        compiler_params=pltpu.CompilerParams(collective_id=0, has_side_effects=True, vmem_limit_bytes=60 * MIB),
        name="backward",
    )(*[values[name] for name in Inputs._fields])


def narrow_kernel(
    small, gstep_w, norm, taps, bias, state_taps, state_bias, steps, rates, skips, gains, gstep_t
):
    model, inner, two, heads = norm.shape[0], bias.shape[0], state_bias.shape[0], steps.shape[0]
    norm[...] = small[15, :model].astype(BF16)
    taps[...] = small[3:7, :inner].astype(BF16)
    bias[...] = small[2, :inner].astype(BF16)
    state_taps[...] = small[8:12, :two].astype(BF16)
    state_bias[...] = small[12, :two].astype(BF16)
    steps[...] = small[13, :heads].astype(BF16)
    rates[...] = small[14, :heads].astype(BF16)
    gains[...] = small[0, :inner].astype(BF16)
    channel = lax.broadcasted_iota(jnp.int32, (inner, LANES), 0)
    head = lax.broadcasted_iota(jnp.int32, (inner, LANES), 1)
    chooser = jnp.where(head == channel // HEAD, 1.0, 0.0).astype(BF16)
    high, low = two_parts(small[0:8, :inner])
    skips[...] = (nn(high, chooser) + nn(low, chooser))[1, :heads].astype(BF16)
    gstep_t[...] = gstep_w[...].T[:heads, :]


def narrow_outputs(small, gstep_w, heads, model, inner, two):
    shapes = (model,), (4, inner), (inner,), (4, two), (two,), (heads,), (heads,), (heads,), (inner,), (heads, model)
    return pl.pallas_call(
        narrow_kernel, out_shape=[jax.ShapeDtypeStruct(item, BF16) for item in shapes], name="narrow_outputs"
    )(small, gstep_w)


def on_device(
    tokens, norm_gain, mix_weight, state_weight, step_weight, conv_weight, conv_bias, state_conv_weight, state_conv_bias,
    step_bias, log_rate, skip_gain, gate_gain, out_weight, cotangent,
):
    model = tokens.shape[1]
    inner = out_weight.shape[0]
    heads = step_bias.shape[0]
    two = state_weight.shape[1]
    both = jnp.transpose(mix_weight, (1, 0, 2))
    step_t = step_weight.T
    narrow = (
        conv_weight, conv_bias, gate_gain, norm_gain, state_conv_weight, state_conv_bias, step_bias, log_rate, skip_gain
    )
    fwd, held = forward(tokens, state_weight, step_t, narrow, both, cotangent, out_weight)
    given = {"tokens": tokens, "cot": cotangent, "w": both, "ow": out_weight, "state_w": state_weight, "step_t": step_t}
    gout, gmix, gstate_w, gstep_w, grad_tokens, _, _, block_out, _, small = backward(fwd, held, given)
    size = lax.axis_size("dp")
    if size > 16:
        rows = [[i + 16 * j for j in range(size // 16)] for i in range(16)]
        gout, gmix, gstate_w, gstep_w, small = lax.psum((gout, gmix, gstate_w, gstep_w, small), "dp", axis_index_groups=rows)
    norm, taps, bias, state_taps, state_bias, steps, rates, skips, gains, gstep_t = narrow_outputs(
        small, gstep_w, heads, model, inner, two
    )
    return (
        block_out, grad_tokens, norm, gmix, gstate_w, gstep_t.T, taps, bias, state_taps, state_bias, steps, rates, skips, gains,
        gout,
    )


def solution(mesh):
    rows, halves = P("dp", None), P("tensor")
    return jax.shard_map(
        on_device,
        mesh=mesh,
        in_specs=(
            rows, P(), P(None, None, "tensor"), P(), P(None, "tensor"), P(None, "tensor"), halves, P(), P(), halves, halves,
            halves, halves, P("tensor", None), rows,
        ),
        out_specs=(
            rows, rows, P(), P(None, None, "tensor"), P(), P(None, "tensor"), P(None, "tensor"), halves, P(), P(), halves,
            halves, halves, halves, P("tensor", None),
        ),
        check_vma=False,
    )
```

```python
import functools
import types
import typing

import jax
import jax.numpy as jnp
from jax import lax
from jax.experimental import pallas as pl
from jax.experimental.pallas import tpu as pltpu
from jax.sharding import PartitionSpec as P

EPSILON = 1e-5
CHUNK = 128
HEAD = 64
GROUP_HEADS = 4
WIDTH = HEAD * GROUP_HEADS
LANES = 128
SLOT = 32
F32, BF16 = jnp.float32, jnp.bfloat16
MIB = 1024 * 1024


def nn(left, right):
    return lax.dot_general(left, right, (((1,), (0,)), ((), ())), preferred_element_type=F32)


def nt(left, right):
    return lax.dot_general(left, right, (((1,), (1,)), ((), ())), preferred_element_type=F32)


def tn(left, right):
    return lax.dot_general(left, right, (((0,), (0,)), ((), ())), preferred_element_type=F32)


def sigmoid(v):
    return jax.nn.sigmoid(v)


def softplus(v):
    return jnp.maximum(v, 0.0) + jnp.log1p(jnp.exp(-jnp.abs(v)))


def split3(v):
    high = v.astype(BF16).astype(F32)
    rest = v - high
    mid = rest.astype(BF16).astype(F32)
    low = rest - mid
    return (high + pltpu.roll(mid, SLOT, 1) + pltpu.roll(low, 2 * SLOT, 1)).astype(BF16)


def spread(group, lanes_each):
    shape = (LANES, GROUP_HEADS * lanes_each)
    slot = lax.broadcasted_iota(jnp.int32, shape, 0)
    lane = lax.broadcasted_iota(jnp.int32, shape, 1)
    hit = (slot % SLOT == group * GROUP_HEADS + lane // lanes_each) & (slot < 3 * SLOT)
    return jnp.where(hit, 1.0, 0.0).astype(BF16)


def gather_heads(group):
    shape = (3 * WIDTH, LANES)
    row = lax.broadcasted_iota(jnp.int32, shape, 0)
    lane = lax.broadcasted_iota(jnp.int32, shape, 1)
    head = group * GROUP_HEADS + row % WIDTH // HEAD
    return jnp.where(lane == head + row // (2 * WIDTH) * (LANES // 2), 1.0, 0.0).astype(BF16)


def two_parts(v):
    high = v.astype(BF16)
    return high, (v - high.astype(F32)).astype(BF16)


def row_sums(v):
    ones = jnp.ones((8, LANES), BF16)
    high, low = two_parts(v)
    return nt(ones, high) + nt(ones, low)


def fold(v):
    return jnp.sum(v.reshape(v.shape[0] // 8, 8, v.shape[1]), axis=0)


class Held(typing.NamedTuple):
    normed_t: object
    state_pre: object
    b: object
    c: object
    c_t: object
    scores: object
    step_pre: object
    step3: object
    cum3: object
    cum_t: object
    rms: object
    vectors: object
    state_rows: object
    heads: object


TAPS, BIAS, GATE_GAIN, NORM_GAIN = 0, 4, 5, 6
RATE, STEP_BIAS, SKIP = 0, 1, 2


def masks():
    row = lax.broadcasted_iota(jnp.int32, (CHUNK, CHUNK), 0)
    col = lax.broadcasted_iota(jnp.int32, (CHUNK, CHUNK), 1)
    return row >= col, col < HEAD


def both_halves(v, first):
    zero = jnp.zeros_like(v)
    return jnp.concatenate([jnp.where(first, v, zero), jnp.where(first, zero, v)], axis=0)


def decay_of(cum_b, cum_t_ref, head, at, lower):
    across = cum_t_ref[head : head + 1, at]
    return jnp.exp(jnp.where(lower, cum_b - across, -1e30))


def pairwise(cum_b, at, first):
    heads = [cum_b[at, h * LANES : (h + 1) * LANES] for h in range(GROUP_HEADS)]
    return jnp.concatenate([jnp.where(first, heads[h], heads[h + 1]) for h in range(0, GROUP_HEADS, 2)], axis=1)


def skip_row(heads_ref, each):
    return nn(split3(heads_ref[...]), each)[SKIP : SKIP + 1, :]


def pack(vectors, state_rows, heads, conv_w, conv_b, gate_gain, norm_gain, state_conv_w, state_conv_b, step_bias, log_rate, skip):
    for ref in (vectors, state_rows, heads):
        ref[...] = jnp.zeros_like(ref)
    count = step_bias.shape[0]
    vectors[TAPS : TAPS + 4, : conv_w.shape[1]] = conv_w[...]
    vectors[BIAS, : conv_b.shape[0]] = conv_b[...]
    vectors[GATE_GAIN, : gate_gain.shape[0]] = gate_gain[...]
    vectors[NORM_GAIN, : norm_gain.shape[0]] = norm_gain[...]
    state_rows[0:4, :] = state_conv_w[...]
    state_rows[4, :] = state_conv_b[...]
    heads[RATE, :count] = -jnp.exp(log_rate[...])
    heads[STEP_BIAS, :count] = step_bias[...]
    heads[SKIP, :count] = skip[...]


def prepare(heads, tokens_ref, state_w_ref, step_t_ref, normed, b_t, halo, step_w, held):
    seq, model = tokens_ref.shape
    vectors_ref, state_rows_ref, heads_ref = held.vectors, held.state_rows, held.heads
    rows = 2 * CHUNK
    step_w[...] = jnp.zeros_like(step_w)
    step_w[0:heads, :] = step_t_ref[...]
    row = lax.broadcasted_iota(jnp.int32, (CHUNK, CHUNK), 0)
    col = lax.broadcasted_iota(jnp.int32, (CHUNK, CHUNK), 1)
    low_tri = jnp.where(row >= col, 1.0, 0.0).astype(BF16)
    hit = (row % 8 < GROUP_HEADS) & (col % SLOT == row // 8 * GROUP_HEADS + row % 8) & (col < 3 * SLOT)
    places = jnp.where(hit, 1.0, 0.0).astype(BF16)

    def norm(i, _):
        here = pl.ds(pl.multiple_of(i * rows, rows), rows)
        values = tokens_ref[here, :].astype(F32)
        inverse = lax.rsqrt(jnp.mean(values * values, axis=1, keepdims=True) + EPSILON)
        held.rms[here, :] = jnp.broadcast_to(inverse, (rows, LANES))
        low = (values * inverse * vectors_ref[NORM_GAIN : NORM_GAIN + 1, :model]).astype(BF16)
        normed[here, :] = low
        held.normed_t[:, here] = low.T
        return 0

    lax.fori_loop(0, seq // rows, norm, 0)
    held.state_pre[...] = nn(normed[...], state_w_ref[...])
    held.step_pre[...] = nt(normed[...], step_w[...]) + heads_ref[STEP_BIAS : STEP_BIAS + 1, :]
    halo[0:8, :] = jnp.zeros((8, halo.shape[1]), F32)
    halo[8:, :] = held.state_pre[...]
    lane = lax.broadcasted_iota(jnp.int32, (CHUNK, LANES), 1)

    def some(c, _):
        start = pl.multiple_of(c * CHUNK, CHUNK)
        at = pl.ds(start, CHUNK)
        around = halo.at[pl.ds(start, CHUNK + 8), :]
        summed = state_rows_ref[4:5, :] + sum(state_rows_ref[t : t + 1, :] * around[5 + t : 5 + t + CHUNK, :] for t in range(4))
        act = summed * sigmoid(summed)
        state = act.shape[1] // 2
        b_wide, c_wide = act[:, :state], act[:, state:]
        (b_high, b_low), (c_high, c_low) = two_parts(b_wide), two_parts(c_wide)
        held.b[at, :] = b_high
        held.c[at, :] = c_high
        b_t[c] = b_wide.T.astype(BF16)
        held.c_t[c] = c_wide.T.astype(BF16)
        held.scores[c] = nt(
            jnp.concatenate([c_high, c_high, c_low], axis=1), jnp.concatenate([b_high, b_low, b_high], axis=1)
        )
        step = jnp.where(lane < heads, softplus(held.step_pre[at, :]), 0.0)
        held.step3[at, :] = split3(step)
        sums = nn(low_tri, split3(step * heads_ref[RATE : RATE + 1, :]))
        sums = sums + pltpu.roll(sums, LANES - SLOT, 1) + pltpu.roll(sums, LANES - 2 * SLOT, 1)
        cum3 = split3(jnp.where(lane < heads, sums, 0.0))
        held.cum3[at, :] = cum3
        held.cum_t[:, at] = nt(places, cum3)
        return 0

    lax.fori_loop(0, seq // CHUNK, some, 0, unroll=4)


def forward_kernel(
    heads,
    tokens_ref, state_w_ref, step_t_ref, *rest,
):
    narrow, (w_ref, cot_ref, ow_ref), rest = rest[:9], rest[9:12], rest[12:]
    (
    gate_ref, mix_ref, y_ref, entering_ref, sums_ref, product_ref, *rest
    ) = rest
    n = len(Held._fields)
    outs, held = Held(*rest[:n]), Held(*rest[n : 2 * n])
    normed, b_t, halo, step_w, carry, square, gained, cum_b, step_e, cot, ow, product, sem, held_sem, product_sem = rest[2 * n :]
    group = pl.program_id(0)
    seq = normed.shape[0]
    chunks = seq // CHUNK
    late = [pltpu.make_async_copy(src, dst, sem.at[i]) for i, (src, dst) in enumerate(((cot_ref, cot), (ow_ref, ow)))]
    keeps = [pltpu.make_async_copy(src, dst, held_sem.at[i]) for i, (src, dst) in enumerate(zip(held, outs))]

    @pl.when(group == 0)
    def _():
        for copy in late:
            copy.start()
        square[...] = jnp.zeros_like(square)
        pack(held.vectors, held.state_rows, held.heads, *narrow)
        prepare(heads, tokens_ref, state_w_ref, step_t_ref, normed, b_t, halo, step_w, held)
        for copy in keeps:
            copy.start()

    mix_ref[0:8, :] = jnp.zeros((8, WIDTH), F32)
    mix_ref[8:, :] = nn(normed[...], w_ref[1])
    gate_ref[...] = nn(normed[...], w_ref[0])
    carry[...] = jnp.zeros_like(carry)
    lanes = pl.ds(pl.multiple_of(group * WIDTH, WIDTH), WIDTH)
    vector = lambda row: held.vectors[row : row + 1, lanes]
    each, wide = spread(group, HEAD), spread(group, LANES)
    lower, first = masks()
    cum_b[...] = nn(held.cum3[...], wide)
    step_e[...] = nn(held.step3[...], each)
    skip = skip_row(held.heads, each)
    cum_t = held.cum_t.at[pl.ds(pl.multiple_of(group * 8, 8), 8), :]

    def chunk(c, _):
        start = pl.multiple_of(c * CHUNK, CHUNK)
        at = pl.ds(start, CHUNK)
        around = mix_ref.at[pl.ds(start, CHUNK + 8), :]
        summed = vector(BIAS) + sum(vector(TAPS + t) * around[5 + t : 5 + t + CHUNK, :] for t in range(4))
        x = summed * sigmoid(summed)
        xs = x * step_e[at, :]
        cum = pairwise(cum_b, at, first)
        ecum = jnp.exp(cum)
        weighted = (xs * jnp.exp(cum[CHUNK - 1 :, :] - cum)).astype(BF16)
        u = xs.astype(BF16)
        scores = held.scores[c]
        state = carry[...]
        state_low = state.astype(BF16)
        entering_ref[0, c] = state_low
        y = nn(held.c[at, :], state_low) * ecum + skip * x
        carry[...] = state * ecum[CHUNK - 1 :, :] + nn(b_t[c], weighted)
        parts = []
        for pair in range(GROUP_HEADS // 2):
            mixing = [
                (scores * decay_of(cum_b[at, h * LANES : (h + 1) * LANES], cum_t, h, at, lower)).astype(BF16)
                for h in (2 * pair, 2 * pair + 1)
            ]
            parts.append(nn(jnp.concatenate(mixing, axis=1), both_halves(u[:, pair * LANES : (pair + 1) * LANES], first)))
        y = y + jnp.concatenate(parts, axis=1)
        y_ref[at, :] = y
        gate = gate_ref[at, :]
        gated = y * gate * sigmoid(gate)
        squares = gated * gated
        square[at, :] += squares[:, :LANES] + squares[:, LANES:]
        gained[at, lanes] = (gated * vector(GATE_GAIN)).astype(BF16)
        return 0

    lax.fori_loop(0, chunks, chunk, 0, unroll=chunks)

    @pl.when(group == pl.num_programs(0) - 1)
    def _():
        for copy in late:
            copy.wait()

        def project(i, _):
            at = pl.ds(pl.multiple_of(i * 4 * CHUNK, CHUNK), 4 * CHUNK)
            wide = nn(gained[at, :], ow[...])
            product[at, :] = wide.astype(BF16)
            pltpu.make_async_copy(product.at[at, :], product_ref.at[at, :], product_sem.at[i]).start()
            dots = wide * cot[at, :].astype(F32)
            dots = sum(dots[:, m * LANES : (m + 1) * LANES] for m in range(dots.shape[1] // LANES))
            sums_ref[0:8, at] = row_sums(square[at, :])
            sums_ref[8:16, at] = row_sums(dots)
            return 0

        lax.fori_loop(0, seq // (4 * CHUNK), project, 0)
        for i in range(seq // (4 * CHUNK)):
            at = pl.ds(i * 4 * CHUNK, 4 * CHUNK)
            pltpu.make_async_copy(product.at[at, :], product_ref.at[at, :], product_sem.at[i]).wait()
        for copy in keeps:
            copy.wait()


def whole_spec(shape):
    return pl.BlockSpec(shape, lambda g: (0,) * len(shape), pipeline_mode=pl.Buffered(1))


def column(rows):
    return pl.BlockSpec((rows, WIDTH), lambda g: (0, g))


def forward(tokens, state_weight, step_t, narrow, both, cotangent, out_weight):
    seq, model = cotangent.shape
    inner = out_weight.shape[0]
    groups = inner // WIDTH
    chunks = seq // CHUNK
    two = state_weight.shape[1]
    state = two // 2
    shape, vmem, dma = jax.ShapeDtypeStruct, pltpu.VMEM, pltpu.SemaphoreType.DMA
    held = Held(
        normed_t=((model, seq), BF16), state_pre=((seq, two), F32), b=((seq, state), BF16), c=((seq, state), BF16),
        c_t=((chunks, state, CHUNK), BF16), scores=((chunks, CHUNK, CHUNK), F32), step_pre=((seq, LANES), F32),
        step3=((seq, LANES), BF16), cum3=((seq, LANES), BF16), cum_t=((LANES, seq), F32), rms=((seq, LANES), F32), vectors=((8, max(inner, model)), F32),
        state_rows=((8, two), F32), heads=((8, LANES), F32),
    )
    whole = [tokens, state_weight, step_t, *narrow]
    outside = pl.BlockSpec(memory_space=pl.ANY)
    outs = pl.pallas_call(
        functools.partial(forward_kernel, step_t.shape[0]),
        grid=(groups,),
        in_specs=[whole_spec(item.shape) for item in whole]
        + [pl.BlockSpec((2, model, WIDTH), lambda g: (0, 0, g)), outside, outside],
        out_specs=[
            column(seq), column(seq + 8), column(seq),
            pl.BlockSpec((1, chunks, state, WIDTH), lambda g: (g, 0, 0, 0)), pl.BlockSpec((16, seq), lambda g: (0, 0)),
            outside, *[outside] * len(held),
        ],
        out_shape=[
            shape((seq, inner), F32), shape((seq + 8, inner), F32), shape((seq, inner), F32),
            shape((groups, chunks, state, WIDTH), BF16), shape((16, seq), F32), shape((seq, model), BF16),
            *[shape(*item) for item in held],
        ],
        scratch_shapes=[
            *[vmem(*item) for item in held],
            vmem((seq, model), BF16), vmem((chunks, state, CHUNK), BF16), vmem((8 + seq, two), F32), vmem((LANES, model), BF16),
            vmem((state, WIDTH), F32), vmem((seq, LANES), F32), vmem((seq, inner), BF16),
            vmem((seq, GROUP_HEADS * LANES), F32), vmem((seq, WIDTH), F32),
            vmem((seq, model), BF16), vmem((inner, model), BF16), vmem((seq, model), BF16),
            dma((2,)), dma((len(held),)), dma((seq // (4 * CHUNK),)),
        ],
        compiler_params=pltpu.CompilerParams(vmem_limit_bytes=56 * MIB),
        name="forward",
    )(*whole, both, cotangent, out_weight)
    return outs[:6], Held(*outs[6:])


class Inputs(typing.NamedTuple):
    normed_t: object
    cot: object
    gate: object
    mix: object
    y: object
    entering: object
    ow: object
    b: object
    c: object
    c_t: object
    scores: object
    step3: object
    cum3: object
    step_pre: object
    rms: object
    state_pre: object
    state_w: object
    step_t: object
    vectors: object
    state_rows: object
    heads: object
    cum_t: object
    w: object
    tokens: object
    sums: object
    product: object


class Outputs(typing.NamedTuple):
    gout: object
    gmix: object
    gstate_w: object
    gstep_w: object
    gtokens: object
    there: object
    mine: object
    block_out: object
    product_there: object
    small: object


class Scratch(typing.NamedTuple):
    gs: object
    dz: object
    cum_b: object
    step_e: object
    saved: object
    kept_carry: object
    kept_partial: object
    dy: object
    factor: object
    sums_there: object
    gscores: object
    decay_sums: object
    inner_sums: object
    gbc: object
    scaled: object
    gate_low: object
    mix_low: object
    gbc_low: object
    gbc_there: object
    inner_row: object
    inner_there: object
    gstep_low: object
    w_block: object
    token_block: object
    stage: object
    o_src: object
    g_src: object
    m_src: object
    s_src: object
    t_src: object
    o_r0: object
    o_r1: object
    o_r2: object
    o_r3: object
    g_r0: object
    g_r1: object
    g_r2: object
    g_r3: object
    m_r0: object
    m_r1: object
    m_r2: object
    m_r3: object
    s_r0: object
    s_r1: object
    s_r2: object
    s_r3: object
    t_r0: object
    t_r1: object
    t_r2: object
    t_r3: object
    g_own: object
    x_own: object
    o_own: object
    small_there: object
    small_last: object
    send_sem: object
    recv_sem: object
    copy_sem: object
    ag_send: object
    ag_recv: object
    near_send: object
    near_recv: object
    part_send: object
    part_recv: object
    small_send: object
    small_recv: object
    load_sem: object
    store_sem: object
    sums_send: object
    sums_recv: object
    product_send: object
    product_recv: object
    row_sem: object
    stage_sem: object
    gate_now: object
    ow_now: object
    now_sem: object
    state_block: object
    step_w: object
    skip: object
    normed_now: object
    cot_now: object
    narrow_sem: object


RING = 3
LANDINGS = 2
BITS = (1, 2, 4, 8)
O, G, M, S, T, X, MEET, PART, FINAL, SMALL, BLOCK = range(11)
MESH = pl.DeviceIdType.MESH


STEPS = ((0, 0), (1, 0), (2, 0), (0, 1), (3, 0), (1, 1), (4, 0), (5, 0), (2, 1), (3, 1), (4, 1), (5, 1))
LAST_OPENING = 7
ROOMS = (0, 1, 2, 0, 1, 3,)
X_FIRST, Z_FIRST = (1, 2, 4, 8), (1, 4, 2, 8)
O_TURNS, X_TURNS, S_TURNS = (1, 0, 0, 1, 1, 1,), (0, 0, 0, 0, 0, 0,), (0,)
MAIN = (
    (0, 3, ((O, 1, 0), (G, 1, 0),)),
    (1, 1, ((G, 2, 0), (O, 2, 0),)),
    (1, 3, ((O, 3, 0), (O, 1, 1), (G, 1, 1), (G, 3, 0),)),
    (2, 6, ((O, 4, 0),)),
    (2, 1, ((G, 4, 0),)),
    (2, 3, ((O, 5, 0), (G, 2, 1), (G, 1, 2), (O, 2, 1), (O, 1, 2),)),
    (3, 3, ((O, 3, 1), (G, 3, 1),)),
    (3, 4, ((O, 6, 0),)),
    (4, 6, ((G, 4, 1), (M, 1, 0), (O, 4, 1), (G, 2, 2), (O, 2, 2),)),
    (4, 3, ((O, 1, 3), (M, 2, 0), (G, 1, 3), (O, 5, 1), (O, 7, 0),)),
    (4, 4, ((O, 8, 0),)),
    (5, 3, ((O, 3, 2), (G, 3, 2), (G, 2, 3),)),
    (6, 6, ((O, 6, 1), (M, 1, 1), (M, 3, 0),)),
    (6, 1, ((G, 4, 2), (O, 4, 2),)),
    (6, 3, ((G, 1, 4), (M, 4, 0), (G, 3, 3), (O, 2, 3), (O, 1, 4), (O, 5, 2),)),
    (7, 1, ((G, 4, 3), (M, 2, 1), (O, 7, 1),)),
    (7, 2, ((O, 3, 3),)),
    (7, 3, ((O, 6, 2), (X, 5, 0), (G, 2, 4), (G, 1, 5), (O, 8, 1),)),
    (7, 4, ((O, 4, 3),)),
    (8, 3, ((M, 3, 1), (O, 2, 4), (O, 1, 5),)),
    (8, 4, ((O, 7, 2), (G, 3, 4), (G, 2, 5), (O, 5, 3),)),
    (8, 5, ((O, 3, 4), (M, 4, 1), (O, 8, 2),)),
    (9, 0, ((MEET, 0, 1), (O, 6, 3), (M, 1, 2),)),
    (9, 3, ((G, 4, 4), (PART, 0, 1), (O, 4, 4), (X, 6, 0),)),
    (9, 4, ((M, 2, 2),)),
    (9, 5, ((G, 3, 5), (PART, 1, 1), (X, 5, 1), (M, 1, 3), (O, 5, 4),)),
    (10, 2, ((PART, 2, 1), (O, 2, 5),)),
    (10, 3, ((G, 4, 5),)),
    (10, 4, ((O, 7, 3), (M, 3, 2), (PART, 3, 1), (O, 6, 4), (O, 8, 3), (X, 7, 0),)),
    (10, 5, ((O, 3, 5), (M, 4, 2), (X, 6, 1),)),
    (11, 0, ((M, 2, 3), (X, 8, 0), (PART, 4, 1), (M, 1, 4),)),
    (11, 3, ((O, 4, 5), (PART, 5, 1),)),
    (11, 4, ((X, 5, 2), (O, 7, 4), (M, 3, 3), (O, 5, 5),)),
    (11, 5, ((O, 8, 4),)),
)
TAIL = (
    (M, 4, 3), (M, 2, 4), (M, 1, 5), (X, 7, 1), (O, 6, 5), (X, 6, 2), (X, 8, 1), (X, 5, 3), (M, 3, 4), (M, 2, 5),
    (MEET, 0, 0), (M, 4, 4), (PART, 0, 0), (S, 1, 0), (O, 7, 5), (X, 7, 2), (PART, 1, 0), (M, 3, 5), (O, 8, 5),
    (PART, 2, 0), (X, 5, 4), (X, 8, 2), (X, 6, 3), (PART, 3, 0), (M, 4, 5), (PART, 4, 0), (S, 2, 0), (PART, 5, 0),
    (SMALL, 0, 0), (BLOCK, 0, 0), (SMALL, 1, 0), (X, 5, 5), (X, 6, 4), (FINAL, 0, 0), (S, 3, 0), (BLOCK, 1, 0),
    (X, 7, 3), (BLOCK, 2, 0), (SMALL, 2, 0), (S, 4, 0), (BLOCK, 3, 0), (X, 8, 3), (X, 6, 5), (S, 5, 0), (SMALL, 3, 0),
    (FINAL, 1, 0), (X, 7, 4), (SMALL, 4, 0), (FINAL, 2, 0), (S, 6, 0), (X, 8, 4), (FINAL, 3, 0), (FINAL, 4, 0),
    (SMALL, 5, 0), (X, 7, 5), (FINAL, 5, 0), (X, 8, 5), (S, 7, 0), (S, 8, 0),
)


class Route:
    def __init__(self, bits, rows):
        me = lax.axis_index("dp")
        mine = [lax.rem(lax.div(me, bit), 2) for bit in bits]
        self.partner = [me + bit - 2 * bit * v for bit, v in zip(bits, mine)]
        self.size = [rows // 2 ** (stage + 1) for stage in range(len(bits))]
        self.base = [0]
        for n, v in zip(self.size, mine):
            self.base.append(self.base[-1] + v * n)
        self.away = [self.base[s] + (1 - mine[s]) * self.size[s] for s in range(len(bits))]


def even(v):
    return v if isinstance(v, int) else pl.multiple_of(v, 16)


def block(index):
    return pl.ds(index * WIDTH if isinstance(index, int) else pl.multiple_of(index * WIDTH, WIDTH), WIDTH)


class Reduction:
    def __init__(self, r):
        self.r = r
        self.src = (r.o_src, r.g_src, r.m_src, r.s_src, r.t_src)
        self.came = (
            (r.o_r0, r.o_r1, r.o_r2, r.o_r3), (r.g_r0, r.g_r1, r.g_r2, r.g_r3), (r.m_r0, r.m_r1, r.m_r2, r.m_r3),
            (r.s_r0, r.s_r1, r.s_r2, r.s_r3), (r.t_r0, r.t_r1, r.t_r2, r.t_r3),
        )
        model = r.g_src.shape[1]
        lengths = (r.o_src.shape[1], model, r.t_src.shape[1])
        self.routes = {order: [Route(order, rows) for rows in lengths] for order in (X_FIRST, Z_FIRST)}

    def route(self, kind, g):
        turns = {O: O_TURNS, S: S_TURNS, T: S_TURNS}.get(kind, X_TURNS)
        order = Z_FIRST if isinstance(g, int) and turns[g] else X_FIRST
        return self.routes[order][{O: 0, T: 2}.get(kind, 1)]

    def slot(self, kind, g):
        return 0 if kind in (S, T) else (g % RING if isinstance(g, int) else lax.rem(g, RING))

    def landing(self, kind, g):
        return 0 if kind in (S, T) else (g % LANDINGS if isinstance(g, int) else lax.rem(g, LANDINGS))

    def place(self, kind, g):
        return g if kind in (O, X) else 0

    def halve(self, kind, s, g):
        r, route, slot, landing = self.r, self.route(kind, g), self.slot(kind, g), self.landing(kind, g)
        return pltpu.make_async_remote_copy(
            src_ref=self.src[kind].at[slot, pl.ds(even(route.away[s]), route.size[s]), :],
            dst_ref=self.came[kind][s].at[landing],
            send_sem=r.send_sem.at[kind, s, landing], recv_sem=r.recv_sem.at[kind, s, landing],
            device_id={"dp": route.partner[s]}, device_id_type=MESH,
        )

    def add(self, kind, s, g):
        route, slot, landing = self.route(kind, g), self.slot(kind, g), self.landing(kind, g)
        src, came = self.src[kind], self.came[kind][s]
        n = route.size[s]
        step = min(n, 64 if kind == O else 384)

        def some(j, _):
            here = pl.ds(pl.multiple_of(route.base[s + 1] + j * step, 16), step)
            there = pl.ds(pl.multiple_of(j * step, 16), step)
            src[slot, here, :] += came[landing, there, :]
            return 0

        lax.fori_loop(0, n // step, some, 0)

    def target(self, kind, s, g):
        r, route = self.r, self.route(kind, g)
        if kind == O:
            return r.gout.at[pl.ds(even(g * WIDTH + route.base[s + 1]), route.size[s]), :]
        if kind == X:
            return r.gmix.at[pl.ds(route.base[s + 1], route.size[s]), :, block(g)]
        return (r.gstate_w if kind == S else r.gstep_w).at[pl.ds(even(route.base[s + 1]), route.size[s]), :]

    def reduced(self, kind, g):
        if kind in (O, X):
            return (self.r.o_own if kind == O else self.r.x_own).at[g]
        route = self.route(kind, g)
        return self.src[kind].at[0, pl.ds(even(route.base[4]), route.size[3]), :]

    def gather(self, kind, s, g):
        i, place = (O, X, S, T).index(kind), self.place(kind, g)
        return pltpu.make_async_remote_copy(
            src_ref=self.reduced(kind, g) if s == 3 else self.target(kind, s, g), dst_ref=self.target(kind, s, g),
            send_sem=self.r.ag_send.at[i, s, place], recv_sem=self.r.ag_recv.at[i, s, place],
            device_id={"dp": self.route(kind, g).partner[s]}, device_id_type=MESH,
        )

    def keep(self, kind, g):
        sem = self.r.copy_sem.at[(O, X, S, T).index(kind), self.place(kind, g)]
        return pltpu.make_async_copy(self.reduced(kind, g), self.target(kind, 3, g), sem)

    def event(self, kind, n, g):
        for each in (S, T) if kind == S else (kind,):
            self.piece(each, n, g)

    def piece(self, kind, n, g):
        r = self.r
        if n == 0:
            self.halve(kind, 0, g).start()
        elif n < 4:
            self.halve(kind, n - 1, g).wait()
            self.add(kind, n - 1, g)
            self.halve(kind, n, g).start()
        elif n == 4:
            self.halve(kind, 3, g).wait()
            self.add(kind, 3, g)
            slot = self.slot(kind, g)
            route = self.route(kind, g)
            at = pl.ds(even(route.base[4]), route.size[3])
            if kind == G:
                r.g_own[g] = r.g_src[slot, at, :]
            else:
                if kind == M:
                    r.x_own[g, :, 0, :] = r.g_own[g]
                    r.x_own[g, :, 1, :] = r.m_src[slot, at, :]
                    kind = X
                if kind == O:
                    r.o_own[g] = r.o_src[slot, at, :]
                self.keep(kind, g).start()
                self.gather(kind, 3, g).start()
        else:
            s = 8 - n
            self.gather(kind, s, g).wait()
            if s == 3:
                self.keep(kind, g).wait()
            if s > 0:
                self.gather(kind, s - 1, g).start()


def by_rows(rows, step, body):
    def some(i, _):
        body(pl.ds(pl.multiple_of(i * step, step), step))
        return 0

    lax.fori_loop(0, rows // step, some, 0)


def twice(v):
    return jnp.concatenate([v, v], axis=1)


def to_column(v, chooser):
    high, low = two_parts(v)
    return tn(high, chooser) + tn(low, chooser)


def group_at(k):
    g, opens = 0, 0
    for step, (group, second) in enumerate(STEPS):
        g = jnp.where(k == step, group, g)
        opens = jnp.where(k == step, 1 - second, opens)
    return g, opens == 1


def backward_kernel(groups, *refs):
    a, b = len(Inputs._fields), len(Inputs._fields) + len(Outputs._fields)
    parts = Inputs(*refs[:a]), Outputs(*refs[a:b]), Scratch(*refs[b:])
    r = types.SimpleNamespace(**{name: ref for part in parts for name, ref in part._asdict().items()})
    k = pl.program_id(0)
    group, opens = group_at(k)
    seq = r.normed_t.shape[1]
    model = r.cot.shape[1]
    chunks = seq // CHUNK
    state = r.b.shape[1]
    blocks = model // WIDTH
    wide = r.small_last.shape[1]
    me = lax.axis_index("dp")
    near = lax.axis_index("tensor")
    reduction = Reduction(r)

    def vector(row):
        return r.vectors[row : row + 1, block(group)]

    def beside(src, dst, send, recv):
        return pltpu.make_async_remote_copy(
            src_ref=src, dst_ref=dst, send_sem=send, recv_sem=recv, device_id={"tensor": 1 - near}, device_id_type=MESH
        )

    def rows_of(half):
        return pl.ds(half * (seq // 2), seq // 2)

    def bc_copy(half):
        at = rows_of(half)
        return beside(r.gbc_low.at[at, :], r.gbc_there.at[at, :], r.near_send.at[0, half], r.near_recv.at[0, half])

    def inner_copy(half):
        at = rows_of(half)
        return beside(r.inner_row.at[:, at], r.inner_there.at[:, at], r.near_send.at[1, half], r.near_recv.at[1, half])

    def sums_copy():
        return beside(r.sums, r.sums_there, r.sums_send, r.sums_recv)

    def product_copy():
        return beside(r.product, r.product_there, r.product_send, r.product_recv)

    def part_copy(j, half):
        at = rows_of(half)
        return beside(r.mine.at[j, at, :], r.there.at[j, at, :], r.part_send.at[half, j], r.part_recv.at[half, j])

    def part_store(j, half):
        return pltpu.make_async_copy(r.stage.at[j % 2], r.mine.at[j, rows_of(half), :], r.stage_sem.at[j % 2])

    def load_w(j):
        return pltpu.make_async_copy(r.w.at[:, block(j), :], r.w_block.at[j % 2], r.load_sem.at[0, j % 2])

    def load_narrow(j):
        return pltpu.make_async_copy(r.state_w.at[block(j), :], r.state_block.at[j % 2], r.narrow_sem.at[j % 2])

    def load_tokens(j):
        return pltpu.make_async_copy(r.tokens.at[:, block(j)], r.token_block.at[j % 2], r.load_sem.at[1, j % 2])

    def start_loads(j):
        load_w(j).start()
        load_tokens(j).start()
        load_narrow(j).start()

    def load_there(j):
        return pltpu.make_async_copy(r.there.at[j], r.scaled, r.load_sem.at[2, 0])

    def load_gate(g):
        return pltpu.make_async_copy(r.gate.at[:, block(g)], r.gate_now, r.now_sem.at[0])

    def load_ow(g):
        return pltpu.make_async_copy(r.ow.at[block(g), :], r.ow_now, r.now_sem.at[1])

    def load_cot():
        return pltpu.make_async_copy(r.cot, r.cot_now, r.now_sem.at[2])

    def load_normed():
        return pltpu.make_async_copy(r.normed_t, r.normed_now, r.now_sem.at[3])

    def load_mine(j):
        return pltpu.make_async_copy(r.mine.at[j], r.gate_low.at[:, block(j)], r.load_sem.at[2, 1])

    def load_state():
        return pltpu.make_async_copy(r.state_pre, r.gs.at[8:, :], r.load_sem.at[2, 1])

    def store_tokens(j):
        return pltpu.make_async_copy(r.mix_low.at[:, block(j)], r.gtokens.at[:, block(j)], r.store_sem.at[j])

    def small_copy(i):
        bit = BITS[i]
        return pltpu.make_async_remote_copy(
            src_ref=r.small, dst_ref=r.small_there.at[i], send_sem=r.small_send.at[i], recv_sem=r.small_recv.at[i],
            device_id={"dp": me + bit - 2 * bit * (lax.rem(lax.div(me, bit), 2))}, device_id_type=MESH,
        )

    def small_near():
        return beside(r.small.at[:, :wide], r.small_last, r.small_send.at[4], r.small_recv.at[4])

    def poll(place):
        here = [(step, events) for step, where, events in MAIN if where == place]

        def one(step, events):
            @pl.when(k == step)
            def _():
                for kind, n, g in events:
                    if kind == MEET:
                        meet(1)
                    elif kind == PART:
                        grad_normed(n, 1)
                    else:
                        reduction.event(kind, n, g)

        def some(entries):
            if len(entries) == 1:
                one(*entries[0])
            elif entries:
                middle = entries[len(entries) // 2][0]
                pl.when(k < middle)(lambda: some(entries[: len(entries) // 2]))
                pl.when(k >= middle)(lambda: some(entries[len(entries) // 2 :]))

        some(here)

    def first_step():
        load_ow(0).start()
        load_cot().start()
        load_gate(0).start()
        load_normed().start()
        r.step_w[...] = jnp.zeros_like(r.step_w)
        r.step_w[0 : r.step_t.shape[0], :] = r.step_t[...]
        barrier = pltpu.get_barrier_semaphore()
        for bit in BITS:
            partner = me + bit - 2 * bit * (lax.rem(lax.div(me, bit), 2))
            pl.semaphore_signal(barrier, inc=1, device_id={"dp": partner}, device_id_type=MESH)
        pl.semaphore_signal(barrier, inc=1, device_id={"tensor": 1 - near}, device_id_type=MESH)
        for ref in (r.gscores, r.decay_sums, r.inner_sums, r.gbc, r.small, r.saved, r.kept_carry, r.kept_partial):
            ref[...] = jnp.zeros_like(ref)
        pl.semaphore_wait(barrier, 5)
        sums_copy().start()
        product_copy().start()
        load_ow(0).wait()
        load_cot().wait()
        grad_scaled()
        sums_copy().wait()
        row = lax.broadcasted_iota(jnp.int32, (16, 2 * LANES), 0)
        lane = lax.broadcasted_iota(jnp.int32, (16, 2 * LANES), 1)
        chooser = (row == lane // LANES * 8).astype(BF16)
        full = 2 * groups * WIDTH

        def factors(at):
            both = to_column(r.sums[:, at] + r.sums_there[:, at], chooser) * (1.0 / full)
            inverse = lax.rsqrt(both[:, :LANES] + EPSILON)
            r.factor[0, at, :] = inverse
            r.factor[1, at, :] = inverse * inverse * inverse * both[:, LANES:]

        by_rows(seq, CHUNK, factors)

    def gating(at, dy):
        lanes = block(group)
        inverse, coefficient = twice(r.factor[0, at, :]), twice(r.factor[1, at, :])
        gate, y, gs, gain = r.gate_now[at, :], r.y[at, :], r.gs[at, :], vector(GATE_GAIN)
        sig = sigmoid(gate)
        silu = gate * sig
        gated = y * silu
        hat = gated * inverse
        r.scaled[at, :] = (hat * gain).astype(BF16)
        r.kept_partial[group, 0] += fold(gs * hat)
        ggated = inverse * (gs * gain) - gated * coefficient
        dy[...] = (ggated * silu).astype(BF16)
        ggate = ggated * y * (sig + silu * (1.0 - sig))
        r.gate_low[at, lanes] = ggate.astype(BF16)
        inner = ggate * gate
        r.inner_sums[at, :] += inner[:, :LANES] + inner[:, LANES:]

    def scan_chunk(c, here, dy, g, chooser, lower, first):
        start = pl.multiple_of(c * CHUNK, CHUNK)
        at = pl.ds(start, CHUNK)
        around = r.mix.at[pl.ds(start, CHUNK + 8), :]
        shifted = [around[5 + t : 5 + t + CHUNK, :] for t in range(4)]
        summed = vector(BIAS) + sum(vector(TAPS + t) * shifted[t] for t in range(4))
        sig = sigmoid(summed)
        x = summed * sig
        step_e = r.step_e[here, :]
        cum = pairwise(r.cum_b, here, first)
        ecum = jnp.exp(cum)
        toend = jnp.exp(cum[CHUNK - 1 :, :] - cum)
        xs = x * step_e
        u = xs.astype(BF16)
        weighted = (xs * toend).astype(BF16)
        gy_low = dy[...]
        gy = gy_low.astype(F32)
        gy_across = (gy * ecum).astype(BF16)
        gstate = r.kept_carry[g]
        gstate_low = gstate.astype(BF16)
        entering = r.entering[0, lax.rem(c, chunks // 2)]
        last = ecum[CHUNK - 1 :, :]
        r.gbc[at, state:] += nt(gy_across, entering)
        r.gbc[at, :state] += nt(weighted, gstate_low)
        from_state = nn(r.b[at, :], gstate_low)
        to_output = nn(r.c[at, :], entering)
        kept = weighted.astype(F32) * from_state
        state_dot = jnp.sum(kept, axis=0, keepdims=True) + last * jnp.sum(
            entering.astype(F32) * gstate, axis=0, keepdims=True
        )
        r.kept_carry[g] = gstate * last + nn(r.c_t[c], gy_across)
        scores = r.scores[c]
        gscore = jnp.zeros((CHUNK, CHUNK), F32)
        parts = []
        for pair in range(GROUP_HEADS // 2):
            lanes = slice(pair * LANES, (pair + 1) * LANES)
            gmixing = nt(gy_low[:, lanes], both_halves(u[:, lanes], first))
            mixing = []
            for j in range(2):
                h = 2 * pair + j
                decay = decay_of(r.cum_b[here, h * LANES : (h + 1) * LANES], r.cum_t, h, at, lower)
                gscore = gscore + gmixing[:, j * CHUNK : (j + 1) * CHUNK] * decay
                mixing.append((scores * decay).astype(BF16))
            back = tn(jnp.concatenate(mixing, axis=1), gy_low[:, lanes])
            parts.append(jnp.where(first, back[:CHUNK], back[CHUNK:]))
        r.gscores[c] += gscore
        gu = jnp.concatenate(parts, axis=1)
        skip = r.skip[0:1, :]
        change = (
            gy * (r.y[at, :] - skip * x - ecum * to_output)
            + gy_across.astype(F32) * to_output
            - u.astype(F32) * gu
            - kept
        )
        gu = gu + from_state * toend
        row = lax.broadcasted_iota(jnp.int32, change.shape, 0)
        change = change + jnp.where(row == CHUNK - 1, state_dot, 0.0)
        r.decay_sums[at, :] += nn(jnp.concatenate([*two_parts(change), (x * gu).astype(BF16)], axis=1), chooser)
        gx = gu * step_e + skip * gy
        gsum = gx * (sig + x * (1.0 - sig))
        r.dz[at, :] = gsum
        r.kept_partial[g, 1] += fold(gy * x)
        r.kept_partial[g, 2] += fold(gsum)
        for t in range(4):
            r.kept_partial[g, 3 + t] += fold(gsum * shifted[t])
        after = r.dz.at[pl.ds(start, CHUNK + 8), :]
        gmix = sum(vector(TAPS + t) * after[3 - t : 3 - t + CHUNK, :] for t in range(4))
        r.mix_low[at, block(g)] = gmix.astype(BF16)
        inner = gmix * shifted[3]
        r.inner_sums[at, :] += inner[:, :LANES] + inner[:, LANES:]

    def early_room(g):
        room = 0
        for each, number in enumerate(ROOMS):
            room = jnp.where(g == each, number, room)
        return room

    def grad_scaled():
        def some(at):
            r.gs[at, :] = nt(r.cot_now[at, :], r.ow_now[...])

        by_rows(seq, 4 * CHUNK, some)

    def gate_step():
        slot = lax.rem(group, RING)


        @pl.when(k > 0)
        def _():
            load_ow(group).wait()
            grad_scaled()

        more = group + 1 < groups
        pl.when(more)(lambda: load_ow(group + 1).start())
        poll(6)
        load_gate(group).wait()
        for half, place in ((0, early_room(group)), (1, max(ROOMS) + 1)):

            def some(i, _):
                start = pl.multiple_of(i * CHUNK, CHUNK)
                at = pl.ds(pl.multiple_of(half * (seq // 2) + start, CHUNK), CHUNK)
                gating(at, r.dy.at[place, pl.ds(start, CHUNK), :])
                return 0

            lax.fori_loop(0, chunks // 2, some, 0)
        pl.when(more)(lambda: load_gate(group + 1).start())
        r.o_src[slot] = tn(r.scaled[...], r.cot_now[...]).astype(BF16)
        reduction.event(O, 0, group)
        poll(1)
        pl.when(k == 0)(lambda: load_normed().wait())
        r.g_src[slot] = nn(r.normed_now[...], r.gate_low[:, block(group)]).astype(BF16)
        reduction.event(G, 0, group)

    def scan_step():
        g = group
        half = jnp.where(opens, 1, 0)
        each, wide, chooser = spread(g, HEAD), spread(g, LANES), gather_heads(g)
        lower, first = masks()
        r.skip[...] = jnp.broadcast_to(skip_row(r.heads, each), (8, WIDTH))
        edge = pl.ds(pl.multiple_of((half + 1) * (seq // 2), 8), 8)
        r.dz[edge, :] = r.saved[g]
        place = jnp.where(opens, max(ROOMS) + 1, early_room(g))

        def chunk(i, _):
            pair = chunks // 4 - 1 - i
            both = pl.ds(pl.multiple_of(half * (seq // 2) + pair * 2 * CHUNK, CHUNK), 2 * CHUNK)
            r.cum_b[...] = nn(r.cum3[both, :], wide)
            r.step_e[...] = nn(r.step3[both, :], each)
            for j in (1, 0):
                dy = r.dy.at[place, pl.ds(pl.multiple_of((2 * pair + j) * CHUNK, CHUNK), CHUNK), :]
                here = slice(j * CHUNK, (j + 1) * CHUNK)
                scan_chunk(half * (chunks // 2) + 2 * pair + j, here, dy, g, chooser, lower, first)

            @pl.when(i == 0)
            def _():
                poll(3)

            return 0

        lax.fori_loop(0, chunks // 4, chunk, 0)
        r.saved[g] = r.dz[pl.ds(pl.multiple_of(half * (seq // 2), 8), 8), :]

    def mix_step():
        g = group
        r.m_src[lax.rem(g, RING)] = nn(r.normed_now[...], r.mix_low[:, block(g)]).astype(BF16)
        reduction.event(M, 0, g)
        r.small[0:7, block(g)] = jnp.concatenate(
            [jnp.sum(r.kept_partial[g, i], axis=0, keepdims=True) for i in range(7)], axis=0
        )

    def finish(half):
        upper = (
            lax.broadcasted_iota(jnp.int32, (CHUNK, CHUNK), 0) <= lax.broadcasted_iota(jnp.int32, (CHUNK, CHUNK), 1)
        ).astype(BF16)
        lane = lax.broadcasted_iota(jnp.int32, (CHUNK, LANES), 1)
        zero = jnp.zeros((8, LANES), F32)

        def some(i, totals):
            c = half * (chunks // 2) + i
            at = pl.ds(pl.multiple_of(c * CHUNK, CHUNK), CHUNK)
            gscore = r.gscores[c]
            high = gscore.astype(BF16)
            low = (gscore - high.astype(F32)).astype(BF16)
            r.gbc_low[at, state:] = (r.gbc[at, state:] + nn(high, r.b[at, :]) + nn(low, r.b[at, :])).astype(BF16)
            r.gbc_low[at, :state] = (r.gbc[at, :state] + tn(high, r.c[at, :]) + tn(low, r.c[at, :])).astype(BF16)
            sums = r.decay_sums[at, :]
            of_step = jnp.where(lane < LANES // 2, pltpu.roll(sums, LANES // 2, 1), 0.0)
            gdecay = nn(upper, split3(jnp.where(lane < SLOT, sums, 0.0)))
            gdecay = gdecay + pltpu.roll(gdecay, LANES - SLOT, 1) + pltpu.roll(gdecay, LANES - 2 * SLOT, 1)
            gdecay = jnp.where(lane < SLOT, gdecay, 0.0)
            gstep = (gdecay * r.heads[RATE : RATE + 1, :] + of_step) * sigmoid(r.step_pre[at, :])
            totals = (
                totals[0] + fold(gstep),
                totals[1] + fold(gdecay * softplus(r.step_pre[at, :]) * r.heads[RATE : RATE + 1, :]),
            )
            r.gstep_low[at, :] = gstep.astype(BF16)
            inner = r.inner_sums[at, :] + gstep * (r.step_pre[at, :] - r.heads[STEP_BIAS : STEP_BIAS + 1, :])
            r.inner_row[:, at] = row_sums(inner)
            return totals

        totals = lax.fori_loop(0, chunks // 2, some, (zero, zero), unroll=4)
        bc_copy(half).start()
        inner_copy(half).start()
        if half == 1:
            load_state().start()
        for j in range(2):
            start_loads(j)
        r.small[5:7, wide : wide + LANES] += jnp.concatenate([jnp.sum(total, axis=0, keepdims=True) for total in totals], axis=0)

    def meet(half):
        bc_copy(half).wait()
        inner_copy(half).wait()
        padded = r.gs
        if half == 1:
            load_state().wait()
            padded[0:8, :] = jnp.zeros((8, WIDTH), F32)
        edge = pl.ds((half + 1) * (seq // 2), 8)
        r.dz[edge, :] = r.saved[groups]
        top = (lax.broadcasted_iota(jnp.int32, (8, LANES), 0) == 0).astype(BF16)
        zero = jnp.zeros((8, WIDTH), F32)

        def some(i, totals):
            c = (half + 1) * (chunks // 2) - 1 - i
            start = pl.multiple_of(c * CHUNK, CHUNK)
            at = pl.ds(start, CHUNK)
            around = padded.at[pl.ds(start, CHUNK + 8), :]
            shifted = [around[5 + t : 5 + t + CHUNK, :] for t in range(4)]
            summed = r.state_rows[4:5, :] + sum(r.state_rows[t : t + 1, :] * shifted[t] for t in range(4))
            sig = sigmoid(summed)
            gact = r.gbc_low[at, :].astype(F32) + r.gbc_there[at, :].astype(F32)
            gsum = gact * (sig + summed * sig * (1.0 - sig))
            r.dz[at, :] = gsum
            totals = tuple(total + fold(gsum * v) for total, v in zip(totals, shifted)) + (totals[4] + fold(gsum),)
            after = r.dz.at[pl.ds(start, CHUNK + 8), :]
            gstate = sum(r.state_rows[t : t + 1, :] * after[3 - t : 3 - t + CHUNK, :] for t in range(4))
            r.gbc_low[at, :] = gstate.astype(BF16)
            column_of = to_column(r.inner_row[:, at] + r.inner_there[:, at], top)
            column_of = column_of + jnp.sum(gstate * shifted[3], axis=1, keepdims=True)
            rms = r.rms[at, :]
            r.decay_sums[at, :] = rms * rms * column_of * (1.0 / model)
            return totals

        totals = lax.fori_loop(0, chunks // 2, some, (zero,) * 5, unroll=2)
        r.saved[groups] = r.dz[pl.ds(half * (seq // 2), 8), :]
        r.small[0:5, wide : wide + WIDTH] += jnp.concatenate([jnp.sum(total, axis=0, keepdims=True) for total in totals], axis=0)
        if half == 0:
            r.s_src[0] = nn(r.normed_now[...], r.gbc_low[...]).astype(BF16)
            third = model // 3
            steps = nn(r.normed_now[...], r.gstep_low[...])
            rest = pltpu.roll(steps[third : 2 * third], SLOT, 1) + pltpu.roll(steps[2 * third :], 2 * SLOT, 1)
            r.t_src[0] = (steps[:third] + rest).astype(BF16)
            reduction.event(S, 0, 0)

    def grad_normed(j, half):
        load_w(j).wait()
        load_tokens(j).wait()
        load_narrow(j).wait()
        share = pl.ds(pl.multiple_of(near * state, LANES), state)
        at = rows_of(half)
        part = (
            nt(r.gate_low[at, :], r.w_block[j % 2, 0])
            + nt(r.mix_low[at, :], r.w_block[j % 2, 1])
            + nn(r.gstep_low[at, :], r.step_w[:, block(j)])
            + nt(r.gbc_low[at, share], r.state_block[j % 2, :, share])
        )
        r.stage[j % 2] = part.astype(BF16)
        part_store(j, half).start()
        total = fold(part * r.token_block[j % 2, at, :].astype(F32) * twice(r.rms[at, :]))
        r.small[7:8, block(j)] += jnp.sum(total, axis=0, keepdims=True)
        part_store(j, half).wait()
        part_copy(j, half).start()
        if j + 2 < blocks:
            start_loads(j + 2)
        elif half == 0:
            load_tokens(j + 2 - blocks).start()

    def grad_tokens(j):
        for half in (1, 0):
            part_copy(j, half).wait()
        load_there(j).start()
        load_mine(j).start()
        load_tokens(j).wait()
        load_there(j).wait()
        load_mine(j).wait()

        def some(at):
            whole = r.gate_low[at, block(j)].astype(F32) + r.scaled[at, :].astype(F32)
            pulled = twice(r.rms[at, :]) * (whole * r.vectors[NORM_GAIN : NORM_GAIN + 1, block(j)])
            pulled = pulled - r.token_block[j % 2, at, :].astype(F32) * twice(r.decay_sums[at, :])
            r.mix_low[at, block(j)] = (r.cot_now[at, block(j)].astype(F32) + pulled).astype(BF16)

        by_rows(seq, CHUNK, some)
        store_tokens(j).start()
        if j + 2 < blocks:
            load_tokens(j + 2).start()

    def small_event(n):
        if 0 < n < 5:
            small_copy(n - 1).wait()
            r.small[...] += r.small_there[n - 1]
        if n < 4:
            small_copy(n).start()
        elif n == 4:
            small_near().start()
        else:
            small_near().wait()
            row = lax.broadcasted_iota(jnp.int32, r.small_last.shape, 0)
            r.small[:, :wide] = r.small[:, :wide] + jnp.where(row == 7, r.small_last[...], 0.0)

    def block_rows(i):
        rows = pl.ds(i * WIDTH, WIDTH)
        room = [r.w_block.at[0, 0, :, :model], r.w_block.at[0, 1, :, :model], r.w_block.at[1, 0, :, :model]]
        made = r.w_block.at[1, 1, :, :model]
        if i == 0:
            product_copy().wait()
        loads = [
            pltpu.make_async_copy(src.at[rows, :], dst, r.row_sem.at[n])
            for n, (src, dst) in enumerate(zip((r.product, r.product_there, r.tokens), room))
        ]
        for load in loads:
            load.start()
        store = lambda n: pltpu.make_async_copy(made, r.block_out.at[pl.ds(n * WIDTH, WIDTH), :], r.row_sem.at[3])
        if i > 0:
            store(i - 1).wait()
        for load in loads:
            load.wait()

        def some(at):
            whole = room[0][at, :].astype(F32) + room[1][at, :].astype(F32)
            factor = r.factor[0, pl.ds(pl.multiple_of(i * WIDTH + at.start, 32), 32), :]
            scale = jnp.concatenate([factor] * (model // LANES), axis=1)
            made[at, :] = (room[2][at, :].astype(F32) + scale * whole).astype(BF16)

        by_rows(WIDTH, 32, some)
        store(i).start()
        if (i + 1) * WIDTH == seq:
            store(i).wait()

    def end():
        parts = {FINAL: grad_tokens, SMALL: small_event, BLOCK: block_rows}
        for kind, n, g in TAIL:
            if kind == MEET:
                meet(0)
            elif kind == PART:
                grad_normed(n, 0)
            elif kind in parts:
                parts[kind](n)
            else:
                reduction.event(kind, n, g)
        for j in range(blocks):
            store_tokens(j).wait()

    pl.when(k == 0)(first_step)

    @pl.when(k < 2 * groups)
    def _():
        poll(0)
        pl.when(opens)(gate_step)
        poll(2)
        scan_step()
        poll(4)
        pl.when(jnp.logical_not(opens))(mix_step)
        poll(5)

    pl.when(k == LAST_OPENING)(lambda: finish(1))
    pl.when(k == 2 * groups - 1)(lambda: finish(0))
    pl.when(k == 2 * groups)(end)


def backward(fwd, held, given):
    gate, mix, y, entering, sums, product = fwd
    seq, model = given["cot"].shape
    inner = given["ow"].shape[0]
    groups = inner // WIDTH
    chunks = seq // CHUNK
    two = given["state_w"].shape[1]
    state = two // 2
    blocks = model // WIDTH
    at = lambda k: group_at(jnp.minimum(k, 2 * groups - 1))[0]
    half_at = lambda k: jnp.where(group_at(jnp.minimum(k, 2 * groups - 1))[1], 1, 0)
    shape, vmem, dma = jax.ShapeDtypeStruct, pltpu.VMEM, pltpu.SemaphoreType.DMA
    stream = lambda rows: pl.BlockSpec((rows, WIDTH), lambda k: (0, at(k)))
    outside = pl.BlockSpec(memory_space=pl.ANY)
    values = dict(
        given, **held._asdict(), gate=gate, mix=mix, y=y, entering=entering, sums=sums, product=product
    )
    specs = {
        "mix": stream(seq + 8), "y": stream(seq), "cum_t": pl.BlockSpec((8, seq), lambda k: (at(k), 0)),
        "entering": pl.BlockSpec((1, chunks // 2, state, WIDTH), lambda k: (at(k), half_at(k), 0, 0)),
        **{name: outside for name in ("gate", "ow", "w", "tokens", "state_pre", "product", "state_w", "cot", "normed_t")},
    }
    wide = max(inner, model)
    halves = lambda rows: [rows // 2, rows // 4, rows // 8, rows // 16]
    ring = lambda rows, width, count=LANDINGS: [vmem((count, n, width), BF16) for n in halves(rows)]
    scratch = [
        vmem((seq + 8, WIDTH), F32), vmem((seq + 8, WIDTH), F32),
        vmem((2 * CHUNK, GROUP_HEADS * LANES), F32), vmem((2 * CHUNK, WIDTH), F32), vmem((groups + 1, 8, WIDTH), F32),
        vmem((groups, state, WIDTH), F32), vmem((groups, 7, 8, WIDTH), F32), vmem((max(ROOMS) + 2, seq // 2, WIDTH), BF16),
        vmem((2, seq, LANES), F32), vmem((16, seq), F32),
        vmem((chunks, CHUNK, CHUNK), F32), vmem((seq, LANES), F32), vmem((seq, LANES), F32), vmem((seq, two), F32),
        vmem((seq, WIDTH), BF16), vmem((seq, inner), BF16), vmem((seq, inner), BF16), vmem((seq, two), BF16),
        vmem((seq, two), BF16), vmem((8, seq), F32), vmem((8, seq), F32), vmem((seq, LANES), BF16),
        vmem((2, 2, WIDTH, inner), BF16), vmem((2, seq, WIDTH), BF16), vmem((2, seq // 2, WIDTH), BF16),
        vmem((RING, WIDTH, model), BF16), vmem((RING, model, WIDTH), BF16), vmem((RING, model, WIDTH), BF16),
        vmem((1, model, two), BF16), vmem((1, model // 3, LANES), BF16),
        *ring(WIDTH, model), *ring(model, WIDTH), *ring(model, WIDTH), *ring(model, two, 1), *ring(model // 3, LANES, 1),
        vmem((groups, model // 16, WIDTH), BF16), vmem((groups, model // 16, 2, WIDTH), BF16), vmem((groups, WIDTH // 16, model), BF16), vmem((4, 8, wide + two), F32),
        vmem((8, wide), F32),
        dma((5, 4, LANDINGS)), dma((5, 4, LANDINGS)), dma((4, groups)), dma((4, 4, groups)), dma((4, 4, groups)), dma((2, 2)), dma((2, 2)),
        dma((2, blocks)), dma((2, blocks)), dma((5,)), dma((5,)), dma((3, 2)), dma((blocks,)),
        dma, dma, dma, dma, dma((4,)), dma((2,)), vmem((seq, WIDTH), F32), vmem((WIDTH, model), BF16), dma((4,)),
        vmem((2, WIDTH, two), BF16), vmem((LANES, model), BF16), vmem((8, WIDTH), F32), vmem((model, seq), BF16),
        vmem((seq, model), BF16), dma((2,)),
    ]
    return pl.pallas_call(
        functools.partial(backward_kernel, groups),
        grid=(2 * groups + 1,),
        in_specs=[specs.get(name, whole_spec(values[name].shape)) for name in Inputs._fields],
        out_specs=[outside] * 9 + [pl.BlockSpec((8, wide + two), lambda k: (0, 0))],
        out_shape=[
            shape((inner, model), BF16), shape((model, 2, inner), BF16), shape((model, two), BF16), shape((model // 3, LANES), BF16),
            shape((seq, model), BF16), shape((blocks, seq, WIDTH), BF16), shape((blocks, seq, WIDTH), BF16),
            shape((seq, model), BF16), shape((seq, model), BF16),
            shape((8, wide + two), F32),
        ],
        scratch_shapes=scratch,
        compiler_params=pltpu.CompilerParams(collective_id=0, has_side_effects=True, vmem_limit_bytes=60 * MIB),
        name="backward",
    )(*[values[name] for name in Inputs._fields])


def narrow_kernel(
    small, gstep_w, norm, taps, bias, state_taps, state_bias, steps, rates, skips, gains, gstep_t
):
    model, inner, two, heads = norm.shape[0], bias.shape[0], state_bias.shape[0], steps.shape[0]
    wide = max(model, inner)
    norm[...] = small[7, :model].astype(BF16)
    taps[...] = small[3:7, :inner].astype(BF16)
    bias[...] = small[2, :inner].astype(BF16)
    state_taps[...] = small[0:4, wide : wide + two].astype(BF16)
    state_bias[...] = small[4, wide : wide + two].astype(BF16)
    steps[...] = small[5, wide : wide + heads].astype(BF16)
    rates[...] = small[6, wide : wide + heads].astype(BF16)
    gains[...] = small[0, :inner].astype(BF16)
    channel = lax.broadcasted_iota(jnp.int32, (inner, LANES), 0)
    head = lax.broadcasted_iota(jnp.int32, (inner, LANES), 1)
    chooser = jnp.where(head == channel // HEAD, 1.0, 0.0).astype(BF16)
    high, low = two_parts(small[0:8, :inner])
    skips[...] = (nn(high, chooser) + nn(low, chooser))[1, :heads].astype(BF16)
    turned, third = gstep_w[...].T, model // 3
    for i in range(3):
        gstep_t[:, i * third : (i + 1) * third] = turned[i * SLOT : i * SLOT + heads, :]


def narrow_outputs(small, gstep_w, heads, model, inner, two):
    shapes = (model,), (4, inner), (inner,), (4, two), (two,), (heads,), (heads,), (heads,), (inner,), (heads, model)
    return pl.pallas_call(
        narrow_kernel, out_shape=[jax.ShapeDtypeStruct(item, BF16) for item in shapes], name="narrow_outputs"
    )(small, gstep_w)


def on_device(
    tokens, norm_gain, mix_weight, state_weight, step_weight, conv_weight, conv_bias, state_conv_weight, state_conv_bias,
    step_bias, log_rate, skip_gain, gate_gain, out_weight, cotangent,
):
    model = tokens.shape[1]
    inner = out_weight.shape[0]
    heads = step_bias.shape[0]
    two = state_weight.shape[1]
    both = jnp.transpose(mix_weight, (1, 0, 2))
    step_t = step_weight.T
    narrow = (
        conv_weight, conv_bias, gate_gain, norm_gain, state_conv_weight, state_conv_bias, step_bias, log_rate, skip_gain
    )
    fwd, held = forward(tokens, state_weight, step_t, narrow, both, cotangent, out_weight)
    given = {"tokens": tokens, "cot": cotangent, "w": both, "ow": out_weight, "state_w": state_weight, "step_t": step_t}
    gout, gmix, gstate_w, gstep_w, grad_tokens, _, _, block_out, _, small = backward(fwd, held, given)
    size = lax.axis_size("dp")
    if size > 16:
        rows = [[i + 16 * j for j in range(size // 16)] for i in range(16)]
        gout, gmix, gstate_w, gstep_w, small = lax.psum((gout, gmix, gstate_w, gstep_w, small), "dp", axis_index_groups=rows)
    norm, taps, bias, state_taps, state_bias, steps, rates, skips, gains, gstep_t = narrow_outputs(
        small, gstep_w, heads, model, inner, two
    )
    return (
        block_out, grad_tokens, norm, gmix, gstate_w, gstep_t.T, taps, bias, state_taps, state_bias, steps, rates, skips, gains,
        gout,
    )


def solution(mesh):
    rows, halves = P("dp", None), P("tensor")
    return jax.shard_map(
        on_device,
        mesh=mesh,
        in_specs=(
            rows, P(), P(None, None, "tensor"), P(), P(None, "tensor"), P(None, "tensor"), halves, P(), P(), halves, halves,
            halves, halves, P("tensor", None), rows,
        ),
        out_specs=(
            rows, rows, P(), P(None, None, "tensor"), P(), P(None, "tensor"), P(None, "tensor"), halves, P(), P(), halves,
            halves, halves, halves, P("tensor", None),
        ),
        check_vma=False,
    )
```
